512 devices in a mesh: heads: 16 (over z_hi, y), batch: 32 (over x, z_lo, core).
Axes of the slice: x: 4, y: 8, z: 8 (z_hi: 2, z_lo: 4; z = z_hi * 4 + z_lo), core: 2. Of those that a mesh axis runs over, the one named last changes fastest.
Arguments:
- q_latent: bfloat16 [128, 1536], P('batch'), may hold values from -8 to 8
- new_latent: bfloat16 [128, 512], P('batch'), may hold values from -6 to 6
- new_rope: bfloat16 [128, 64], P('batch'), may hold values from -6 to 6
- latent_cache: bfloat16 [128, 1024, 512], P('batch'), may hold values from -8 to 8
- rope_cache: bfloat16 [128, 1024, 64], P('batch'), may hold values from -6 to 6
- lengths: int32 [128], P('batch'), may hold values from 1 to 1024, as said below
- q_up: bfloat16 [6144, 1536], P(('heads', 'batch')), may hold values from -5 to 5
- kv_up: bfloat16 [8192, 512], P(('heads', 'batch')), may hold values from -2 to 2
- out_proj: bfloat16 [7168, 4096], P(('heads', 'batch')), may hold values from -1.5 to 1.5
Outputs:
- attn_out: bfloat16 [128, 7168], P('batch', 'heads')
The draws below stay inside these ranges and needn't reach their ends.
Inputs may be any that keep to these rules, and one draw needn't show every extreme that they name: `lengths`: every aligned block of 4 rows holds at least one row of length 1024.
All inputs are finite; a program needn't handle non-finite values.
Results may differ from the reference program's by a relative error of at most 0.011.
Values may be sent and summed in bfloat16 or wider, within the bound.
A program may use at most 64 MiB of HBM per device.

```python
import jax
import jax.numpy as jnp
from jax import lax

D = 7168
HEADS = 32
QR = 1536
KVR = 512
NOPE = 128
ROPE = 64
VDIM = 128
ROWS_DEV = 4
CACHE = 1024
ROWS = 128


def length_values(key):
    key = jax.random.fold_in(key, 23)
    base_key, offset_key = jax.random.split(key)
    base = jax.random.randint(base_key, (ROWS,), 1, CACHE + 1)
    offsets = jax.random.randint(offset_key, (ROWS // ROWS_DEV,), 0, ROWS_DEV)
    chosen = jnp.repeat(offsets, ROWS_DEV)
    hit_rows = jnp.arange(ROWS) % ROWS_DEV == chosen
    return jnp.where(hit_rows, CACHE, base).astype(jnp.int32)


def head_key_rows(key):
    key = jax.random.fold_in(key, 41)
    return jnp.clip(jax.random.normal(key, (HEADS, NOPE, KVR), jnp.float32), -6.0, 6.0)


def draw_lengths(key, part):
    return length_values(key)


def draw_kv_up(key, part):
    shared = head_key_rows(key)
    own_key = jax.random.fold_in(key, 5)
    value_rows = jnp.clip(jax.random.normal(own_key, (HEADS, VDIM, KVR), jnp.float32), -6.0, 6.0)
    return (jnp.concatenate([shared, value_rows], 1) * KVR ** (-0.5)).reshape(HEADS * (NOPE + VDIM), KVR).astype(jnp.bfloat16)


def draw_q_up(key, part):
    own_key = jax.random.fold_in(key, 7)
    fresh = jnp.clip(jax.random.normal(own_key, (HEADS, NOPE + ROPE, QR), jnp.float32), -6.0, 6.0)
    return (fresh * QR ** (-0.5)).reshape(HEADS * (NOPE + ROPE), QR).astype(jnp.bfloat16)


def draw_q_latent(key, part):
    own_key = jax.random.fold_in(key, 13)
    return jnp.clip(jax.random.normal(own_key, (ROWS, QR), jnp.float32), -6.0, 6.0).astype(jnp.bfloat16)


def draw_latent_cache(key, part):
    own_key = jax.random.fold_in(key, 11)
    return jnp.clip(jax.random.normal(own_key, (ROWS, CACHE, KVR), jnp.float32), -6.0, 6.0).astype(jnp.bfloat16)


def block_scale(stream_key, dims, cuts, low, largest):
    factor_of = 1.0
    for dim, shards_of in cuts:
        heights = jax.random.uniform(jax.random.fold_in(jax.random.fold_in(stream_key, 6), dim), (shards_of,), jnp.float32, low / len(cuts), largest / len(cuts))
        factor_of = factor_of * jnp.repeat(jnp.exp(heights), dims[dim] // shards_of).reshape((-1,) + (1,) * (len(dims) - 1 - dim))
    return factor_of


def normal_values(key, extent, scale, bound, cuts=(), held_as=jnp.bfloat16):
    level = block_scale(key, extent, cuts, -0.22, 0.18) if cuts else 1.0
    values = jax.random.normal(key, extent, jnp.float32) * scale * level
    return jnp.minimum(jnp.maximum(values, -bound), bound).astype(held_as)


def setup_inputs(seed: int = 0) -> dict:
    key_list = jax.random.split(jax.random.key(seed), 10)
    q_latent = draw_q_latent(jax.random.fold_in(key_list[9], 71), 0)
    new_latent = normal_values(key_list[1], (ROWS, KVR), 1.0, 6.0, ((0, 32),))
    new_rope = normal_values(key_list[2], (ROWS, ROPE), 1.0, 6.0, ((0, 32),))
    latent_cache = draw_latent_cache(jax.random.fold_in(key_list[9], 71), 0)
    rope_cache = normal_values(key_list[4], (ROWS, CACHE, ROPE), 1.0, 6.0, ((0, 32),))
    lengths = draw_lengths(jax.random.fold_in(key_list[9], 71), 0)
    q_up = draw_q_up(jax.random.fold_in(key_list[9], 71), 0)
    kv_up = draw_kv_up(jax.random.fold_in(key_list[9], 71), 0)
    out_proj = normal_values(key_list[8], (D, HEADS * VDIM), (VDIM // 8) ** -0.5, 1.5, ((0, 512),))
    return dict(q_latent=q_latent, new_latent=new_latent, new_rope=new_rope, latent_cache=latent_cache, rope_cache=rope_cache, lengths=lengths, q_up=q_up, kv_up=kv_up, out_proj=out_proj)


def rotate_half(values, angles):
    half_size = values.shape[-1] // 2
    cosine = jnp.cos(angles)
    sine = jnp.sin(angles)
    first_half = values[..., :half_size]
    second_half = values[..., half_size:]
    return jnp.concatenate([first_half * cosine - second_half * sine, second_half * cosine + first_half * sine], axis=-1)


def rope_angles(lengths, width):
    half_size = width // 2
    inverse = 50000.0 ** (-2.0 * jnp.arange(half_size, dtype=jnp.float32) / width)
    return lengths.astype(jnp.float32)[:, None] * inverse[None, :]


def reference(q_latent, new_latent, new_rope, latent_cache, rope_cache, lengths, q_up, kv_up, out_proj):
    scale_factor = (NOPE + ROPE) ** -0.5
    angles = rope_angles(lengths, ROPE)
    key_new = rotate_half(new_rope.astype(jnp.float32), angles).astype(jnp.bfloat16)
    query_w = q_up.reshape(HEADS, NOPE + ROPE, QR)
    kv_w = kv_up.reshape(HEADS, NOPE + VDIM, KVR)
    out_w = out_proj.reshape(D, HEADS, VDIM).transpose(1, 0, 2)
    cache_f = latent_cache.astype(jnp.float32)
    rope_f = rope_cache.astype(jnp.float32)
    new_f = new_latent.astype(jnp.float32)
    valid = jnp.arange(CACHE)[None, :] < lengths[:, None]

    def one_head(total, weights):
        query_head, kv_head, out_head = weights
        absorbed_q = jnp.dot(kv_head[:NOPE].T, query_head[:NOPE], preferred_element_type=jnp.float32).astype(jnp.bfloat16)
        query_abs = jnp.dot(q_latent, absorbed_q.T, preferred_element_type=jnp.float32).astype(jnp.bfloat16)
        query_rope = rotate_half(jnp.dot(q_latent, query_head[NOPE:].T, preferred_element_type=jnp.float32), angles).astype(jnp.bfloat16)
        abs_f = query_abs.astype(jnp.float32)
        rope_q = query_rope.astype(jnp.float32)
        scores = (jnp.einsum('rc,rtc->rt', abs_f, cache_f) + jnp.einsum('rp,rtp->rt', rope_q, rope_f)) * scale_factor
        score_new = (jnp.sum(abs_f * new_f, -1) + jnp.sum(rope_q * key_new.astype(jnp.float32), -1)) * scale_factor
        scores = jnp.where(valid, scores, -1e30)
        top_score = jnp.maximum(jnp.max(scores, -1), score_new)
        weights_old = jnp.exp(scores - top_score[:, None])
        weight_new = jnp.exp(score_new - top_score)
        denom = jnp.sum(weights_old, -1) + weight_new
        probs = (weights_old / denom[:, None]).astype(jnp.bfloat16)
        prob_new = (weight_new / denom).astype(jnp.bfloat16)
        context = (jnp.einsum('rt,rtc->rc', probs.astype(jnp.float32), cache_f) + prob_new.astype(jnp.float32)[:, None] * new_f).astype(jnp.bfloat16)
        value_out = jnp.dot(context, kv_head[NOPE:].T, preferred_element_type=jnp.float32).astype(jnp.bfloat16)
        return total + jnp.dot(value_out, out_head.T, preferred_element_type=jnp.float32), None

    total, _ = lax.scan(one_head, jnp.zeros((ROWS, D), jnp.float32), (query_w, kv_w, out_w))
    return total.astype(jnp.bfloat16)
```

```python
import functools
import math

import jax
import jax.numpy as jnp
from jax import lax
from jax.experimental import pallas as pl
from jax.experimental.pallas import tpu as pltpu
from jax.sharding import PartitionSpec as P

QR = 1536
KVR = 512
NOPE = 128
ROPE = 64
CACHE = 1024
QROWS = 12
SLOT = 16
XS, ZS = 4, 4
HS = 16
QC = QR // 4
OUT_K = 4096
F32 = jnp.float32
BF16 = jnp.bfloat16
NT = (((1,), (1,)), ((), ()))


def dot_nt(a, b):
    return lax.dot_general(a, b, NT, preferred_element_type=F32)


def dot_nn(a, b):
    return jnp.dot(a, b, preferred_element_type=F32)


def kernel(
    ql_hbm, nl_hbm, nr_hbm, lat_hbm, rope_hbm, len_hbm, qup_hbm, kvup_hbm, outp_hbm, y_ref,
    ql_in, nl_in, nr_in, len_in, qup_in, outp_in, lat, rope,
    qbuf, qlbuf, qsend, qrecv, kvbuf, wbuf, sel, sel_out, vx, vh, ysend, yrecv,
    in_sem, q_send, q_recv, ql_send, ql_recv, qx_send, qx_recv, kvz_send, kvb_send, kv_recv,
    w_send, w_recv, vx_send, vx_recv, vh_send, vh_recv, y_send, y_recv,
):
    h = lax.axis_index("heads")
    b = lax.axis_index("batch")
    x, z, c = b // 8, (b // 2) % 4, b % 2

    def index(xx, zz, cc):
        return xx * 8 + zz * 2 + cc

    zk = [z, z + 1 - 2 * (z % 2), (z + 2) % 4, 3 - z]
    xr, xl, xo = (x + 1) % 4, (x + 3) % 4, (x + 2) % 4
    right, left, sibling = index(xr, z, c), index(xl, z, c), index(x, z, 1 - c)
    mine, theirs = x * 2 + c, x * 2 + 1 - c
    own = z * 2 + c

    loads = [
        pltpu.make_async_copy(source, target, in_sem.at[i])
        for i, (source, target) in enumerate(
            [
                (qup_hbm, qup_in), (ql_hbm, ql_in), (kvup_hbm, kvbuf.at[mine, z]),
                (nl_hbm, nl_in), (nr_hbm, nr_in), (len_hbm, len_in), (outp_hbm, outp_in),
                (lat_hbm, lat), (rope_hbm, rope),
            ]
        )
    ]
    for load in loads:
        load.start()

    barrier = pltpu.get_barrier_semaphore()

    def greet(target):
        pl.semaphore_signal(barrier, inc=1, device_id={"batch": target})

    greet(right)
    greet(left)
    greet(sibling)
    for k in range(1, ZS):
        greet(index(x, zk[k], c))
        greet(index(x, zk[k], 1 - c))

    @pl.loop(1, HS)
    def _(i):
        pl.semaphore_signal(barrier, inc=1, device_id={"heads": (h + i) % HS})

    loads[0].wait()
    qbuf[x, :, :] = jnp.concatenate([qup_in[...], jnp.zeros((SLOT - QROWS, QR), BF16)], axis=0)
    loads[1].wait()
    ql_own = ql_in[...].astype(F32)
    qlbuf[own, :, :] = jnp.concatenate(
        [ql_own[:, j * QC: (j + 1) * QC] for j in range(4)], axis=0
    ).astype(BF16)
    loads[2].wait()

    pl.semaphore_wait(barrier, 2 + 1 + 6 + HS - 1)

    def remote(source, target, send_sem, recv_sem, device):
        return pltpu.make_async_remote_copy(
            src_ref=source, dst_ref=target, send_sem=send_sem, recv_sem=recv_sem,
            device_id=device,
        )

    def push(ref, send_sem, recv_sem, target):
        remote(ref, ref, send_sem, recv_sem, {"batch": target}).start()

    def arrive(ref, recv_sem):
        pltpu.make_async_copy(ref, ref, recv_sem).wait()

    for target in (right, left):
        push(qbuf.at[x], q_send.at[0], q_recv.at[x, 0], target)
    for k in range(1, ZS):
        push(kvbuf.at[mine, z], kvz_send.at[0], kv_recv.at[z], index(x, zk[k], c))
    for k in range(1, ZS):
        push(qlbuf.at[own], ql_send.at[0], ql_recv.at[own], index(x, zk[k], c))
    push(qlbuf.at[own], ql_send.at[0], ql_recv.at[own], sibling)

    @pl.loop(0, 32)
    def _(t):
        x_t = t % 4
        first_row = QROWS * ((x_t % 2) * 8 + (t // 8) * 2 + (t // 4) % 2)
        shape = (SLOT, 2 * NOPE + 2 * ROPE)
        within = lax.broadcasted_iota(jnp.int32, shape, 0)
        col = lax.broadcasted_iota(jnp.int32, shape, 1)
        row = within + first_row
        nope = (row < NOPE) & (col == row + (x_t // 2) * NOPE)
        rotary = row - NOPE
        swapped = (rotary + ROPE // 2) % ROPE
        rope_at = (row >= NOPE) & (
            (col == 2 * NOPE + rotary) | (col == 2 * NOPE + ROPE + swapped)
        )
        block = jnp.where((within < QROWS) & (nope | rope_at), 1.0, 0.0).astype(BF16)
        sel[pl.ds(pl.multiple_of(t * SLOT, SLOT), SLOT), :] = block

    arrive(qbuf.at[xl], q_recv.at[xl, 0])
    push(qbuf.at[xl, :, pl.ds(0, QR // 2)], q_send.at[0], q_recv.at[xl, 0], right)
    arrive(qbuf.at[xr], q_recv.at[xr, 0])
    push(qbuf.at[xr, :, pl.ds(QR // 2, QR // 2)], q_send.at[0], q_recv.at[xr, 1], left)

    for k in range(1, ZS):
        arrive(kvbuf.at[mine, zk[k]], kv_recv.at[zk[k]])
    for target in (right, left):
        push(kvbuf.at[mine], kvb_send.at[0], kv_recv.at[4 + x], target)
    push(kvbuf.at[mine], kvb_send.at[0], kv_recv.at[4 + x], sibling)
    for k in range(1, ZS):
        slot = zk[k] * 2 + c
        arrive(qlbuf.at[slot], ql_recv.at[slot])
        push(qlbuf.at[slot], ql_send.at[0], ql_recv.at[slot], sibling)

    loads[6].wait()
    wbuf[mine, :, :] = jnp.concatenate([outp_in[...], jnp.zeros((2, OUT_K), BF16)], axis=0)

    from_left, from_right, from_far = xl * 2 + c, xr * 2 + c, xo * 2 + c
    arrive(kvbuf.at[from_left], kv_recv.at[4 + xl])
    push(kvbuf.at[from_left, pl.ds(0, 2)], kvb_send.at[0], kv_recv.at[12], right)
    push(kvbuf.at[from_left], kvb_send.at[0], kv_recv.at[8 + xl], sibling)
    arrive(kvbuf.at[from_right], kv_recv.at[4 + xr])
    push(kvbuf.at[from_right, pl.ds(2, 2)], kvb_send.at[0], kv_recv.at[13], left)
    push(kvbuf.at[from_right], kvb_send.at[0], kv_recv.at[8 + xr], sibling)

    for target in (right, left, sibling):
        push(wbuf.at[mine], w_send.at[0], w_recv.at[mine, 0], target)

    arrive(qbuf.at[xo, :, pl.ds(0, QR // 2)], q_recv.at[xo, 0])
    arrive(qbuf.at[xo, :, pl.ds(QR // 2, QR // 2)], q_recv.at[xo, 1])
    for zz in range(ZS):
        slot = zz * 2 + 1 - c
        arrive(qlbuf.at[slot], ql_recv.at[slot])
    ql_rows = qlbuf[...].reshape(8 * SLOT, QC)
    block_of = (lax.broadcasted_iota(jnp.int32, (8 * SLOT, XS * SLOT), 0) // 4) % 4
    partial = jnp.zeros((8 * SLOT, XS * SLOT), F32)
    for j in range(4):
        columns = qbuf[:, :, j * QC: (j + 1) * QC].reshape(XS * SLOT, QC)
        partial = jnp.where(block_of == j, dot_nt(ql_rows, columns), partial)
    partial = partial.reshape(8, SLOT, XS * SLOT)
    partial = partial[:, 0:8] + partial[:, 8:16]
    partial = jnp.concatenate([partial, partial], axis=2)
    lane_of = lax.broadcasted_iota(jnp.int32, (8, 8, 128), 2)
    qsend[...] = jnp.where(lane_of // 64 == c, partial, 0.0)
    for k in range(1, ZS):
        for cc in (c, 1 - c):
            slot = zk[k] * 2 + cc
            remote(
                qsend.at[slot], qrecv.at[own], qx_send.at[0], qx_recv.at[own],
                {"batch": index(x, zk[k], cc)},
            ).start()
    remote(
        qsend.at[z * 2 + 1 - c], qrecv.at[own], qx_send.at[0], qx_recv.at[own], {"batch": sibling}
    ).start()
    qrecv[own, :, :] = qsend[own]

    arrive(kvbuf.at[from_far, pl.ds(0, 2)], kv_recv.at[12])
    arrive(kvbuf.at[from_far, pl.ds(2, 2)], kv_recv.at[13])
    push(kvbuf.at[from_far], kvb_send.at[0], kv_recv.at[8 + xo], sibling)

    row8 = lax.broadcasted_iota(jnp.int32, (8, 1), 0)
    row_of = row8 % 4
    low = row8 < 4
    for load in loads[3:6]:
        load.wait()
    length = jnp.zeros((8, 1), jnp.int32)
    for r in range(4):
        length = jnp.where(row_of == r, len_in[r], length)

    lane64 = lax.broadcasted_iota(jnp.int32, (8, ROPE), 1)
    inverse = jnp.exp((lane64 % (ROPE // 2)).astype(F32) * (-2.0 * math.log(50000.0) / ROPE))
    angles = length.astype(F32) * inverse
    cosine = jnp.cos(angles)
    sine = jnp.sin(angles)
    sine = jnp.where(lane64 < ROPE // 2, -sine, sine)

    def twice(values):
        return jnp.concatenate([values, values], axis=0)

    nr8 = twice(nr_in[...].astype(F32))
    nr_swapped = jnp.concatenate([nr8[:, ROPE // 2:], nr8[:, : ROPE // 2]], axis=1)
    key_new = (nr8 * cosine + nr_swapped * sine).astype(BF16).astype(F32)
    nl8 = twice(nl_in[...].astype(F32))

    for k in range(1, ZS):
        for cc in (c, 1 - c):
            slot = zk[k] * 2 + cc
            arrive(qrecv.at[slot], qx_recv.at[slot])
    arrive(qrecv.at[z * 2 + 1 - c], qx_recv.at[z * 2 + 1 - c])
    pieces = []
    for zz in range(ZS):
        piece = qrecv[2 * zz] + qrecv[2 * zz + 1]
        pieces.append(piece + pltpu.roll(piece, 4, 0))
    q_all = jnp.concatenate(pieces, axis=1)
    lane_q = lax.broadcasted_iota(jnp.int32, (8, 512), 1)
    q_all = jnp.where((lane_q % 64 < 32) == low, q_all, 0.0)
    q_hi = q_all.astype(BF16)
    q_lo = (q_all - q_hi.astype(F32)).astype(BF16)
    selection = sel[...]
    q_sel = dot_nn(q_hi, selection) + dot_nn(q_lo, selection)
    q_nope = q_sel[:, 0: 2 * NOPE].astype(BF16)
    query_rope = (
        q_sel[:, 2 * NOPE: 2 * NOPE + ROPE] * cosine + q_sel[:, 2 * NOPE + ROPE:] * sine
    ).astype(BF16)

    arrive(kvbuf.at[theirs], kv_recv.at[4 + x])
    for xx in (xl, xr, xo):
        block = xx * 2 + 1 - c
        arrive(kvbuf.at[block], kv_recv.at[8 + xx])

    def kv_rows(xx):
        return jnp.concatenate(
            [kvbuf[xx * 2 + cc, zz] for zz in range(ZS) for cc in range(2)], axis=0
        )

    query_abs = (
        dot_nn(q_nope[:, :NOPE], kv_rows(0)) + dot_nn(q_nope[:, NOPE:], kv_rows(2))
    ).astype(BF16)

    loads[7].wait()
    loads[8].wait()
    scale = (NOPE + ROPE) ** (-0.5)
    scores = jnp.zeros((8, CACHE), F32)
    for r in range(4):
        of_row = dot_nt(query_abs, lat[r]) + dot_nn(query_rope, rope[r])
        scores = jnp.where(row_of == r, of_row, scores)
    score_new = scale * (
        jnp.sum(query_abs.astype(F32) * nl8, axis=1, keepdims=True)
        + jnp.sum(query_rope.astype(F32) * key_new, axis=1, keepdims=True)
    )
    position = lax.broadcasted_iota(jnp.int32, (8, CACHE), 1)
    scores = jnp.where(position < length, scores * scale, -1e30)
    top = jnp.maximum(jnp.max(scores, axis=1, keepdims=True), score_new)
    old = jnp.exp(scores - top)
    new = jnp.exp(score_new - top)
    denom = jnp.sum(old, axis=1, keepdims=True) + new
    probs = (old / denom).astype(BF16)
    prob_new = (new / denom).astype(BF16).astype(F32)
    context = jnp.zeros((8, KVR), F32)
    for r in range(4):
        context = jnp.where(row_of == r, dot_nn(probs, lat[r]), context)
    context = (context + prob_new * nl8).astype(BF16)
    value = jnp.where(low, dot_nt(context, kv_rows(1)), dot_nt(context, kv_rows(3)))
    vx[z, :, :] = value.astype(BF16).astype(F32)

    for k in range(1, ZS):
        push(vx.at[z], vx_send.at[0], vx_recv.at[z], index(x, zk[k], c))

    arrive(wbuf.at[from_left], w_recv.at[from_left, 0])
    push(
        wbuf.at[from_left, :, pl.ds(0, OUT_K // 2)], w_send.at[0], w_recv.at[from_left, 0], right
    )
    push(wbuf.at[from_left], w_send.at[0], w_recv.at[from_left, 0], sibling)
    arrive(wbuf.at[from_right], w_recv.at[from_right, 0])
    push(
        wbuf.at[from_right, :, pl.ds(OUT_K // 2, OUT_K // 2)], w_send.at[0],
        w_recv.at[from_right, 1], left,
    )
    push(wbuf.at[from_right], w_send.at[0], w_recv.at[from_right, 0], sibling)

    for k in range(1, ZS):
        arrive(vx.at[zk[k]], vx_recv.at[zk[k]])
    vh[h, :, :] = vx[...].reshape(32, 128).astype(BF16)

    @pl.loop(1, HS)
    def _(i):
        remote(
            vh.at[h], vh.at[h], vh_send.at[0], vh_recv.at[h], {"heads": (h + i) % HS}
        ).start()

    arrive(wbuf.at[from_far, :, pl.ds(0, OUT_K // 2)], w_recv.at[from_far, 0])
    arrive(wbuf.at[from_far, :, pl.ds(OUT_K // 2, OUT_K // 2)], w_recv.at[from_far, 1])
    push(wbuf.at[from_far], w_send.at[0], w_recv.at[from_far, 0], sibling)

    @pl.loop(0, 32)
    def _(t):
        start = (((t // 2) % 4) * 8 + (t // 8) * 2 + t % 2) * 14
        col = lax.broadcasted_iota(jnp.int32, (SLOT, 448), 1) - start
        row = lax.broadcasted_iota(jnp.int32, (SLOT, 448), 0)
        block = jnp.where((col == row) & (row < 14), 1.0, 0.0).astype(BF16)
        sel_out[pl.ds(pl.multiple_of(t * SLOT, SLOT), SLOT), :] = block

    for xx in (x, xl, xr, xo):
        block = xx * 2 + 1 - c
        arrive(wbuf.at[block], w_recv.at[block, 0])

    @pl.loop(1, HS)
    def _(i):
        other = (h + i) % HS
        arrive(vh.at[other], vh_recv.at[other])

    row32 = lax.broadcasted_iota(jnp.int32, (32, 128), 0)
    is_low = (row32 % 8) < 4
    zero = jnp.zeros((32, 128), BF16)
    chunks = []
    for hh in range(HS):
        block = vh[hh]
        chunks.append(jnp.where(is_low, block, zero))
        chunks.append(jnp.where(is_low, zero, block))
    y_all = dot_nt(jnp.concatenate(chunks, axis=1), wbuf[...].reshape(8 * SLOT, OUT_K))
    ysend[...] = y_all.reshape(ZS, 8, 128)

    for k in range(1, ZS):
        remote(
            ysend.at[zk[k]], yrecv.at[z], y_send.at[0], y_recv.at[z],
            {"batch": index(x, zk[k], c)},
        ).start()
    yrecv[z, :, :] = ysend[z]
    for k in range(1, ZS):
        arrive(yrecv.at[zk[k]], y_recv.at[zk[k]])
    pieces = []
    for zz in range(ZS):
        piece = yrecv[zz]
        pieces.append(piece + pltpu.roll(piece, 4, 0))
    summed = jnp.concatenate(pieces, axis=1).astype(BF16)
    y_ref[...] = dot_nn(summed, sel_out[...])[0:4]

    for ref, sem in (
        (qbuf.at[0:3], q_send), (kvbuf.at[0, 0:3], kvz_send), (kvbuf.at[0:7], kvb_send),
        (qlbuf.at[0:7], ql_send), (qsend.at[0:7], qx_send), (wbuf.at[0:7], w_send),
        (vx.at[0:3], vx_send), (vh.at[0:15], vh_send), (ysend.at[0:3], y_send),
    ):
        arrive(ref, sem.at[0])


def shards(
    q_latent, new_latent, new_rope, latent_cache, rope_cache, lengths, q_up, kv_up, out_proj
):
    hbm = pl.BlockSpec(memory_space=pltpu.HBM)
    dma = pltpu.SemaphoreType.DMA
    return pl.pallas_call(
        kernel,
        out_shape=jax.ShapeDtypeStruct((4, 448), F32),
        in_specs=[hbm] * 9,
        out_specs=pl.BlockSpec(memory_space=pltpu.VMEM),
        scratch_shapes=[
            pltpu.VMEM((4, QR), BF16),
            pltpu.VMEM((4, KVR), BF16),
            pltpu.VMEM((4, ROPE), BF16),
            pltpu.SMEM((4,), jnp.int32),
            pltpu.VMEM((QROWS, QR), BF16),
            pltpu.VMEM((14, OUT_K), BF16),
            pltpu.VMEM((4, CACHE, KVR), BF16),
            pltpu.VMEM((4, ROPE, CACHE), BF16),
            pltpu.VMEM((XS, SLOT, QR), BF16),
            pltpu.VMEM((8, SLOT, QC), BF16),
            pltpu.VMEM((8, 8, 128), F32),
            pltpu.VMEM((8, 8, 128), F32),
            pltpu.VMEM((8, ZS, SLOT, KVR), BF16),
            pltpu.VMEM((8, SLOT, OUT_K), BF16),
            pltpu.VMEM((512, 2 * NOPE + 2 * ROPE), BF16),
            pltpu.VMEM((512, 448), BF16),
            pltpu.VMEM((ZS, 8, 128), F32),
            pltpu.VMEM((HS, 32, 128), BF16),
            pltpu.VMEM((ZS, 8, 128), F32),
            pltpu.VMEM((ZS, 8, 128), F32),
            dma((9,)),
            dma((1,)), dma((XS, 2)),
            dma((1,)), dma((8,)),
            dma((1,)), dma((8,)),
            dma((1,)), dma((1,)), dma((14,)),
            dma((1,)), dma((8, 2)),
            dma((1,)), dma((ZS,)),
            dma((1,)), dma((HS,)),
            dma((1,)), dma((ZS,)),
        ],
        compiler_params=pltpu.CompilerParams(
            collective_id=0, has_side_effects=True, vmem_limit_bytes=60 * 2**20
        ),
        cost_estimate=pl.CostEstimate(
            flops=4 * 10**8, bytes_accessed=5 * 10**6, transcendentals=10**4
        ),
    )(
        q_latent, new_latent, new_rope, latent_cache, jnp.swapaxes(rope_cache, 1, 2), lengths,
        q_up, kv_up, out_proj,
    ).astype(BF16)


def solution(mesh):
    placed = (
        P("batch", None),
        P("batch", None),
        P("batch", None),
        P("batch", None, None),
        P("batch", None, None),
        P("batch"),
        P(("heads", "batch"), None),
        P(("heads", "batch"), None),
        P(("heads", "batch"), None),
    )
    return jax.shard_map(
        shards, mesh=mesh, in_specs=placed, out_specs=P("batch", "heads"), check_vma=False
    )
```

```python
import functools
import math

import jax
import jax.numpy as jnp
from jax import lax
from jax.experimental import pallas as pl
from jax.experimental.pallas import tpu as pltpu
from jax.sharding import PartitionSpec as P

QR = 1536
KVR = 512
NOPE = 128
ROPE = 64
CACHE = 1024
QROWS = 12
SLOT = 16
XS, ZS = 4, 4
YS = 8
QC = QR // 4
OUT_K = 4096
F32 = jnp.float32
BF16 = jnp.bfloat16
NT = (((1,), (1,)), ((), ()))


def dot_nt(a, b):
    return lax.dot_general(a, b, NT, preferred_element_type=F32)


def dot_nn(a, b):
    return jnp.dot(a, b, preferred_element_type=F32)


def kernel(
    ql_hbm, nl_hbm, nr_hbm, lat_hbm, rope_hbm, len_hbm, qup_hbm, kvup_hbm, outp_hbm, y_ref,
    ql_in, nl_in, nr_in, len_in, qup_in, outp_in, lat, rope,
    qbuf, qlbuf, qsend, qrecv, kvbuf, wbuf, sel, sel_out, vx, vh, ysend, yrecv,
    in_sem, q_send, q_recv, ql_send, ql_recv, qx_send, qx_recv, kvz_send, kvb_send, kv_recv,
    w_send, w_recv, vx_send, vx_recv, vh_send, vh_recv, y_send, y_recv,
):
    h = lax.axis_index("heads")
    b = lax.axis_index("batch")
    x, z, c = b // 8, (b // 2) % 4, b % 2
    y, up = h % YS, h // YS

    def index(xx, zz, cc):
        return xx * 8 + zz * 2 + cc

    zk = [z, z + 1 - 2 * (z % 2), (z + 2) % 4, 3 - z]
    xr, xl, xo = (x + 1) % 4, (x + 3) % 4, (x + 2) % 4
    right, left, sibling = index(xr, z, c), index(xl, z, c), index(x, z, 1 - c)
    mine, theirs = x * 2 + c, x * 2 + 1 - c
    own = z * 2 + c

    loads = [
        pltpu.make_async_copy(source, target, in_sem.at[i])
        for i, (source, target) in enumerate(
            [
                (qup_hbm, qup_in), (ql_hbm, ql_in), (kvup_hbm, kvbuf.at[mine, z]),
                (nl_hbm, nl_in), (nr_hbm, nr_in), (len_hbm, len_in), (outp_hbm, outp_in),
                (lat_hbm, lat), (rope_hbm, rope),
            ]
        )
    ]
    for load in loads:
        load.start()

    barrier = pltpu.get_barrier_semaphore()

    def greet(target):
        pl.semaphore_signal(barrier, inc=1, device_id={"batch": target})

    across = (1 - up) * YS + y
    for k in range(ZS):
        pl.semaphore_signal(
            barrier, inc=1, device_id={"heads": across, "batch": index(x, zk[k], c)}
        )

    @pl.loop(1, YS)
    def _(i):
        pl.semaphore_signal(barrier, inc=1, device_id={"heads": up * YS + (y + i) % YS})

    for k in range(1, ZS):
        greet(index(x, zk[k], c))
        greet(index(x, zk[k], 1 - c))
    greet(right)
    greet(left)
    greet(sibling)

    loads[0].wait()
    qbuf[x, :, :] = jnp.concatenate([qup_in[...], jnp.zeros((SLOT - QROWS, QR), BF16)], axis=0)
    loads[1].wait()
    ql_own = ql_in[...].astype(F32)
    qlbuf[own, :, :] = jnp.concatenate(
        [ql_own[:, j * QC: (j + 1) * QC] for j in range(4)], axis=0
    ).astype(BF16)
    loads[2].wait()

    pl.semaphore_wait(barrier, ZS + YS - 1 + 6 + 2 + 1)

    def remote(source, target, send_sem, recv_sem, device):
        return pltpu.make_async_remote_copy(
            src_ref=source, dst_ref=target, send_sem=send_sem, recv_sem=recv_sem,
            device_id=device,
        )

    def push(ref, send_sem, recv_sem, target):
        remote(ref, ref, send_sem, recv_sem, {"batch": target}).start()

    def arrive(ref, recv_sem):
        pltpu.make_async_copy(ref, ref, recv_sem).wait()

    for target in (right, left):
        push(qbuf.at[x], q_send.at[0], q_recv.at[x, 0], target)
    for k in range(1, ZS):
        push(kvbuf.at[mine, z], kvz_send.at[0], kv_recv.at[z], index(x, zk[k], c))
    for k in range(1, ZS):
        push(qlbuf.at[own], ql_send.at[0], ql_recv.at[own], index(x, zk[k], c))
    push(qlbuf.at[own], ql_send.at[0], ql_recv.at[own], sibling)

    @pl.loop(0, 32)
    def _(t):
        x_t = t % 4
        first_row = QROWS * ((x_t % 2) * 8 + (t // 8) * 2 + (t // 4) % 2)
        shape = (SLOT, 2 * NOPE + 2 * ROPE)
        within = lax.broadcasted_iota(jnp.int32, shape, 0)
        col = lax.broadcasted_iota(jnp.int32, shape, 1)
        row = within + first_row
        nope = (row < NOPE) & (col == row + (x_t // 2) * NOPE)
        rotary = row - NOPE
        swapped = (rotary + ROPE // 2) % ROPE
        rope_at = (row >= NOPE) & (
            (col == 2 * NOPE + rotary) | (col == 2 * NOPE + ROPE + swapped)
        )
        block = jnp.where((within < QROWS) & (nope | rope_at), 1.0, 0.0).astype(BF16)
        sel[pl.ds(pl.multiple_of(t * SLOT, SLOT), SLOT), :] = block

    arrive(qbuf.at[xl], q_recv.at[xl, 0])
    push(qbuf.at[xl, :, pl.ds(0, QR // 2)], q_send.at[0], q_recv.at[xl, 0], right)
    arrive(qbuf.at[xr], q_recv.at[xr, 0])
    push(qbuf.at[xr, :, pl.ds(QR // 2, QR // 2)], q_send.at[0], q_recv.at[xr, 1], left)

    for k in range(1, ZS):
        arrive(kvbuf.at[mine, zk[k]], kv_recv.at[zk[k]])
    for target in (right, left):
        push(kvbuf.at[mine], kvb_send.at[0], kv_recv.at[4 + x], target)
    push(kvbuf.at[mine], kvb_send.at[0], kv_recv.at[4 + x], sibling)
    for k in range(1, ZS):
        slot = zk[k] * 2 + c
        arrive(qlbuf.at[slot], ql_recv.at[slot])
        push(qlbuf.at[slot], ql_send.at[0], ql_recv.at[slot], sibling)

    loads[6].wait()
    wbuf[mine, :, :] = jnp.concatenate([outp_in[...], jnp.zeros((2, OUT_K), BF16)], axis=0)

    from_left, from_right, from_far = xl * 2 + c, xr * 2 + c, xo * 2 + c
    arrive(kvbuf.at[from_left], kv_recv.at[4 + xl])
    push(kvbuf.at[from_left, pl.ds(0, 2)], kvb_send.at[0], kv_recv.at[12], right)
    push(kvbuf.at[from_left], kvb_send.at[0], kv_recv.at[8 + xl], sibling)
    arrive(kvbuf.at[from_right], kv_recv.at[4 + xr])
    push(kvbuf.at[from_right, pl.ds(2, 2)], kvb_send.at[0], kv_recv.at[13], left)
    push(kvbuf.at[from_right], kvb_send.at[0], kv_recv.at[8 + xr], sibling)

    for target in (right, left, sibling):
        push(wbuf.at[mine], w_send.at[0], w_recv.at[mine, 0], target)

    arrive(qbuf.at[xo, :, pl.ds(0, QR // 2)], q_recv.at[xo, 0])
    arrive(qbuf.at[xo, :, pl.ds(QR // 2, QR // 2)], q_recv.at[xo, 1])
    for zz in range(ZS):
        slot = zz * 2 + 1 - c
        arrive(qlbuf.at[slot], ql_recv.at[slot])
    ql_rows = qlbuf[...].reshape(8 * SLOT, QC)
    block_of = (lax.broadcasted_iota(jnp.int32, (8 * SLOT, XS * SLOT), 0) // 4) % 4
    partial = jnp.zeros((8 * SLOT, XS * SLOT), F32)
    for j in range(4):
        columns = qbuf[:, :, j * QC: (j + 1) * QC].reshape(XS * SLOT, QC)
        partial = jnp.where(block_of == j, dot_nt(ql_rows, columns), partial)
    partial = partial.reshape(8, SLOT, XS * SLOT)
    partial = partial[:, 0:8] + partial[:, 8:16]
    partial = jnp.concatenate([partial, partial], axis=2)
    lane_of = lax.broadcasted_iota(jnp.int32, (8, 8, 128), 2)
    qsend[...] = jnp.where(lane_of // 64 == c, partial, 0.0)
    for k in range(1, ZS):
        for cc in (c, 1 - c):
            slot = zk[k] * 2 + cc
            remote(
                qsend.at[slot], qrecv.at[own], qx_send.at[0], qx_recv.at[own],
                {"batch": index(x, zk[k], cc)},
            ).start()
    remote(
        qsend.at[z * 2 + 1 - c], qrecv.at[own], qx_send.at[0], qx_recv.at[own], {"batch": sibling}
    ).start()
    qrecv[own, :, :] = qsend[own]

    arrive(kvbuf.at[from_far, pl.ds(0, 2)], kv_recv.at[12])
    arrive(kvbuf.at[from_far, pl.ds(2, 2)], kv_recv.at[13])
    push(kvbuf.at[from_far], kvb_send.at[0], kv_recv.at[8 + xo], sibling)

    row8 = lax.broadcasted_iota(jnp.int32, (8, 1), 0)
    row_of = row8 % 4
    low = row8 < 4
    for load in loads[3:6]:
        load.wait()
    length = jnp.zeros((8, 1), jnp.int32)
    for r in range(4):
        length = jnp.where(row_of == r, len_in[r], length)

    lane64 = lax.broadcasted_iota(jnp.int32, (8, ROPE), 1)
    inverse = jnp.exp((lane64 % (ROPE // 2)).astype(F32) * (-2.0 * math.log(50000.0) / ROPE))
    angles = length.astype(F32) * inverse
    cosine = jnp.cos(angles)
    sine = jnp.sin(angles)
    sine = jnp.where(lane64 < ROPE // 2, -sine, sine)

    def twice(values):
        return jnp.concatenate([values, values], axis=0)

    nr8 = twice(nr_in[...].astype(F32))
    nr_swapped = jnp.concatenate([nr8[:, ROPE // 2:], nr8[:, : ROPE // 2]], axis=1)
    key_new = (nr8 * cosine + nr_swapped * sine).astype(BF16).astype(F32)
    nl8 = twice(nl_in[...].astype(F32))

    for k in range(1, ZS):
        for cc in (c, 1 - c):
            slot = zk[k] * 2 + cc
            arrive(qrecv.at[slot], qx_recv.at[slot])
    arrive(qrecv.at[z * 2 + 1 - c], qx_recv.at[z * 2 + 1 - c])
    pieces = []
    for zz in range(ZS):
        piece = qrecv[2 * zz] + qrecv[2 * zz + 1]
        pieces.append(piece + pltpu.roll(piece, 4, 0))
    q_all = jnp.concatenate(pieces, axis=1)
    lane_q = lax.broadcasted_iota(jnp.int32, (8, 512), 1)
    q_all = jnp.where((lane_q % 64 < 32) == low, q_all, 0.0)
    q_hi = q_all.astype(BF16)
    q_lo = (q_all - q_hi.astype(F32)).astype(BF16)
    selection = sel[...]
    q_sel = dot_nn(q_hi, selection) + dot_nn(q_lo, selection)
    q_nope = q_sel[:, 0: 2 * NOPE].astype(BF16)
    query_rope = (
        q_sel[:, 2 * NOPE: 2 * NOPE + ROPE] * cosine + q_sel[:, 2 * NOPE + ROPE:] * sine
    ).astype(BF16)

    arrive(kvbuf.at[theirs], kv_recv.at[4 + x])
    for xx in (xl, xr, xo):
        block = xx * 2 + 1 - c
        arrive(kvbuf.at[block], kv_recv.at[8 + xx])

    def kv_rows(xx):
        return jnp.concatenate(
            [kvbuf[xx * 2 + cc, zz] for zz in range(ZS) for cc in range(2)], axis=0
        )

    query_abs = (
        dot_nn(q_nope[:, :NOPE], kv_rows(0)) + dot_nn(q_nope[:, NOPE:], kv_rows(2))
    ).astype(BF16)

    loads[7].wait()
    loads[8].wait()
    scale = (NOPE + ROPE) ** (-0.5)
    scores = jnp.zeros((8, CACHE), F32)
    for r in range(4):
        of_row = dot_nt(query_abs, lat[r]) + dot_nn(query_rope, rope[r])
        scores = jnp.where(row_of == r, of_row, scores)
    score_new = scale * (
        jnp.sum(query_abs.astype(F32) * nl8, axis=1, keepdims=True)
        + jnp.sum(query_rope.astype(F32) * key_new, axis=1, keepdims=True)
    )
    position = lax.broadcasted_iota(jnp.int32, (8, CACHE), 1)
    scores = jnp.where(position < length, scores * scale, -1e30)
    top = jnp.maximum(jnp.max(scores, axis=1, keepdims=True), score_new)
    old = jnp.exp(scores - top)
    new = jnp.exp(score_new - top)
    denom = jnp.sum(old, axis=1, keepdims=True) + new
    probs = (old / denom).astype(BF16)
    prob_new = (new / denom).astype(BF16).astype(F32)
    context = jnp.zeros((8, KVR), F32)
    for r in range(4):
        context = jnp.where(row_of == r, dot_nn(probs, lat[r]), context)
    context = (context + prob_new * nl8).astype(BF16)
    value = jnp.where(low, dot_nt(context, kv_rows(1)), dot_nt(context, kv_rows(3)))
    z_of_8 = up * ZS + z
    vx[z_of_8, :, :] = value.astype(BF16).astype(F32)

    def vx_push(heads, k):
        remote(
            vx.at[z_of_8], vx.at[z_of_8], vx_send.at[0], vx_recv.at[z_of_8],
            {"heads": heads, "batch": index(x, zk[k], c)},
        ).start()

    for k in range(ZS):
        vx_push(across, k)
    for k in range(1, ZS):
        vx_push(h, k)

    arrive(wbuf.at[from_left], w_recv.at[from_left, 0])
    push(
        wbuf.at[from_left, :, pl.ds(0, OUT_K // 2)], w_send.at[0], w_recv.at[from_left, 0], right
    )
    push(wbuf.at[from_left], w_send.at[0], w_recv.at[from_left, 0], sibling)
    arrive(wbuf.at[from_right], w_recv.at[from_right, 0])
    push(
        wbuf.at[from_right, :, pl.ds(OUT_K // 2, OUT_K // 2)], w_send.at[0],
        w_recv.at[from_right, 1], left,
    )
    push(wbuf.at[from_right], w_send.at[0], w_recv.at[from_right, 0], sibling)

    for k in range(1, ZS):
        arrive(vx.at[up * ZS + zk[k]], vx_recv.at[up * ZS + zk[k]])
    for k in range(ZS):
        slot = (1 - up) * ZS + zk[k]
        arrive(vx.at[slot], vx_recv.at[slot])
    vh[y, :, :] = vx[...].reshape(64, 128).astype(BF16)

    for i in (4, 3, 5, 2, 6, 1, 7):
        remote(
            vh.at[y], vh.at[y], vh_send.at[0], vh_recv.at[y],
            {"heads": up * YS + (y + i) % YS},
        ).start()

    arrive(wbuf.at[from_far, :, pl.ds(0, OUT_K // 2)], w_recv.at[from_far, 0])
    arrive(wbuf.at[from_far, :, pl.ds(OUT_K // 2, OUT_K // 2)], w_recv.at[from_far, 1])
    push(wbuf.at[from_far], w_send.at[0], w_recv.at[from_far, 0], sibling)

    @pl.loop(0, 32)
    def _(t):
        start = (((t // 2) % 4) * 8 + (t // 8) * 2 + t % 2) * 14
        col = lax.broadcasted_iota(jnp.int32, (SLOT, 448), 1) - start
        row = lax.broadcasted_iota(jnp.int32, (SLOT, 448), 0)
        block = jnp.where((col == row) & (row < 14), 1.0, 0.0).astype(BF16)
        sel_out[pl.ds(pl.multiple_of(t * SLOT, SLOT), SLOT), :] = block

    for xx in (x, xl, xr, xo):
        block = xx * 2 + 1 - c
        arrive(wbuf.at[block], w_recv.at[block, 0])

    for i in (1, 7, 2, 6, 3, 5, 4):
        other = (y + i) % YS
        arrive(vh.at[other], vh_recv.at[other])

    row32 = lax.broadcasted_iota(jnp.int32, (32, 128), 0)
    is_low = (row32 % 8) < 4
    zero = jnp.zeros((32, 128), BF16)
    chunks = []
    for hh in range(2 * YS):
        block = vh[hh % YS, hh // YS * 32: hh // YS * 32 + 32]
        chunks.append(jnp.where(is_low, block, zero))
        chunks.append(jnp.where(is_low, zero, block))
    y_all = dot_nt(jnp.concatenate(chunks, axis=1), wbuf[...].reshape(8 * SLOT, OUT_K))
    ysend[...] = y_all.reshape(ZS, 8, 128)

    for k in range(1, ZS):
        remote(
            ysend.at[zk[k]], yrecv.at[z], y_send.at[0], y_recv.at[z],
            {"batch": index(x, zk[k], c)},
        ).start()
    yrecv[z, :, :] = ysend[z]
    for k in range(1, ZS):
        arrive(yrecv.at[zk[k]], y_recv.at[zk[k]])
    pieces = []
    for zz in range(ZS):
        piece = yrecv[zz]
        pieces.append(piece + pltpu.roll(piece, 4, 0))
    summed = jnp.concatenate(pieces, axis=1).astype(BF16)
    y_ref[...] = dot_nn(summed, sel_out[...])[0:4]

    for ref, sem in (
        (qbuf.at[0:3], q_send), (kvbuf.at[0, 0:3], kvz_send), (kvbuf.at[0:7], kvb_send),
        (qlbuf.at[0:7], ql_send), (qsend.at[0:7], qx_send), (wbuf.at[0:7], w_send),
        (vx.at[0:7], vx_send), (vh.at[0:7], vh_send), (ysend.at[0:3], y_send),
    ):
        arrive(ref, sem.at[0])


def shards(
    q_latent, new_latent, new_rope, latent_cache, rope_cache, lengths, q_up, kv_up, out_proj
):
    hbm = pl.BlockSpec(memory_space=pltpu.HBM)
    dma = pltpu.SemaphoreType.DMA
    return pl.pallas_call(
        kernel,
        out_shape=jax.ShapeDtypeStruct((4, 448), F32),
        in_specs=[hbm] * 9,
        out_specs=pl.BlockSpec(memory_space=pltpu.VMEM),
        scratch_shapes=[
            pltpu.VMEM((4, QR), BF16),
            pltpu.VMEM((4, KVR), BF16),
            pltpu.VMEM((4, ROPE), BF16),
            pltpu.SMEM((4,), jnp.int32),
            pltpu.VMEM((QROWS, QR), BF16),
            pltpu.VMEM((14, OUT_K), BF16),
            pltpu.VMEM((4, CACHE, KVR), BF16),
            pltpu.VMEM((4, ROPE, CACHE), BF16),
            pltpu.VMEM((XS, SLOT, QR), BF16),
            pltpu.VMEM((8, SLOT, QC), BF16),
            pltpu.VMEM((8, 8, 128), F32),
            pltpu.VMEM((8, 8, 128), F32),
            pltpu.VMEM((8, ZS, SLOT, KVR), BF16),
            pltpu.VMEM((8, SLOT, OUT_K), BF16),
            pltpu.VMEM((512, 2 * NOPE + 2 * ROPE), BF16),
            pltpu.VMEM((512, 448), BF16),
            pltpu.VMEM((2 * ZS, 8, 128), F32),
            pltpu.VMEM((YS, 64, 128), BF16),
            pltpu.VMEM((ZS, 8, 128), F32),
            pltpu.VMEM((ZS, 8, 128), F32),
            dma((9,)),
            dma((1,)), dma((XS, 2)),
            dma((1,)), dma((8,)),
            dma((1,)), dma((8,)),
            dma((1,)), dma((1,)), dma((14,)),
            dma((1,)), dma((8, 2)),
            dma((1,)), dma((2 * ZS,)),
            dma((1,)), dma((YS,)),
            dma((1,)), dma((ZS,)),
        ],
        compiler_params=pltpu.CompilerParams(
            collective_id=0, has_side_effects=True, vmem_limit_bytes=60 * 2**20
        ),
        cost_estimate=pl.CostEstimate(
            flops=4 * 10**8, bytes_accessed=5 * 10**6, transcendentals=10**4
        ),
    )(
        q_latent, new_latent, new_rope, latent_cache, jnp.swapaxes(rope_cache, 1, 2), lengths,
        q_up, kv_up, out_proj,
    ).astype(BF16)


def solution(mesh):
    placed = (
        P("batch", None),
        P("batch", None),
        P("batch", None),
        P("batch", None, None),
        P("batch", None, None),
        P("batch"),
        P(("heads", "batch"), None),
        P(("heads", "batch"), None),
        P(("heads", "batch"), None),
    )
    return jax.shard_map(
        shards, mesh=mesh, in_specs=placed, out_specs=P("batch", "heads"), check_vma=False
    )
```

```python
import functools
import math

import jax
import jax.numpy as jnp
from jax import lax
from jax.experimental import pallas as pl
from jax.experimental.pallas import tpu as pltpu
from jax.sharding import PartitionSpec as P

QR = 1536
KVR = 512
NOPE = 128
ROPE = 64
CACHE = 1024
QROWS = 12
SLOT = 16
XS, ZS = 4, 4
YS = 8
QC = QR // 4
OUT_K = 4096
F32 = jnp.float32
BF16 = jnp.bfloat16
NT = (((1,), (1,)), ((), ()))


def dot_nt(a, b):
    return lax.dot_general(a, b, NT, preferred_element_type=F32)


def dot_nn(a, b):
    return jnp.dot(a, b, preferred_element_type=F32)


def kernel(
    ql_hbm, nl_hbm, nr_hbm, lat_hbm, rope_hbm, len_hbm, qup_hbm, kvup_hbm, outp_hbm, y_ref,
    ql_in, nl_in, nr_in, len_in, qup_in, outp_in, lat, rope,
    qbuf, qlbuf, qsend, qrecv, kvbuf, wbuf, sel, sel_out, vx, vh, ysend, yrecv,
    in_sem, q_send, q_recv, ql_send, ql_recv, qx_send, qx_recv, kvz_send, kvb_send, kv_recv,
    w_send, w_recv, vx_send, vx_recv, vh_send, vh_recv, y_send, y_recv,
):
    h = lax.axis_index("heads")
    b = lax.axis_index("batch")
    x, z, c = b // 8, (b // 2) % 4, b % 2
    y, up = h % YS, h // YS

    def index(xx, zz, cc):
        return xx * 8 + zz * 2 + cc

    zk = [z, z + 1 - 2 * (z % 2), (z + 2) % 4, 3 - z]
    xr, xl, xo = (x + 1) % 4, (x + 3) % 4, (x + 2) % 4
    right, left, sibling = index(xr, z, c), index(xl, z, c), index(x, z, 1 - c)
    mine, theirs = x * 2 + c, x * 2 + 1 - c
    own = z * 2 + c

    loads = [
        pltpu.make_async_copy(source, target, in_sem.at[i])
        for i, (source, target) in enumerate(
            [
                (qup_hbm, qup_in), (ql_hbm, ql_in), (kvup_hbm, kvbuf.at[mine, z]),
                (nl_hbm, nl_in), (nr_hbm, nr_in), (len_hbm, len_in), (outp_hbm, outp_in),
                (lat_hbm, lat), (rope_hbm, rope),
            ]
        )
    ]
    barrier = pltpu.get_barrier_semaphore()

    def greet(target):
        pl.semaphore_signal(barrier, inc=1, device_id={"batch": target})

    across = (1 - up) * YS + y
    for k in range(ZS):
        pl.semaphore_signal(
            barrier, inc=1, device_id={"heads": across, "batch": index(x, zk[k], c)}
        )

    @pl.loop(1, YS)
    def _(i):
        pl.semaphore_signal(barrier, inc=1, device_id={"heads": up * YS + (y + i) % YS})

    for k in range(1, ZS):
        greet(index(x, zk[k], c))
        greet(index(x, zk[k], 1 - c))
    greet(right)
    greet(left)
    greet(sibling)

    for i in (2, 0, 1, 3, 4, 5, 6, 7, 8):
        loads[i].start()
    loads[2].wait()
    pl.semaphore_wait(barrier, ZS + YS - 1 + 6 + 2 + 1)

    def remote(source, target, send_sem, recv_sem, device):
        return pltpu.make_async_remote_copy(
            src_ref=source, dst_ref=target, send_sem=send_sem, recv_sem=recv_sem,
            device_id=device,
        )

    def push(ref, send_sem, recv_sem, target):
        remote(ref, ref, send_sem, recv_sem, {"batch": target}).start()

    def arrive(ref, recv_sem):
        pltpu.make_async_copy(ref, ref, recv_sem).wait()

    for k in (3, 2, 1):
        push(kvbuf.at[mine, z], kvz_send.at[0], kv_recv.at[z], index(x, zk[k], c))

    loads[0].wait()
    qbuf[x, :, :] = jnp.concatenate([qup_in[...], jnp.zeros((SLOT - QROWS, QR), BF16)], axis=0)
    for target in (right, left):
        push(qbuf.at[x], q_send.at[0], q_recv.at[x, 0], target)
    loads[1].wait()
    ql_own = ql_in[...].astype(F32)
    qlbuf[own, :, :] = jnp.concatenate(
        [ql_own[:, j * QC: (j + 1) * QC] for j in range(4)], axis=0
    ).astype(BF16)
    for k in range(1, ZS):
        push(qlbuf.at[own], ql_send.at[0], ql_recv.at[own], index(x, zk[k], c))
    push(qlbuf.at[own], ql_send.at[0], ql_recv.at[own], sibling)

    @pl.loop(0, 32)
    def _(t):
        x_t = t % 4
        first_row = QROWS * ((x_t % 2) * 8 + (t // 8) * 2 + (t // 4) % 2)
        shape = (SLOT, 2 * NOPE + 2 * ROPE)
        within = lax.broadcasted_iota(jnp.int32, shape, 0)
        col = lax.broadcasted_iota(jnp.int32, shape, 1)
        row = within + first_row
        nope = (row < NOPE) & (col == row + (x_t // 2) * NOPE)
        rotary = row - NOPE
        swapped = (rotary + ROPE // 2) % ROPE
        rope_at = (row >= NOPE) & (
            (col == 2 * NOPE + rotary) | (col == 2 * NOPE + ROPE + swapped)
        )
        block = jnp.where((within < QROWS) & (nope | rope_at), 1.0, 0.0).astype(BF16)
        sel[pl.ds(pl.multiple_of(t * SLOT, SLOT), SLOT), :] = block

    arrive(qbuf.at[xl], q_recv.at[xl, 0])
    push(qbuf.at[xl, :, pl.ds(0, QR // 2)], q_send.at[0], q_recv.at[xl, 0], right)
    arrive(qbuf.at[xr], q_recv.at[xr, 0])
    push(qbuf.at[xr, :, pl.ds(QR // 2, QR // 2)], q_send.at[0], q_recv.at[xr, 1], left)

    for k in range(1, ZS):
        arrive(kvbuf.at[mine, zk[k]], kv_recv.at[zk[k]])
    for target in (right, left):
        push(kvbuf.at[mine], kvb_send.at[0], kv_recv.at[4 + x], target)
    push(kvbuf.at[mine], kvb_send.at[0], kv_recv.at[4 + x], sibling)
    for k in range(1, ZS):
        slot = zk[k] * 2 + c
        arrive(qlbuf.at[slot], ql_recv.at[slot])
        push(qlbuf.at[slot], ql_send.at[0], ql_recv.at[slot], sibling)

    loads[6].wait()
    wbuf[mine, :, :] = jnp.concatenate([outp_in[...], jnp.zeros((2, OUT_K), BF16)], axis=0)

    from_left, from_right, from_far = xl * 2 + c, xr * 2 + c, xo * 2 + c
    arrive(kvbuf.at[from_left], kv_recv.at[4 + xl])
    push(kvbuf.at[from_left, pl.ds(0, 2)], kvb_send.at[0], kv_recv.at[12], right)
    push(kvbuf.at[from_left], kvb_send.at[0], kv_recv.at[8 + xl], sibling)
    arrive(kvbuf.at[from_right], kv_recv.at[4 + xr])
    push(kvbuf.at[from_right, pl.ds(2, 2)], kvb_send.at[0], kv_recv.at[13], left)
    push(kvbuf.at[from_right], kvb_send.at[0], kv_recv.at[8 + xr], sibling)

    for target in (right, left, sibling):
        push(wbuf.at[mine], w_send.at[0], w_recv.at[mine, 0], target)

    arrive(qbuf.at[xo, :, pl.ds(0, QR // 2)], q_recv.at[xo, 0])
    arrive(qbuf.at[xo, :, pl.ds(QR // 2, QR // 2)], q_recv.at[xo, 1])
    for zz in range(ZS):
        slot = zz * 2 + 1 - c
        arrive(qlbuf.at[slot], ql_recv.at[slot])
    ql_rows = qlbuf[...].reshape(8 * SLOT, QC)
    block_of = (lax.broadcasted_iota(jnp.int32, (8 * SLOT, XS * SLOT), 0) // 4) % 4
    partial = jnp.zeros((8 * SLOT, XS * SLOT), F32)
    for j in range(4):
        columns = qbuf[:, :, j * QC: (j + 1) * QC].reshape(XS * SLOT, QC)
        partial = jnp.where(block_of == j, dot_nt(ql_rows, columns), partial)
    partial = partial.reshape(8, SLOT, XS * SLOT)
    partial = partial[:, 0:8] + partial[:, 8:16]
    partial = jnp.concatenate([partial, partial], axis=2)
    lane_of = lax.broadcasted_iota(jnp.int32, (8, 8, 128), 2)
    qsend[...] = jnp.where(lane_of // 64 == c, partial, 0.0)
    for k in range(1, ZS):
        for cc in (c, 1 - c):
            slot = zk[k] * 2 + cc
            remote(
                qsend.at[slot], qrecv.at[own], qx_send.at[0], qx_recv.at[own],
                {"batch": index(x, zk[k], cc)},
            ).start()
    remote(
        qsend.at[z * 2 + 1 - c], qrecv.at[own], qx_send.at[0], qx_recv.at[own], {"batch": sibling}
    ).start()
    qrecv[own, :, :] = qsend[own]

    arrive(kvbuf.at[from_far, pl.ds(0, 2)], kv_recv.at[12])
    arrive(kvbuf.at[from_far, pl.ds(2, 2)], kv_recv.at[13])
    push(kvbuf.at[from_far], kvb_send.at[0], kv_recv.at[8 + xo], sibling)

    row8 = lax.broadcasted_iota(jnp.int32, (8, 1), 0)
    row_of = row8 % 4
    low = row8 < 4
    for load in loads[3:6]:
        load.wait()
    length = jnp.zeros((8, 1), jnp.int32)
    for r in range(4):
        length = jnp.where(row_of == r, len_in[r], length)

    lane64 = lax.broadcasted_iota(jnp.int32, (8, ROPE), 1)
    inverse = jnp.exp((lane64 % (ROPE // 2)).astype(F32) * (-2.0 * math.log(50000.0) / ROPE))
    angles = length.astype(F32) * inverse
    cosine = jnp.cos(angles)
    sine = jnp.sin(angles)
    sine = jnp.where(lane64 < ROPE // 2, -sine, sine)

    def twice(values):
        return jnp.concatenate([values, values], axis=0)

    nr8 = twice(nr_in[...].astype(F32))
    nr_swapped = jnp.concatenate([nr8[:, ROPE // 2:], nr8[:, : ROPE // 2]], axis=1)
    key_new = (nr8 * cosine + nr_swapped * sine).astype(BF16).astype(F32)
    nl8 = twice(nl_in[...].astype(F32))

    for k in range(1, ZS):
        for cc in (c, 1 - c):
            slot = zk[k] * 2 + cc
            arrive(qrecv.at[slot], qx_recv.at[slot])
    arrive(qrecv.at[z * 2 + 1 - c], qx_recv.at[z * 2 + 1 - c])
    pieces = []
    for zz in range(ZS):
        piece = qrecv[2 * zz] + qrecv[2 * zz + 1]
        pieces.append(piece + pltpu.roll(piece, 4, 0))
    q_all = jnp.concatenate(pieces, axis=1)
    lane_q = lax.broadcasted_iota(jnp.int32, (8, 512), 1)
    q_all = jnp.where((lane_q % 64 < 32) == low, q_all, 0.0)
    q_hi = q_all.astype(BF16)
    q_lo = (q_all - q_hi.astype(F32)).astype(BF16)
    selection = sel[...]
    q_sel = dot_nn(q_hi, selection) + dot_nn(q_lo, selection)
    q_nope = q_sel[:, 0: 2 * NOPE].astype(BF16)
    query_rope = (
        q_sel[:, 2 * NOPE: 2 * NOPE + ROPE] * cosine + q_sel[:, 2 * NOPE + ROPE:] * sine
    ).astype(BF16)

    arrive(kvbuf.at[theirs], kv_recv.at[4 + x])
    for xx in (xl, xr, xo):
        block = xx * 2 + 1 - c
        arrive(kvbuf.at[block], kv_recv.at[8 + xx])

    def kv_rows(xx):
        return jnp.concatenate(
            [kvbuf[xx * 2 + cc, zz] for zz in range(ZS) for cc in range(2)], axis=0
        )

    query_abs = (
        dot_nn(q_nope[:, :NOPE], kv_rows(0)) + dot_nn(q_nope[:, NOPE:], kv_rows(2))
    ).astype(BF16)

    loads[7].wait()
    loads[8].wait()
    scale = (NOPE + ROPE) ** (-0.5)
    scores = jnp.zeros((8, CACHE), F32)
    for r in range(4):
        of_row = dot_nt(query_abs, lat[r]) + dot_nn(query_rope, rope[r])
        scores = jnp.where(row_of == r, of_row, scores)
    score_new = scale * (
        jnp.sum(query_abs.astype(F32) * nl8, axis=1, keepdims=True)
        + jnp.sum(query_rope.astype(F32) * key_new, axis=1, keepdims=True)
    )
    position = lax.broadcasted_iota(jnp.int32, (8, CACHE), 1)
    scores = jnp.where(position < length, scores * scale, -1e30)
    top = jnp.maximum(jnp.max(scores, axis=1, keepdims=True), score_new)
    old = jnp.exp(scores - top)
    new = jnp.exp(score_new - top)
    denom = jnp.sum(old, axis=1, keepdims=True) + new
    probs = (old / denom).astype(BF16)
    prob_new = (new / denom).astype(BF16).astype(F32)
    context = jnp.zeros((8, KVR), F32)
    for r in range(4):
        context = jnp.where(row_of == r, dot_nn(probs, lat[r]), context)
    context = (context + prob_new * nl8).astype(BF16)
    value = jnp.where(low, dot_nt(context, kv_rows(1)), dot_nt(context, kv_rows(3)))
    z_of_8 = up * ZS + z
    vx[z_of_8, :, :] = value.astype(BF16).astype(F32)

    def vx_push(heads, k):
        remote(
            vx.at[z_of_8], vx.at[z_of_8], vx_send.at[0], vx_recv.at[z_of_8],
            {"heads": heads, "batch": index(x, zk[k], c)},
        ).start()

    for k in range(ZS):
        vx_push(across, k)
    for k in range(1, ZS):
        vx_push(h, k)

    arrive(wbuf.at[from_left], w_recv.at[from_left, 0])
    push(
        wbuf.at[from_left, :, pl.ds(0, OUT_K // 2)], w_send.at[0], w_recv.at[from_left, 0], right
    )
    push(wbuf.at[from_left], w_send.at[0], w_recv.at[from_left, 0], sibling)
    arrive(wbuf.at[from_right], w_recv.at[from_right, 0])
    push(
        wbuf.at[from_right, :, pl.ds(OUT_K // 2, OUT_K // 2)], w_send.at[0],
        w_recv.at[from_right, 1], left,
    )
    push(wbuf.at[from_right], w_send.at[0], w_recv.at[from_right, 0], sibling)

    for k in range(1, ZS):
        arrive(vx.at[up * ZS + zk[k]], vx_recv.at[up * ZS + zk[k]])
    for k in range(ZS):
        slot = (1 - up) * ZS + zk[k]
        arrive(vx.at[slot], vx_recv.at[slot])
    vh[y, :, :] = vx[...].reshape(64, 128).astype(BF16)

    for i in (4, 3, 5, 2, 6, 1, 7):
        remote(
            vh.at[y], vh.at[y], vh_send.at[0], vh_recv.at[y],
            {"heads": up * YS + (y + i) % YS},
        ).start()

    arrive(wbuf.at[from_far, :, pl.ds(0, OUT_K // 2)], w_recv.at[from_far, 0])
    arrive(wbuf.at[from_far, :, pl.ds(OUT_K // 2, OUT_K // 2)], w_recv.at[from_far, 1])
    push(wbuf.at[from_far], w_send.at[0], w_recv.at[from_far, 0], sibling)

    @pl.loop(0, 32)
    def _(t):
        start = (((t // 2) % 4) * 8 + (t // 8) * 2 + t % 2) * 14
        col = lax.broadcasted_iota(jnp.int32, (SLOT, 448), 1) - start
        row = lax.broadcasted_iota(jnp.int32, (SLOT, 448), 0)
        block = jnp.where((col == row) & (row < 14), 1.0, 0.0).astype(BF16)
        sel_out[pl.ds(pl.multiple_of(t * SLOT, SLOT), SLOT), :] = block

    for xx in (x, xl, xr, xo):
        block = xx * 2 + 1 - c
        arrive(wbuf.at[block], w_recv.at[block, 0])

    for i in (1, 7, 2, 6, 3, 5, 4):
        other = (y + i) % YS
        arrive(vh.at[other], vh_recv.at[other])

    row32 = lax.broadcasted_iota(jnp.int32, (32, 128), 0)
    is_low = (row32 % 8) < 4
    zero = jnp.zeros((32, 128), BF16)
    chunks = []
    for hh in range(2 * YS):
        block = vh[hh % YS, hh // YS * 32: hh // YS * 32 + 32]
        chunks.append(jnp.where(is_low, block, zero))
        chunks.append(jnp.where(is_low, zero, block))
    y_all = dot_nt(jnp.concatenate(chunks, axis=1), wbuf[...].reshape(8 * SLOT, OUT_K))
    ysend[...] = y_all.reshape(ZS, 8, 128)

    for k in range(1, ZS):
        remote(
            ysend.at[zk[k]], yrecv.at[z], y_send.at[0], y_recv.at[z],
            {"batch": index(x, zk[k], c)},
        ).start()
    yrecv[z, :, :] = ysend[z]
    for k in range(1, ZS):
        arrive(yrecv.at[zk[k]], y_recv.at[zk[k]])
    pieces = []
    for zz in range(ZS):
        piece = yrecv[zz]
        pieces.append(piece + pltpu.roll(piece, 4, 0))
    summed = jnp.concatenate(pieces, axis=1).astype(BF16)
    y_ref[...] = dot_nn(summed, sel_out[...])[0:4]

    for ref, sem in (
        (qbuf.at[0:3], q_send), (kvbuf.at[0, 0:3], kvz_send), (kvbuf.at[0:7], kvb_send),
        (qlbuf.at[0:7], ql_send), (qsend.at[0:7], qx_send), (wbuf.at[0:7], w_send),
        (vx.at[0:7], vx_send), (vh.at[0:7], vh_send), (ysend.at[0:3], y_send),
    ):
        arrive(ref, sem.at[0])


def shards(
    q_latent, new_latent, new_rope, latent_cache, rope_cache, lengths, q_up, kv_up, out_proj
):
    hbm = pl.BlockSpec(memory_space=pltpu.HBM)
    dma = pltpu.SemaphoreType.DMA
    return pl.pallas_call(
        kernel,
        out_shape=jax.ShapeDtypeStruct((4, 448), F32),
        in_specs=[hbm] * 9,
        out_specs=pl.BlockSpec(memory_space=pltpu.VMEM),
        scratch_shapes=[
            pltpu.VMEM((4, QR), BF16),
            pltpu.VMEM((4, KVR), BF16),
            pltpu.VMEM((4, ROPE), BF16),
            pltpu.SMEM((4,), jnp.int32),
            pltpu.VMEM((QROWS, QR), BF16),
            pltpu.VMEM((14, OUT_K), BF16),
            pltpu.VMEM((4, CACHE, KVR), BF16),
            pltpu.VMEM((4, ROPE, CACHE), BF16),
            pltpu.VMEM((XS, SLOT, QR), BF16),
            pltpu.VMEM((8, SLOT, QC), BF16),
            pltpu.VMEM((8, 8, 128), F32),
            pltpu.VMEM((8, 8, 128), F32),
            pltpu.VMEM((8, ZS, SLOT, KVR), BF16),
            pltpu.VMEM((8, SLOT, OUT_K), BF16),
            pltpu.VMEM((512, 2 * NOPE + 2 * ROPE), BF16),
            pltpu.VMEM((512, 448), BF16),
            pltpu.VMEM((2 * ZS, 8, 128), F32),
            pltpu.VMEM((YS, 64, 128), BF16),
            pltpu.VMEM((ZS, 8, 128), F32),
            pltpu.VMEM((ZS, 8, 128), F32),
            dma((9,)),
            dma((1,)), dma((XS, 2)),
            dma((1,)), dma((8,)),
            dma((1,)), dma((8,)),
            dma((1,)), dma((1,)), dma((14,)),
            dma((1,)), dma((8, 2)),
            dma((1,)), dma((2 * ZS,)),
            dma((1,)), dma((YS,)),
            dma((1,)), dma((ZS,)),
        ],
        compiler_params=pltpu.CompilerParams(
            collective_id=0, has_side_effects=True, vmem_limit_bytes=60 * 2**20
        ),
        cost_estimate=pl.CostEstimate(
            flops=4 * 10**8, bytes_accessed=5 * 10**6, transcendentals=10**4
        ),
    )(
        q_latent, new_latent, new_rope, latent_cache, jnp.swapaxes(rope_cache, 1, 2), lengths,
        q_up, kv_up, out_proj,
    ).astype(BF16)


def solution(mesh):
    placed = (
        P("batch", None),
        P("batch", None),
        P("batch", None),
        P("batch", None, None),
        P("batch", None, None),
        P("batch"),
        P(("heads", "batch"), None),
        P(("heads", "batch"), None),
        P(("heads", "batch"), None),
    )
    return jax.shard_map(
        shards, mesh=mesh, in_specs=placed, out_specs=P("batch", "heads"), check_vma=False
    )
```

```python
import functools
import math

import jax
import jax.numpy as jnp
from jax import lax
from jax.experimental import pallas as pl
from jax.experimental.pallas import tpu as pltpu
from jax.sharding import PartitionSpec as P

QR = 1536
KVR = 512
NOPE = 128
ROPE = 64
CACHE = 1024
QROWS = 12
SLOT = 16
XS, ZS = 4, 4
YS = 8
QC = QR // 4
OUT_K = 4096
F32 = jnp.float32
BF16 = jnp.bfloat16
NT = (((1,), (1,)), ((), ()))


def dot_nt(a, b):
    return lax.dot_general(a, b, NT, preferred_element_type=F32)


def dot_nn(a, b):
    return jnp.dot(a, b, preferred_element_type=F32)


def kernel(
    ql_hbm, nl_hbm, nr_hbm, lat_hbm, rope_hbm, len_hbm, qup_hbm, kvup_hbm, outp_hbm, y_ref,
    ql_in, nl_in, nr_in, len_in, qup_in, outp_in, lat, rope,
    qbuf, qlbuf, qsend, qrecv, kvbuf, wbuf, sel, sel_out, vx, vh, ysend, yrecv,
    in_sem, q_send, q_recv, ql_send, ql_recv, qx_send, qx_recv, kvz_send, kvp_send, kvb_send, kv_recv,
    w_send, w_recv, vx_send, vx_recv, vh_send, vh_recv, y_send, y_recv,
):
    h = lax.axis_index("heads")
    b = lax.axis_index("batch")
    x, z, c = b // 8, (b // 2) % 4, b % 2
    y, up = h % YS, h // YS

    def index(xx, zz, cc):
        return xx * 8 + zz * 2 + cc

    zk = [z, z + 1 - 2 * (z % 2), (z + 2) % 4, 3 - z]
    xr, xl, xo = (x + 1) % 4, (x + 3) % 4, (x + 2) % 4
    right, left, sibling = index(xr, z, c), index(xl, z, c), index(x, z, 1 - c)
    mine, theirs = x * 2 + c, x * 2 + 1 - c
    own = z * 2 + c

    loads = [
        pltpu.make_async_copy(source, target, in_sem.at[i])
        for i, (source, target) in enumerate(
            [
                (qup_hbm, qup_in), (ql_hbm, ql_in), (kvup_hbm, kvbuf.at[mine, z]),
                (nl_hbm, nl_in), (nr_hbm, nr_in), (len_hbm, len_in), (outp_hbm, outp_in),
                (lat_hbm, lat), (rope_hbm, rope),
            ]
        )
    ]
    barrier = pltpu.get_barrier_semaphore()

    def greet(target):
        pl.semaphore_signal(barrier, inc=1, device_id={"batch": target})

    across = (1 - up) * YS + y
    for k in range(ZS):
        pl.semaphore_signal(
            barrier, inc=1, device_id={"heads": across, "batch": index(x, zk[k], c)}
        )

    @pl.loop(1, YS)
    def _(i):
        pl.semaphore_signal(barrier, inc=1, device_id={"heads": up * YS + (y + i) % YS})

    for k in range(1, ZS):
        greet(index(x, zk[k], c))
        greet(index(x, zk[k], 1 - c))
    for cc in (c, 1 - c):
        greet(index(xr, z, cc))
        greet(index(xl, z, cc))
    greet(sibling)

    for i in (2, 0, 1, 3, 4, 5, 6, 7, 8):
        loads[i].start()
    loads[2].wait()
    pl.semaphore_wait(barrier, ZS + YS - 1 + 6 + 4 + 1)

    def remote(source, target, send_sem, recv_sem, device):
        return pltpu.make_async_remote_copy(
            src_ref=source, dst_ref=target, send_sem=send_sem, recv_sem=recv_sem,
            device_id=device,
        )

    def push(ref, send_sem, recv_sem, target):
        remote(ref, ref, send_sem, recv_sem, {"batch": target}).start()

    def arrive(ref, recv_sem):
        pltpu.make_async_copy(ref, ref, recv_sem).wait()

    for k in (3, 2, 1):
        push(kvbuf.at[mine, z], kvz_send.at[0], kv_recv.at[z], index(x, zk[k], c))

    loads[0].wait()
    qbuf[x, :, :] = jnp.concatenate([qup_in[...], jnp.zeros((SLOT - QROWS, QR), BF16)], axis=0)
    for target in (right, left):
        push(qbuf.at[x], q_send.at[0], q_recv.at[x, 0], target)
    loads[1].wait()
    ql_own = ql_in[...].astype(F32)
    qlbuf[own, :, :] = jnp.concatenate(
        [ql_own[:, j * QC: (j + 1) * QC] for j in range(4)], axis=0
    ).astype(BF16)
    for k in range(1, ZS):
        push(qlbuf.at[own], ql_send.at[0], ql_recv.at[own], index(x, zk[k], c))
    push(qlbuf.at[own], ql_send.at[0], ql_recv.at[own], sibling)

    @pl.loop(0, 32)
    def _(t):
        x_t = t % 4
        first_row = QROWS * ((x_t % 2) * 8 + (t // 8) * 2 + (t // 4) % 2)
        shape = (SLOT, 2 * NOPE + 2 * ROPE)
        within = lax.broadcasted_iota(jnp.int32, shape, 0)
        col = lax.broadcasted_iota(jnp.int32, shape, 1)
        row = within + first_row
        nope = (row < NOPE) & (col == row + (x_t // 2) * NOPE)
        rotary = row - NOPE
        swapped = (rotary + ROPE // 2) % ROPE
        rope_at = (row >= NOPE) & (
            (col == 2 * NOPE + rotary) | (col == 2 * NOPE + ROPE + swapped)
        )
        block = jnp.where((within < QROWS) & (nope | rope_at), 1.0, 0.0).astype(BF16)
        sel[pl.ds(pl.multiple_of(t * SLOT, SLOT), SLOT), :] = block

    arrive(qbuf.at[xl], q_recv.at[xl, 0])
    push(qbuf.at[xl, :, pl.ds(0, QR // 2)], q_send.at[0], q_recv.at[xl, 0], right)
    arrive(qbuf.at[xr], q_recv.at[xr, 0])
    push(qbuf.at[xr, :, pl.ds(QR // 2, QR // 2)], q_send.at[0], q_recv.at[xr, 1], left)

    def pair(block, half):
        return kvbuf.at[block, pl.ds(2 * half, 2)]

    def kv_pair_out(half):
        for target in (right, left):
            push(pair(mine, half), kvp_send.at[0], kv_recv.at[4 + x * 2 + half], target)

    arrive(kvbuf.at[mine, zk[1]], kv_recv.at[zk[1]])
    kv_pair_out(z // 2)
    for k in range(2, ZS):
        arrive(kvbuf.at[mine, zk[k]], kv_recv.at[zk[k]])
    kv_pair_out(1 - z // 2)
    push(kvbuf.at[mine], kvb_send.at[0], kv_recv.at[12 + x], sibling)
    for k in range(1, ZS):
        slot = zk[k] * 2 + c
        arrive(qlbuf.at[slot], ql_recv.at[slot])
        push(qlbuf.at[slot], ql_send.at[0], ql_recv.at[slot], sibling)

    loads[6].wait()
    wbuf[mine, :, :] = jnp.concatenate([outp_in[...], jnp.zeros((2, OUT_K), BF16)], axis=0)

    from_left, from_right, from_far = xl * 2 + c, xr * 2 + c, xo * 2 + c
    arrive(pair(from_left, 0), kv_recv.at[4 + xl * 2])
    push(pair(from_left, 0), kvp_send.at[0], kv_recv.at[4 + xl * 2], right)
    push(pair(from_left, 0), kvp_send.at[0], kv_recv.at[16], index(xr, z, 1 - c))
    arrive(pair(from_right, 1), kv_recv.at[4 + xr * 2 + 1])
    push(pair(from_right, 1), kvp_send.at[0], kv_recv.at[4 + xr * 2 + 1], left)
    push(pair(from_right, 1), kvp_send.at[0], kv_recv.at[17], index(xl, z, 1 - c))
    arrive(pair(from_left, 1), kv_recv.at[4 + xl * 2 + 1])
    push(kvbuf.at[from_left], kvb_send.at[0], kv_recv.at[12 + xl], sibling)
    arrive(pair(from_right, 0), kv_recv.at[4 + xr * 2])
    push(kvbuf.at[from_right], kvb_send.at[0], kv_recv.at[12 + xr], sibling)

    for target in (right, left, sibling):
        push(wbuf.at[mine], w_send.at[0], w_recv.at[mine, 0], target)

    arrive(qbuf.at[xo, :, pl.ds(0, QR // 2)], q_recv.at[xo, 0])
    arrive(qbuf.at[xo, :, pl.ds(QR // 2, QR // 2)], q_recv.at[xo, 1])
    for zz in range(ZS):
        slot = zz * 2 + 1 - c
        arrive(qlbuf.at[slot], ql_recv.at[slot])
    ql_rows = qlbuf[...].reshape(8 * SLOT, QC)
    block_of = (lax.broadcasted_iota(jnp.int32, (8 * SLOT, XS * SLOT), 0) // 4) % 4
    partial = jnp.zeros((8 * SLOT, XS * SLOT), F32)
    for j in range(4):
        columns = qbuf[:, :, j * QC: (j + 1) * QC].reshape(XS * SLOT, QC)
        partial = jnp.where(block_of == j, dot_nt(ql_rows, columns), partial)
    partial = partial.reshape(8, SLOT, XS * SLOT)
    partial = partial[:, 0:8] + partial[:, 8:16]
    partial = jnp.concatenate([partial, partial], axis=2)
    lane_of = lax.broadcasted_iota(jnp.int32, (8, 8, 128), 2)
    qsend[...] = jnp.where(lane_of // 64 == c, partial, 0.0)
    for k in range(1, ZS):
        for cc in (c, 1 - c):
            slot = zk[k] * 2 + cc
            remote(
                qsend.at[slot], qrecv.at[own], qx_send.at[0], qx_recv.at[own],
                {"batch": index(x, zk[k], cc)},
            ).start()
    remote(
        qsend.at[z * 2 + 1 - c], qrecv.at[own], qx_send.at[0], qx_recv.at[own], {"batch": sibling}
    ).start()
    qrecv[own, :, :] = qsend[own]

    row8 = lax.broadcasted_iota(jnp.int32, (8, 1), 0)
    row_of = row8 % 4
    low = row8 < 4
    for load in loads[3:6]:
        load.wait()
    length = jnp.zeros((8, 1), jnp.int32)
    for r in range(4):
        length = jnp.where(row_of == r, len_in[r], length)

    lane64 = lax.broadcasted_iota(jnp.int32, (8, ROPE), 1)
    inverse = jnp.exp((lane64 % (ROPE // 2)).astype(F32) * (-2.0 * math.log(50000.0) / ROPE))
    angles = length.astype(F32) * inverse
    cosine = jnp.cos(angles)
    sine = jnp.sin(angles)
    sine = jnp.where(lane64 < ROPE // 2, -sine, sine)

    def twice(values):
        return jnp.concatenate([values, values], axis=0)

    nr8 = twice(nr_in[...].astype(F32))
    nr_swapped = jnp.concatenate([nr8[:, ROPE // 2:], nr8[:, : ROPE // 2]], axis=1)
    key_new = (nr8 * cosine + nr_swapped * sine).astype(BF16).astype(F32)
    nl8 = twice(nl_in[...].astype(F32))

    for k in range(1, ZS):
        for cc in (c, 1 - c):
            slot = zk[k] * 2 + cc
            arrive(qrecv.at[slot], qx_recv.at[slot])
    arrive(qrecv.at[z * 2 + 1 - c], qx_recv.at[z * 2 + 1 - c])
    pieces = []
    for zz in range(ZS):
        piece = qrecv[2 * zz] + qrecv[2 * zz + 1]
        pieces.append(piece + pltpu.roll(piece, 4, 0))
    q_all = jnp.concatenate(pieces, axis=1)
    lane_q = lax.broadcasted_iota(jnp.int32, (8, 512), 1)
    q_all = jnp.where((lane_q % 64 < 32) == low, q_all, 0.0)
    q_hi = q_all.astype(BF16)
    q_lo = (q_all - q_hi.astype(F32)).astype(BF16)
    selection = sel[...]
    q_sel = dot_nn(q_hi, selection) + dot_nn(q_lo, selection)
    q_nope = q_sel[:, 0: 2 * NOPE].astype(BF16)
    query_rope = (
        q_sel[:, 2 * NOPE: 2 * NOPE + ROPE] * cosine + q_sel[:, 2 * NOPE + ROPE:] * sine
    ).astype(BF16)

    loads[8].wait()
    rope_scores = jnp.zeros((8, CACHE), F32)
    for r in range(4):
        rope_scores = jnp.where(row_of == r, dot_nn(query_rope, rope[r]), rope_scores)

    for xx in (x, xl, xr):
        block = xx * 2 + 1 - c
        arrive(kvbuf.at[block], kv_recv.at[12 + xx])
    for half in range(2):
        arrive(pair(from_far, half), kv_recv.at[4 + xo * 2 + half])
        arrive(pair(xo * 2 + 1 - c, half), kv_recv.at[16 + half])

    def kv_rows(xx):
        return jnp.concatenate(
            [kvbuf[xx * 2 + cc, zz] for zz in range(ZS) for cc in range(2)], axis=0
        )

    query_abs = (
        dot_nn(q_nope[:, :NOPE], kv_rows(0)) + dot_nn(q_nope[:, NOPE:], kv_rows(2))
    ).astype(BF16)

    loads[7].wait()
    scale = (NOPE + ROPE) ** (-0.5)
    scores = jnp.zeros((8, CACHE), F32)
    for r in range(4):
        scores = jnp.where(row_of == r, dot_nt(query_abs, lat[r]), scores)
    scores = scores + rope_scores
    score_new = scale * (
        jnp.sum(query_abs.astype(F32) * nl8, axis=1, keepdims=True)
        + jnp.sum(query_rope.astype(F32) * key_new, axis=1, keepdims=True)
    )
    position = lax.broadcasted_iota(jnp.int32, (8, CACHE), 1)
    scores = jnp.where(position < length, scores * scale, -1e30)
    top = jnp.maximum(jnp.max(scores, axis=1, keepdims=True), score_new)
    old = jnp.exp(scores - top)
    new = jnp.exp(score_new - top)
    denom = jnp.sum(old, axis=1, keepdims=True) + new
    probs = (old / denom).astype(BF16)
    prob_new = (new / denom).astype(BF16).astype(F32)
    context = jnp.zeros((8, KVR), F32)
    for r in range(4):
        context = jnp.where(row_of == r, dot_nn(probs, lat[r]), context)
    context = (context + prob_new * nl8).astype(BF16)
    value = jnp.where(low, dot_nt(context, kv_rows(1)), dot_nt(context, kv_rows(3)))
    z_of_8 = up * ZS + z
    vx[z_of_8, :, :] = value.astype(BF16).astype(F32)

    def vx_push(heads, k):
        remote(
            vx.at[z_of_8], vx.at[z_of_8], vx_send.at[0], vx_recv.at[z_of_8],
            {"heads": heads, "batch": index(x, zk[k], c)},
        ).start()

    for k in range(ZS):
        vx_push(across, k)
    for k in range(1, ZS):
        vx_push(h, k)

    arrive(wbuf.at[from_left], w_recv.at[from_left, 0])
    push(
        wbuf.at[from_left, :, pl.ds(0, OUT_K // 2)], w_send.at[0], w_recv.at[from_left, 0], right
    )
    push(wbuf.at[from_left], w_send.at[0], w_recv.at[from_left, 0], sibling)
    arrive(wbuf.at[from_right], w_recv.at[from_right, 0])
    push(
        wbuf.at[from_right, :, pl.ds(OUT_K // 2, OUT_K // 2)], w_send.at[0],
        w_recv.at[from_right, 1], left,
    )
    push(wbuf.at[from_right], w_send.at[0], w_recv.at[from_right, 0], sibling)

    for k in range(1, ZS):
        arrive(vx.at[up * ZS + zk[k]], vx_recv.at[up * ZS + zk[k]])
    for k in range(ZS):
        slot = (1 - up) * ZS + zk[k]
        arrive(vx.at[slot], vx_recv.at[slot])
    vh[y, :, :] = vx[...].reshape(64, 128).astype(BF16)

    for i in (4, 3, 5, 2, 6, 1, 7):
        remote(
            vh.at[y], vh.at[y], vh_send.at[0], vh_recv.at[y],
            {"heads": up * YS + (y + i) % YS},
        ).start()

    arrive(wbuf.at[from_far, :, pl.ds(0, OUT_K // 2)], w_recv.at[from_far, 0])
    arrive(wbuf.at[from_far, :, pl.ds(OUT_K // 2, OUT_K // 2)], w_recv.at[from_far, 1])
    push(wbuf.at[from_far], w_send.at[0], w_recv.at[from_far, 0], sibling)

    @pl.loop(0, 32)
    def _(t):
        start = (((t // 2) % 4) * 8 + (t // 8) * 2 + t % 2) * 14
        col = lax.broadcasted_iota(jnp.int32, (SLOT, 448), 1) - start
        row = lax.broadcasted_iota(jnp.int32, (SLOT, 448), 0)
        block = jnp.where((col == row) & (row < 14), 1.0, 0.0).astype(BF16)
        sel_out[pl.ds(pl.multiple_of(t * SLOT, SLOT), SLOT), :] = block

    for xx in (x, xl, xr, xo):
        block = xx * 2 + 1 - c
        arrive(wbuf.at[block], w_recv.at[block, 0])

    for i in (1, 7, 2, 6, 3, 5, 4):
        other = (y + i) % YS
        arrive(vh.at[other], vh_recv.at[other])

    row32 = lax.broadcasted_iota(jnp.int32, (32, 128), 0)
    is_low = (row32 % 8) < 4
    zero = jnp.zeros((32, 128), BF16)
    chunks = []
    for hh in range(2 * YS):
        block = vh[hh % YS, hh // YS * 32: hh // YS * 32 + 32]
        chunks.append(jnp.where(is_low, block, zero))
        chunks.append(jnp.where(is_low, zero, block))
    y_all = dot_nt(jnp.concatenate(chunks, axis=1), wbuf[...].reshape(8 * SLOT, OUT_K))
    ysend[...] = y_all.reshape(ZS, 8, 128)

    for k in range(1, ZS):
        remote(
            ysend.at[zk[k]], yrecv.at[z], y_send.at[0], y_recv.at[z],
            {"batch": index(x, zk[k], c)},
        ).start()
    yrecv[z, :, :] = ysend[z]
    for k in range(1, ZS):
        arrive(yrecv.at[zk[k]], y_recv.at[zk[k]])
    pieces = []
    for zz in range(ZS):
        piece = yrecv[zz]
        pieces.append(piece + pltpu.roll(piece, 4, 0))
    summed = jnp.concatenate(pieces, axis=1).astype(BF16)
    y_ref[...] = dot_nn(summed, sel_out[...])[0:4]

    for ref, sem in (
        (qbuf.at[0:3], q_send), (kvbuf.at[0, 0:3], kvz_send), (kvbuf.at[0:4], kvp_send),
        (kvbuf.at[0:3], kvb_send),
        (qlbuf.at[0:7], ql_send), (qsend.at[0:7], qx_send), (wbuf.at[0:7], w_send),
        (vx.at[0:7], vx_send), (vh.at[0:7], vh_send), (ysend.at[0:3], y_send),
    ):
        arrive(ref, sem.at[0])


def shards(
    q_latent, new_latent, new_rope, latent_cache, rope_cache, lengths, q_up, kv_up, out_proj
):
    hbm = pl.BlockSpec(memory_space=pltpu.HBM)
    dma = pltpu.SemaphoreType.DMA
    return pl.pallas_call(
        kernel,
        out_shape=jax.ShapeDtypeStruct((4, 448), F32),
        in_specs=[hbm] * 9,
        out_specs=pl.BlockSpec(memory_space=pltpu.VMEM),
        scratch_shapes=[
            pltpu.VMEM((4, QR), BF16),
            pltpu.VMEM((4, KVR), BF16),
            pltpu.VMEM((4, ROPE), BF16),
            pltpu.SMEM((4,), jnp.int32),
            pltpu.VMEM((QROWS, QR), BF16),
            pltpu.VMEM((14, OUT_K), BF16),
            pltpu.VMEM((4, CACHE, KVR), BF16),
            pltpu.VMEM((4, ROPE, CACHE), BF16),
            pltpu.VMEM((XS, SLOT, QR), BF16),
            pltpu.VMEM((8, SLOT, QC), BF16),
            pltpu.VMEM((8, 8, 128), F32),
            pltpu.VMEM((8, 8, 128), F32),
            pltpu.VMEM((8, ZS, SLOT, KVR), BF16),
            pltpu.VMEM((8, SLOT, OUT_K), BF16),
            pltpu.VMEM((512, 2 * NOPE + 2 * ROPE), BF16),
            pltpu.VMEM((512, 448), BF16),
            pltpu.VMEM((2 * ZS, 8, 128), F32),
            pltpu.VMEM((YS, 64, 128), BF16),
            pltpu.VMEM((ZS, 8, 128), F32),
            pltpu.VMEM((ZS, 8, 128), F32),
            dma((9,)),
            dma((1,)), dma((XS, 2)),
            dma((1,)), dma((8,)),
            dma((1,)), dma((8,)),
            dma((1,)), dma((1,)), dma((1,)), dma((18,)),
            dma((1,)), dma((8, 2)),
            dma((1,)), dma((2 * ZS,)),
            dma((1,)), dma((YS,)),
            dma((1,)), dma((ZS,)),
        ],
        compiler_params=pltpu.CompilerParams(
            collective_id=0, has_side_effects=True, vmem_limit_bytes=60 * 2**20
        ),
        cost_estimate=pl.CostEstimate(
            flops=4 * 10**8, bytes_accessed=5 * 10**6, transcendentals=10**4
        ),
    )(
        q_latent, new_latent, new_rope, latent_cache, jnp.swapaxes(rope_cache, 1, 2), lengths,
        q_up, kv_up, out_proj,
    ).astype(BF16)


def solution(mesh):
    placed = (
        P("batch", None),
        P("batch", None),
        P("batch", None),
        P("batch", None, None),
        P("batch", None, None),
        P("batch"),
        P(("heads", "batch"), None),
        P(("heads", "batch"), None),
        P(("heads", "batch"), None),
    )
    return jax.shard_map(
        shards, mesh=mesh, in_specs=placed, out_specs=P("batch", "heads"), check_vma=False
    )
```

```python
import functools
import math

import jax
import jax.numpy as jnp
from jax import lax
from jax.experimental import pallas as pl
from jax.experimental.pallas import tpu as pltpu
from jax.sharding import PartitionSpec as P

QR = 1536
KVR = 512
NOPE = 128
ROPE = 64
CACHE = 1024
QROWS = 12
SLOT = 16
XS, ZS = 4, 4
YS = 8
QC = QR // 4
OUT_K = 4096
F32 = jnp.float32
BF16 = jnp.bfloat16
NT = (((1,), (1,)), ((), ()))


def dot_nt(a, b):
    return lax.dot_general(a, b, NT, preferred_element_type=F32)


def dot_nn(a, b):
    return jnp.dot(a, b, preferred_element_type=F32)


def kernel(
    ql_hbm, nl_hbm, nr_hbm, lat_hbm, rope_hbm, len_hbm, qup_hbm, kvup_hbm, outp_hbm, y_ref,
    ql_in, nl_in, nr_in, len_in, qup_in, outp_in, lat, rope,
    qbuf, qlbuf, qsend, qrecv, kvbuf, wbuf, sel, sel_out, vx, vh, ysend, yrecv,
    in_sem, q_send, q_recv, ql_send, ql_recv, qx_send, qx_recv, kvz_send, kvp_send, kvb_send, kv_recv,
    w_send, w_recv, vx_send, vx_recv, vh_send, vh_recv, y_send, y_recv,
):
    h = lax.axis_index("heads")
    b = lax.axis_index("batch")
    x, z, c = b // 8, (b // 2) % 4, b % 2
    y, up = h % YS, h // YS

    def index(xx, zz, cc):
        return xx * 8 + zz * 2 + cc

    zk = [z, z + 1 - 2 * (z % 2), (z + 2) % 4, 3 - z]
    xr, xl, xo = (x + 1) % 4, (x + 3) % 4, (x + 2) % 4
    right, left, sibling = index(xr, z, c), index(xl, z, c), index(x, z, 1 - c)
    mine, theirs = x * 2 + c, x * 2 + 1 - c
    own = z * 2 + c

    loads = [
        pltpu.make_async_copy(source, target, in_sem.at[i])
        for i, (source, target) in enumerate(
            [
                (qup_hbm, qup_in), (ql_hbm, ql_in), (kvup_hbm, kvbuf.at[mine, z]),
                (nl_hbm, nl_in), (nr_hbm, nr_in), (len_hbm, len_in), (outp_hbm, outp_in),
                (lat_hbm, lat), (rope_hbm, rope),
            ]
        )
    ]
    barrier = pltpu.get_barrier_semaphore()

    def greet(target):
        pl.semaphore_signal(barrier, inc=1, device_id={"batch": target})

    across = (1 - up) * YS + y
    for k in range(ZS):
        pl.semaphore_signal(
            barrier, inc=1, device_id={"heads": across, "batch": index(x, zk[k], c)}
        )

    @pl.loop(1, YS)
    def _(i):
        pl.semaphore_signal(barrier, inc=1, device_id={"heads": up * YS + (y + i) % YS})

    for k in range(1, ZS):
        greet(index(x, zk[k], c))
        greet(index(x, zk[k], 1 - c))
    for cc in (c, 1 - c):
        greet(index(xr, z, cc))
        greet(index(xl, z, cc))
    greet(sibling)

    for i in (2, 0, 1, 3, 4, 5, 6, 7, 8):
        loads[i].start()
    loads[2].wait()
    pl.semaphore_wait(barrier, ZS + YS - 1 + 6 + 4 + 1)

    def remote(source, target, send_sem, recv_sem, device):
        return pltpu.make_async_remote_copy(
            src_ref=source, dst_ref=target, send_sem=send_sem, recv_sem=recv_sem,
            device_id=device,
        )

    def push(ref, send_sem, recv_sem, target):
        remote(ref, ref, send_sem, recv_sem, {"batch": target}).start()

    def arrive(ref, recv_sem):
        pltpu.make_async_copy(ref, ref, recv_sem).wait()

    for k in (3, 2, 1):
        push(kvbuf.at[mine, z], kvz_send.at[0], kv_recv.at[z], index(x, zk[k], c))

    loads[0].wait()
    qbuf[x, :, :] = jnp.concatenate([qup_in[...], jnp.zeros((SLOT - QROWS, QR), BF16)], axis=0)
    for target in (right, left):
        push(qbuf.at[x], q_send.at[0], q_recv.at[x, 0], target)
    loads[1].wait()
    ql_own = ql_in[...].astype(F32)
    qlbuf[own, :, :] = jnp.concatenate(
        [ql_own[:, j * QC: (j + 1) * QC] for j in range(4)], axis=0
    ).astype(BF16)
    for k in range(1, ZS):
        push(qlbuf.at[own], ql_send.at[0], ql_recv.at[own], index(x, zk[k], c))
    push(qlbuf.at[own], ql_send.at[0], ql_recv.at[own], sibling)

    @pl.loop(0, 32)
    def _(t):
        x_t = (x + t % 4 + (t % 4) // 2 - 2 * ((t % 4) // 3)) % 4
        first_row = QROWS * ((x_t % 2) * 8 + (t // 8) * 2 + (t // 4) % 2)
        shape = (SLOT, 2 * NOPE + 2 * ROPE)
        within = lax.broadcasted_iota(jnp.int32, shape, 0)
        col = lax.broadcasted_iota(jnp.int32, shape, 1)
        row = within + first_row
        nope = (row < NOPE) & (col == row + (x_t // 2) * NOPE)
        rotary = row - NOPE
        swapped = (rotary + ROPE // 2) % ROPE
        rope_at = (row >= NOPE) & (
            (col == 2 * NOPE + rotary) | (col == 2 * NOPE + ROPE + swapped)
        )
        block = jnp.where((within < QROWS) & (nope | rope_at), 1.0, 0.0).astype(BF16)
        sel[pl.ds(pl.multiple_of(t * SLOT, SLOT), SLOT), :] = block

    arrive(qbuf.at[xl], q_recv.at[xl, 0])
    push(qbuf.at[xl, :, pl.ds(0, QR // 2)], q_send.at[0], q_recv.at[xl, 0], right)
    arrive(qbuf.at[xr], q_recv.at[xr, 0])
    push(qbuf.at[xr, :, pl.ds(QR // 2, QR // 2)], q_send.at[0], q_recv.at[xr, 1], left)

    def pair(block, half):
        return kvbuf.at[block, pl.ds(2 * half, 2)]

    def kv_pair_out(half):
        for target in (right, left):
            push(pair(mine, half), kvp_send.at[0], kv_recv.at[4 + x * 2 + half], target)

    arrive(kvbuf.at[mine, zk[1]], kv_recv.at[zk[1]])
    kv_pair_out(z // 2)
    for k in range(2, ZS):
        arrive(kvbuf.at[mine, zk[k]], kv_recv.at[zk[k]])
    kv_pair_out(1 - z // 2)
    push(kvbuf.at[mine], kvb_send.at[0], kv_recv.at[12 + x], sibling)
    for k in range(1, ZS):
        slot = zk[k] * 2 + c
        arrive(qlbuf.at[slot], ql_recv.at[slot])
        push(qlbuf.at[slot], ql_send.at[0], ql_recv.at[slot], sibling)

    loads[6].wait()
    wbuf[mine, :, :] = jnp.concatenate([outp_in[...], jnp.zeros((2, OUT_K), BF16)], axis=0)

    from_left, from_right, from_far = xl * 2 + c, xr * 2 + c, xo * 2 + c
    arrive(pair(from_left, 0), kv_recv.at[4 + xl * 2])
    push(pair(from_left, 0), kvp_send.at[0], kv_recv.at[4 + xl * 2], right)
    push(pair(from_left, 0), kvp_send.at[0], kv_recv.at[16], index(xr, z, 1 - c))
    arrive(pair(from_right, 1), kv_recv.at[4 + xr * 2 + 1])
    push(pair(from_right, 1), kvp_send.at[0], kv_recv.at[4 + xr * 2 + 1], left)
    push(pair(from_right, 1), kvp_send.at[0], kv_recv.at[17], index(xl, z, 1 - c))
    arrive(pair(from_left, 1), kv_recv.at[4 + xl * 2 + 1])
    push(kvbuf.at[from_left], kvb_send.at[0], kv_recv.at[12 + xl], sibling)
    arrive(pair(from_right, 0), kv_recv.at[4 + xr * 2])
    push(kvbuf.at[from_right], kvb_send.at[0], kv_recv.at[12 + xr], sibling)

    for target in (right, left, sibling):
        push(wbuf.at[mine], w_send.at[0], w_recv.at[mine, 0], target)

    for zz in range(ZS):
        slot = zz * 2 + 1 - c
        arrive(qlbuf.at[slot], ql_recv.at[slot])
    ql_rows = qlbuf[...].reshape(8 * SLOT, QC)

    def partial_q(slots):
        width = len(slots) * SLOT
        block_of = (lax.broadcasted_iota(jnp.int32, (8 * SLOT, width), 0) // 4) % 4
        total = jnp.zeros((8 * SLOT, width), F32)
        for j in range(4):
            columns = jnp.concatenate(
                [qbuf[slot, :, j * QC: (j + 1) * QC] for slot in slots], axis=0
            )
            total = jnp.where(block_of == j, dot_nt(ql_rows, columns), total)
        return total

    near = partial_q([x, xr, xl])
    arrive(qbuf.at[xo, :, pl.ds(0, QR // 2)], q_recv.at[xo, 0])
    arrive(qbuf.at[xo, :, pl.ds(QR // 2, QR // 2)], q_recv.at[xo, 1])
    partial = jnp.concatenate([near, partial_q([xo])], axis=1)
    partial = partial.reshape(8, SLOT, XS * SLOT)
    partial = partial[:, 0:8] + partial[:, 8:16]
    partial = jnp.concatenate([partial, partial], axis=2)
    lane_of = lax.broadcasted_iota(jnp.int32, (8, 8, 128), 2)
    qsend[...] = jnp.where(lane_of // 64 == c, partial, 0.0)
    for k in range(1, ZS):
        for cc in (c, 1 - c):
            slot = zk[k] * 2 + cc
            remote(
                qsend.at[slot], qrecv.at[own], qx_send.at[0], qx_recv.at[own],
                {"batch": index(x, zk[k], cc)},
            ).start()
    remote(
        qsend.at[z * 2 + 1 - c], qrecv.at[own], qx_send.at[0], qx_recv.at[own], {"batch": sibling}
    ).start()
    qrecv[own, :, :] = qsend[own]

    row8 = lax.broadcasted_iota(jnp.int32, (8, 1), 0)
    row_of = row8 % 4
    low = row8 < 4
    for load in loads[3:6]:
        load.wait()
    length = jnp.zeros((8, 1), jnp.int32)
    for r in range(4):
        length = jnp.where(row_of == r, len_in[r], length)

    lane64 = lax.broadcasted_iota(jnp.int32, (8, ROPE), 1)
    inverse = jnp.exp((lane64 % (ROPE // 2)).astype(F32) * (-2.0 * math.log(50000.0) / ROPE))
    angles = length.astype(F32) * inverse
    cosine = jnp.cos(angles)
    sine = jnp.sin(angles)
    sine = jnp.where(lane64 < ROPE // 2, -sine, sine)

    def twice(values):
        return jnp.concatenate([values, values], axis=0)

    nr8 = twice(nr_in[...].astype(F32))
    nr_swapped = jnp.concatenate([nr8[:, ROPE // 2:], nr8[:, : ROPE // 2]], axis=1)
    key_new = (nr8 * cosine + nr_swapped * sine).astype(BF16).astype(F32)
    nl8 = twice(nl_in[...].astype(F32))

    for k in range(1, ZS):
        for cc in (c, 1 - c):
            slot = zk[k] * 2 + cc
            arrive(qrecv.at[slot], qx_recv.at[slot])
    arrive(qrecv.at[z * 2 + 1 - c], qx_recv.at[z * 2 + 1 - c])
    pieces = []
    for zz in range(ZS):
        piece = qrecv[2 * zz] + qrecv[2 * zz + 1]
        pieces.append(piece + pltpu.roll(piece, 4, 0))
    q_all = jnp.concatenate(pieces, axis=1)
    lane_q = lax.broadcasted_iota(jnp.int32, (8, 512), 1)
    turn = lane_q % 64 // 16
    x_of = (x + turn + turn // 2 - 2 * (turn // 3)) % 4
    q_all = jnp.where((x_of < 2) == low, q_all, 0.0)
    q_hi = q_all.astype(BF16)
    q_lo = (q_all - q_hi.astype(F32)).astype(BF16)
    selection = sel[...]
    q_sel = dot_nn(q_hi, selection) + dot_nn(q_lo, selection)
    q_nope = q_sel[:, 0: 2 * NOPE].astype(BF16)
    query_rope = (
        q_sel[:, 2 * NOPE: 2 * NOPE + ROPE] * cosine + q_sel[:, 2 * NOPE + ROPE:] * sine
    ).astype(BF16)

    loads[8].wait()
    rope_scores = jnp.zeros((8, CACHE), F32)
    for r in range(4):
        rope_scores = jnp.where(row_of == r, dot_nn(query_rope, rope[r]), rope_scores)

    for xx in (x, xl, xr):
        block = xx * 2 + 1 - c
        arrive(kvbuf.at[block], kv_recv.at[12 + xx])
    for half in range(2):
        arrive(pair(from_far, half), kv_recv.at[4 + xo * 2 + half])
        arrive(pair(xo * 2 + 1 - c, half), kv_recv.at[16 + half])

    def kv_rows(xx):
        return jnp.concatenate(
            [kvbuf[xx * 2 + cc, zz] for zz in range(ZS) for cc in range(2)], axis=0
        )

    query_abs = (
        dot_nn(q_nope[:, :NOPE], kv_rows(0)) + dot_nn(q_nope[:, NOPE:], kv_rows(2))
    ).astype(BF16)

    loads[7].wait()
    scale = (NOPE + ROPE) ** (-0.5)
    scores = jnp.zeros((8, CACHE), F32)
    for r in range(4):
        scores = jnp.where(row_of == r, dot_nt(query_abs, lat[r]), scores)
    scores = scores + rope_scores
    score_new = scale * (
        jnp.sum(query_abs.astype(F32) * nl8, axis=1, keepdims=True)
        + jnp.sum(query_rope.astype(F32) * key_new, axis=1, keepdims=True)
    )
    position = lax.broadcasted_iota(jnp.int32, (8, CACHE), 1)
    scores = jnp.where(position < length, scores * scale, -1e30)
    top = jnp.maximum(jnp.max(scores, axis=1, keepdims=True), score_new)
    old = jnp.exp(scores - top)
    new = jnp.exp(score_new - top)
    denom = jnp.sum(old, axis=1, keepdims=True) + new
    probs = (old / denom).astype(BF16)
    prob_new = (new / denom).astype(BF16).astype(F32)
    context = jnp.zeros((8, KVR), F32)
    for r in range(4):
        context = jnp.where(row_of == r, dot_nn(probs, lat[r]), context)
    context = (context + prob_new * nl8).astype(BF16)
    value = jnp.where(low, dot_nt(context, kv_rows(1)), dot_nt(context, kv_rows(3)))
    z_of_8 = up * ZS + z
    vx[z_of_8, :, :] = value.astype(BF16).astype(F32)

    def vx_push(heads, k):
        remote(
            vx.at[z_of_8], vx.at[z_of_8], vx_send.at[0], vx_recv.at[z_of_8],
            {"heads": heads, "batch": index(x, zk[k], c)},
        ).start()

    for k in range(ZS):
        vx_push(across, k)
    for k in range(1, ZS):
        vx_push(h, k)

    arrive(wbuf.at[from_left], w_recv.at[from_left, 0])
    push(
        wbuf.at[from_left, :, pl.ds(0, OUT_K // 2)], w_send.at[0], w_recv.at[from_left, 0], right
    )
    push(wbuf.at[from_left], w_send.at[0], w_recv.at[from_left, 0], sibling)
    arrive(wbuf.at[from_right], w_recv.at[from_right, 0])
    push(
        wbuf.at[from_right, :, pl.ds(OUT_K // 2, OUT_K // 2)], w_send.at[0],
        w_recv.at[from_right, 1], left,
    )
    push(wbuf.at[from_right], w_send.at[0], w_recv.at[from_right, 0], sibling)

    for k in range(1, ZS):
        arrive(vx.at[up * ZS + zk[k]], vx_recv.at[up * ZS + zk[k]])
    for k in range(ZS):
        slot = (1 - up) * ZS + zk[k]
        arrive(vx.at[slot], vx_recv.at[slot])
    vh[y, :, :] = vx[...].reshape(64, 128).astype(BF16)

    for i in (4, 3, 5, 2, 6, 1, 7):
        remote(
            vh.at[y], vh.at[y], vh_send.at[0], vh_recv.at[y],
            {"heads": up * YS + (y + i) % YS},
        ).start()

    arrive(wbuf.at[from_far, :, pl.ds(0, OUT_K // 2)], w_recv.at[from_far, 0])
    arrive(wbuf.at[from_far, :, pl.ds(OUT_K // 2, OUT_K // 2)], w_recv.at[from_far, 1])
    push(wbuf.at[from_far], w_send.at[0], w_recv.at[from_far, 0], sibling)

    @pl.loop(0, 32)
    def _(t):
        start = (((t // 2) % 4) * 8 + (t // 8) * 2 + t % 2) * 14
        col = lax.broadcasted_iota(jnp.int32, (SLOT, 448), 1) - start
        row = lax.broadcasted_iota(jnp.int32, (SLOT, 448), 0)
        block = jnp.where((col == row) & (row < 14), 1.0, 0.0).astype(BF16)
        sel_out[pl.ds(pl.multiple_of(t * SLOT, SLOT), SLOT), :] = block

    for xx in (x, xl, xr, xo):
        block = xx * 2 + 1 - c
        arrive(wbuf.at[block], w_recv.at[block, 0])

    row32 = lax.broadcasted_iota(jnp.int32, (32, 128), 0)
    is_low = (row32 % 8) < 4
    zero = jnp.zeros((32, 128), BF16)
    y_all = jnp.zeros((32, 128), F32)
    for i in (0, 1, 7, 2, 6, 3, 5, 4):
        other = (y + i) % YS
        if i:
            arrive(vh.at[other], vh_recv.at[other])
        for half in range(2):
            block = vh[other, half * 32: half * 32 + 32]
            block = jnp.concatenate(
                [jnp.where(is_low, block, zero), jnp.where(is_low, zero, block)], axis=1
            )
            columns = pl.ds(pl.multiple_of((half * YS + other) * 256, 256), 256)
            y_all = y_all + dot_nt(block, wbuf[:, :, columns].reshape(8 * SLOT, 256))
    ysend[...] = y_all.reshape(ZS, 8, 128)

    for k in range(1, ZS):
        remote(
            ysend.at[zk[k]], yrecv.at[z], y_send.at[0], y_recv.at[z],
            {"batch": index(x, zk[k], c)},
        ).start()
    yrecv[z, :, :] = ysend[z]
    for k in range(1, ZS):
        arrive(yrecv.at[zk[k]], y_recv.at[zk[k]])
    pieces = []
    for zz in range(ZS):
        piece = yrecv[zz]
        pieces.append(piece + pltpu.roll(piece, 4, 0))
    summed = jnp.concatenate(pieces, axis=1).astype(BF16)
    y_ref[...] = dot_nn(summed, sel_out[...])[0:4]

    for ref, sem in (
        (qbuf.at[0:3], q_send), (kvbuf.at[0, 0:3], kvz_send), (kvbuf.at[0:4], kvp_send),
        (kvbuf.at[0:3], kvb_send),
        (qlbuf.at[0:7], ql_send), (qsend.at[0:7], qx_send), (wbuf.at[0:7], w_send),
        (vx.at[0:7], vx_send), (vh.at[0:7], vh_send), (ysend.at[0:3], y_send),
    ):
        arrive(ref, sem.at[0])


def shards(
    q_latent, new_latent, new_rope, latent_cache, rope_cache, lengths, q_up, kv_up, out_proj
):
    hbm = pl.BlockSpec(memory_space=pltpu.HBM)
    dma = pltpu.SemaphoreType.DMA
    return pl.pallas_call(
        kernel,
        out_shape=jax.ShapeDtypeStruct((4, 448), F32),
        in_specs=[hbm] * 9,
        out_specs=pl.BlockSpec(memory_space=pltpu.VMEM),
        scratch_shapes=[
            pltpu.VMEM((4, QR), BF16),
            pltpu.VMEM((4, KVR), BF16),
            pltpu.VMEM((4, ROPE), BF16),
            pltpu.SMEM((4,), jnp.int32),
            pltpu.VMEM((QROWS, QR), BF16),
            pltpu.VMEM((14, OUT_K), BF16),
            pltpu.VMEM((4, CACHE, KVR), BF16),
            pltpu.VMEM((4, ROPE, CACHE), BF16),
            pltpu.VMEM((XS, SLOT, QR), BF16),
            pltpu.VMEM((8, SLOT, QC), BF16),
            pltpu.VMEM((8, 8, 128), F32),
            pltpu.VMEM((8, 8, 128), F32),
            pltpu.VMEM((8, ZS, SLOT, KVR), BF16),
            pltpu.VMEM((8, SLOT, OUT_K), BF16),
            pltpu.VMEM((512, 2 * NOPE + 2 * ROPE), BF16),
            pltpu.VMEM((512, 448), BF16),
            pltpu.VMEM((2 * ZS, 8, 128), F32),
            pltpu.VMEM((YS, 64, 128), BF16),
            pltpu.VMEM((ZS, 8, 128), F32),
            pltpu.VMEM((ZS, 8, 128), F32),
            dma((9,)),
            dma((1,)), dma((XS, 2)),
            dma((1,)), dma((8,)),
            dma((1,)), dma((8,)),
            dma((1,)), dma((1,)), dma((1,)), dma((18,)),
            dma((1,)), dma((8, 2)),
            dma((1,)), dma((2 * ZS,)),
            dma((1,)), dma((YS,)),
            dma((1,)), dma((ZS,)),
        ],
        compiler_params=pltpu.CompilerParams(
            collective_id=0, has_side_effects=True, vmem_limit_bytes=60 * 2**20
        ),
        cost_estimate=pl.CostEstimate(
            flops=4 * 10**8, bytes_accessed=5 * 10**6, transcendentals=10**4
        ),
    )(
        q_latent, new_latent, new_rope, latent_cache, jnp.swapaxes(rope_cache, 1, 2), lengths,
        q_up, kv_up, out_proj,
    ).astype(BF16)


def solution(mesh):
    placed = (
        P("batch", None),
        P("batch", None),
        P("batch", None),
        P("batch", None, None),
        P("batch", None, None),
        P("batch"),
        P(("heads", "batch"), None),
        P(("heads", "batch"), None),
        P(("heads", "batch"), None),
    )
    return jax.shard_map(
        shards, mesh=mesh, in_specs=placed, out_specs=P("batch", "heads"), check_vma=False
    )
```

```python
import functools
import math

import jax
import jax.numpy as jnp
from jax import lax
from jax.experimental import pallas as pl
from jax.experimental.pallas import tpu as pltpu
from jax.sharding import PartitionSpec as P

QR = 1536
KVR = 512
NOPE = 128
ROPE = 64
CACHE = 1024
QROWS = 12
SLOT = 16
XS, ZS = 4, 4
YS = 8
QC = QR // 4
OUT_K = 4096
F32 = jnp.float32
BF16 = jnp.bfloat16
NT = (((1,), (1,)), ((), ()))


def dot_nt(a, b):
    return lax.dot_general(a, b, NT, preferred_element_type=F32)


def dot_nn(a, b):
    return jnp.dot(a, b, preferred_element_type=F32)


def kernel(
    ql_hbm, nl_hbm, nr_hbm, lat_hbm, rope_hbm, len_hbm, qup_hbm, kvup_hbm, outp_hbm, y_ref,
    ql_in, nl_in, nr_in, len_in, qup_in, outp_in, lat, rope,
    qbuf, qlbuf, qsend, qrecv, kvbuf, wbuf, sel, sel_out, vx, vh, ysend, yrecv,
    in_sem, q_send, q_recv, ql_send, ql_recv, qx_send, qx_recv, kvz_send, kvp_send, kvb_send, kv_recv,
    w_send, w_recv, vx_send, vx_recv, vh_send, vh_recv, y_send, y_recv,
):
    h = lax.axis_index("heads")
    b = lax.axis_index("batch")
    x, z, c = b // 8, (b // 2) % 4, b % 2
    y, up = h % YS, h // YS

    def index(xx, zz, cc):
        return xx * 8 + zz * 2 + cc

    zk = [z, z + 1 - 2 * (z % 2), (z + 2) % 4, 3 - z]
    xr, xl, xo = (x + 1) % 4, (x + 3) % 4, (x + 2) % 4
    right, left, sibling = index(xr, z, c), index(xl, z, c), index(x, z, 1 - c)
    mine, theirs = x * 2 + c, x * 2 + 1 - c
    own = z * 2 + c

    loads = [
        pltpu.make_async_copy(source, target, in_sem.at[i])
        for i, (source, target) in enumerate(
            [
                (qup_hbm, qup_in), (ql_hbm, ql_in), (kvup_hbm, kvbuf.at[mine, z]),
                (nl_hbm, nl_in), (nr_hbm, nr_in), (len_hbm, len_in), (outp_hbm, outp_in),
                (lat_hbm, lat), (rope_hbm, rope),
            ]
        )
    ]
    barrier = pltpu.get_barrier_semaphore()

    def greet(target):
        pl.semaphore_signal(barrier, inc=1, device_id={"batch": target})

    across = (1 - up) * YS + y
    for k in range(ZS):
        pl.semaphore_signal(
            barrier, inc=1, device_id={"heads": across, "batch": index(x, zk[k], c)}
        )

    @pl.loop(1, YS)
    def _(i):
        pl.semaphore_signal(barrier, inc=1, device_id={"heads": up * YS + (y + i) % YS})

    for k in range(1, ZS):
        greet(index(x, zk[k], c))
        greet(index(x, zk[k], 1 - c))
    for cc in (c, 1 - c):
        greet(index(xr, z, cc))
        greet(index(xl, z, cc))
    greet(sibling)

    for i in (2, 0, 1, 3, 4, 5, 6, 7, 8):
        loads[i].start()
    loads[2].wait()
    pl.semaphore_wait(barrier, ZS + YS - 1 + 6 + 4 + 1)

    def remote(source, target, send_sem, recv_sem, device):
        return pltpu.make_async_remote_copy(
            src_ref=source, dst_ref=target, send_sem=send_sem, recv_sem=recv_sem,
            device_id=device,
        )

    def push(ref, send_sem, recv_sem, target):
        remote(ref, ref, send_sem, recv_sem, {"batch": target}).start()

    def arrive(ref, recv_sem):
        pltpu.make_async_copy(ref, ref, recv_sem).wait()

    for k in (3, 2, 1):
        push(kvbuf.at[mine, z], kvz_send.at[0], kv_recv.at[z], index(x, zk[k], c))

    loads[0].wait()
    qbuf[x, :, :] = jnp.concatenate([qup_in[...], jnp.zeros((SLOT - QROWS, QR), BF16)], axis=0)
    for target in (right, left):
        push(qbuf.at[x], q_send.at[0], q_recv.at[x, 0], target)
    loads[1].wait()
    ql_own = ql_in[...].astype(F32)
    qlbuf[own, :, :] = jnp.concatenate(
        [ql_own[:, j * QC: (j + 1) * QC] for j in range(4)], axis=0
    ).astype(BF16)
    for k in range(1, ZS):
        push(qlbuf.at[own], ql_send.at[0], ql_recv.at[own], index(x, zk[k], c))
    push(qlbuf.at[own], ql_send.at[0], ql_recv.at[own], sibling)

    @pl.loop(0, 32)
    def _(t):
        x_t = (x + t % 4 + (t % 4) // 2 - 2 * ((t % 4) // 3)) % 4
        first_row = QROWS * ((x_t % 2) * 8 + (t // 8) * 2 + (t // 4) % 2)
        shape = (SLOT, 2 * NOPE + 2 * ROPE)
        within = lax.broadcasted_iota(jnp.int32, shape, 0)
        col = lax.broadcasted_iota(jnp.int32, shape, 1)
        row = within + first_row
        nope = (row < NOPE) & (col == row + (x_t // 2) * NOPE)
        rotary = row - NOPE
        swapped = (rotary + ROPE // 2) % ROPE
        rope_at = (row >= NOPE) & (
            (col == 2 * NOPE + rotary) | (col == 2 * NOPE + ROPE + swapped)
        )
        block = jnp.where((within < QROWS) & (nope | rope_at), 1.0, 0.0).astype(BF16)
        sel[pl.ds(pl.multiple_of(t * SLOT, SLOT), SLOT), :] = block

    arrive(qbuf.at[xl], q_recv.at[xl, 0])
    push(qbuf.at[xl, :, pl.ds(0, QR // 2)], q_send.at[0], q_recv.at[xl, 0], right)
    arrive(qbuf.at[xr], q_recv.at[xr, 0])
    push(qbuf.at[xr, :, pl.ds(QR // 2, QR // 2)], q_send.at[0], q_recv.at[xr, 1], left)

    def pair(block, half):
        return kvbuf.at[block, pl.ds(2 * half, 2)]

    def kv_pair_out(half):
        for target in (right, left):
            push(pair(mine, half), kvp_send.at[0], kv_recv.at[4 + x * 2 + half], target)

    arrive(kvbuf.at[mine, zk[1]], kv_recv.at[zk[1]])
    kv_pair_out(z // 2)
    for k in range(2, ZS):
        arrive(kvbuf.at[mine, zk[k]], kv_recv.at[zk[k]])
    kv_pair_out(1 - z // 2)
    push(kvbuf.at[mine], kvb_send.at[0], kv_recv.at[12 + x], sibling)
    for k in range(1, ZS):
        slot = zk[k] * 2 + c
        arrive(qlbuf.at[slot], ql_recv.at[slot])
        push(qlbuf.at[slot], ql_send.at[0], ql_recv.at[slot], sibling)

    loads[6].wait()
    wbuf[mine, :, :] = jnp.concatenate([outp_in[...], jnp.zeros((2, OUT_K), BF16)], axis=0)

    for target in (right, left, sibling):
        push(wbuf.at[mine], w_send.at[0], w_recv.at[mine, 0], target)

    from_left, from_right, from_far = xl * 2 + c, xr * 2 + c, xo * 2 + c
    arrive(pair(from_left, 0), kv_recv.at[4 + xl * 2])
    push(pair(from_left, 0), kvp_send.at[0], kv_recv.at[4 + xl * 2], right)
    push(pair(from_left, 0), kvp_send.at[0], kv_recv.at[16], index(xr, z, 1 - c))
    arrive(pair(from_right, 1), kv_recv.at[4 + xr * 2 + 1])
    push(pair(from_right, 1), kvp_send.at[0], kv_recv.at[4 + xr * 2 + 1], left)
    push(pair(from_right, 1), kvp_send.at[0], kv_recv.at[17], index(xl, z, 1 - c))
    arrive(pair(from_left, 1), kv_recv.at[4 + xl * 2 + 1])
    push(kvbuf.at[from_left], kvb_send.at[0], kv_recv.at[12 + xl], sibling)
    arrive(pair(from_right, 0), kv_recv.at[4 + xr * 2])
    push(kvbuf.at[from_right], kvb_send.at[0], kv_recv.at[12 + xr], sibling)

    for zz in range(ZS):
        slot = zz * 2 + 1 - c
        arrive(qlbuf.at[slot], ql_recv.at[slot])
    ql_rows = qlbuf[...].reshape(8 * SLOT, QC)

    def partial_q(slots):
        width = len(slots) * SLOT
        block_of = (lax.broadcasted_iota(jnp.int32, (8 * SLOT, width), 0) // 4) % 4
        total = jnp.zeros((8 * SLOT, width), F32)
        for j in range(4):
            columns = jnp.concatenate(
                [qbuf[slot, :, j * QC: (j + 1) * QC] for slot in slots], axis=0
            )
            total = jnp.where(block_of == j, dot_nt(ql_rows, columns), total)
        return total

    near = partial_q([x, xr, xl])
    arrive(qbuf.at[xo, :, pl.ds(0, QR // 2)], q_recv.at[xo, 0])
    arrive(qbuf.at[xo, :, pl.ds(QR // 2, QR // 2)], q_recv.at[xo, 1])
    partial = jnp.concatenate([near, partial_q([xo])], axis=1)
    partial = partial.reshape(8, SLOT, XS * SLOT)
    partial = partial[:, 0:8] + partial[:, 8:16]
    partial = jnp.concatenate([partial, partial], axis=2)
    lane_of = lax.broadcasted_iota(jnp.int32, (8, 8, 128), 2)
    qsend[...] = jnp.where(lane_of // 64 == c, partial, 0.0)
    for k in range(1, ZS):
        for cc in (c, 1 - c):
            slot = zk[k] * 2 + cc
            remote(
                qsend.at[slot], qrecv.at[own], qx_send.at[0], qx_recv.at[own],
                {"batch": index(x, zk[k], cc)},
            ).start()
    remote(
        qsend.at[z * 2 + 1 - c], qrecv.at[own], qx_send.at[0], qx_recv.at[own], {"batch": sibling}
    ).start()
    qrecv[own, :, :] = qsend[own]

    arrive(wbuf.at[from_left], w_recv.at[from_left, 0])
    push(
        wbuf.at[from_left, :, pl.ds(0, OUT_K // 2)], w_send.at[0], w_recv.at[from_left, 0], right
    )
    push(wbuf.at[from_left], w_send.at[0], w_recv.at[from_left, 0], sibling)
    arrive(wbuf.at[from_right], w_recv.at[from_right, 0])
    push(
        wbuf.at[from_right, :, pl.ds(OUT_K // 2, OUT_K // 2)], w_send.at[0],
        w_recv.at[from_right, 1], left,
    )
    push(wbuf.at[from_right], w_send.at[0], w_recv.at[from_right, 0], sibling)

    row8 = lax.broadcasted_iota(jnp.int32, (8, 1), 0)
    row_of = row8 % 4
    low = row8 < 4
    for load in loads[3:6]:
        load.wait()
    length = jnp.zeros((8, 1), jnp.int32)
    for r in range(4):
        length = jnp.where(row_of == r, len_in[r], length)

    lane64 = lax.broadcasted_iota(jnp.int32, (8, ROPE), 1)
    inverse = jnp.exp((lane64 % (ROPE // 2)).astype(F32) * (-2.0 * math.log(50000.0) / ROPE))
    angles = length.astype(F32) * inverse
    cosine = jnp.cos(angles)
    sine = jnp.sin(angles)
    sine = jnp.where(lane64 < ROPE // 2, -sine, sine)

    def twice(values):
        return jnp.concatenate([values, values], axis=0)

    nr8 = twice(nr_in[...].astype(F32))
    nr_swapped = jnp.concatenate([nr8[:, ROPE // 2:], nr8[:, : ROPE // 2]], axis=1)
    key_new = (nr8 * cosine + nr_swapped * sine).astype(BF16).astype(F32)
    nl8 = twice(nl_in[...].astype(F32))

    for k in range(1, ZS):
        for cc in (c, 1 - c):
            slot = zk[k] * 2 + cc
            arrive(qrecv.at[slot], qx_recv.at[slot])
    arrive(qrecv.at[z * 2 + 1 - c], qx_recv.at[z * 2 + 1 - c])
    pieces = []
    for zz in range(ZS):
        piece = qrecv[2 * zz] + qrecv[2 * zz + 1]
        pieces.append(piece + pltpu.roll(piece, 4, 0))
    q_all = jnp.concatenate(pieces, axis=1)
    lane_q = lax.broadcasted_iota(jnp.int32, (8, 512), 1)
    turn = lane_q % 64 // 16
    x_of = (x + turn + turn // 2 - 2 * (turn // 3)) % 4
    q_all = jnp.where((x_of < 2) == low, q_all, 0.0)
    q_hi = q_all.astype(BF16)
    q_lo = (q_all - q_hi.astype(F32)).astype(BF16)
    selection = sel[...]
    q_sel = dot_nn(q_hi, selection) + dot_nn(q_lo, selection)
    q_nope = q_sel[:, 0: 2 * NOPE].astype(BF16)
    query_rope = (
        q_sel[:, 2 * NOPE: 2 * NOPE + ROPE] * cosine + q_sel[:, 2 * NOPE + ROPE:] * sine
    ).astype(BF16)

    loads[8].wait()
    rope_scores = jnp.zeros((8, CACHE), F32)
    for r in range(4):
        rope_scores = jnp.where(row_of == r, dot_nn(query_rope, rope[r]), rope_scores)

    for xx in (x, xl, xr):
        block = xx * 2 + 1 - c
        arrive(kvbuf.at[block], kv_recv.at[12 + xx])
    for half in range(2):
        arrive(pair(from_far, half), kv_recv.at[4 + xo * 2 + half])
        arrive(pair(xo * 2 + 1 - c, half), kv_recv.at[16 + half])

    def kv_rows(xx):
        return jnp.concatenate(
            [kvbuf[xx * 2 + cc, zz] for zz in range(ZS) for cc in range(2)], axis=0
        )

    query_abs = (
        dot_nn(q_nope[:, :NOPE], kv_rows(0)) + dot_nn(q_nope[:, NOPE:], kv_rows(2))
    ).astype(BF16)

    loads[7].wait()
    scale = (NOPE + ROPE) ** (-0.5)
    scores = jnp.zeros((8, CACHE), F32)
    for r in range(4):
        scores = jnp.where(row_of == r, dot_nt(query_abs, lat[r]), scores)
    scores = scores + rope_scores
    arrive(wbuf.at[from_far, :, pl.ds(0, OUT_K // 2)], w_recv.at[from_far, 0])
    arrive(wbuf.at[from_far, :, pl.ds(OUT_K // 2, OUT_K // 2)], w_recv.at[from_far, 1])
    push(wbuf.at[from_far], w_send.at[0], w_recv.at[from_far, 0], sibling)

    score_new = scale * (
        jnp.sum(query_abs.astype(F32) * nl8, axis=1, keepdims=True)
        + jnp.sum(query_rope.astype(F32) * key_new, axis=1, keepdims=True)
    )
    position = lax.broadcasted_iota(jnp.int32, (8, CACHE), 1)
    scores = jnp.where(position < length, scores * scale, -1e30)
    top = jnp.maximum(jnp.max(scores, axis=1, keepdims=True), score_new)
    old = jnp.exp(scores - top)
    new = jnp.exp(score_new - top)
    denom = jnp.sum(old, axis=1, keepdims=True) + new
    probs = (old / denom).astype(BF16)
    prob_new = (new / denom).astype(BF16).astype(F32)
    context = jnp.zeros((8, KVR), F32)
    for r in range(4):
        context = jnp.where(row_of == r, dot_nn(probs, lat[r]), context)
    context = (context + prob_new * nl8).astype(BF16)
    value = jnp.where(low, dot_nt(context, kv_rows(1)), dot_nt(context, kv_rows(3)))
    z_of_8 = up * ZS + z
    vx[z_of_8, :, :] = value.astype(BF16).astype(F32)

    def vx_push(heads, k):
        remote(
            vx.at[z_of_8], vx.at[z_of_8], vx_send.at[0], vx_recv.at[z_of_8],
            {"heads": heads, "batch": index(x, zk[k], c)},
        ).start()

    for k in range(ZS):
        vx_push(across, k)
    for k in range(1, ZS):
        vx_push(h, k)

    for k in range(1, ZS):
        arrive(vx.at[up * ZS + zk[k]], vx_recv.at[up * ZS + zk[k]])
    for k in range(ZS):
        slot = (1 - up) * ZS + zk[k]
        arrive(vx.at[slot], vx_recv.at[slot])
    vh[y, :, :] = vx[...].reshape(64, 128).astype(BF16)

    for i in (4, 3, 5, 2, 6, 1, 7):
        remote(
            vh.at[y], vh.at[y], vh_send.at[0], vh_recv.at[y],
            {"heads": up * YS + (y + i) % YS},
        ).start()

    @pl.loop(0, 32)
    def _(t):
        start = (((t // 2) % 4) * 8 + (t // 8) * 2 + t % 2) * 14
        col = lax.broadcasted_iota(jnp.int32, (SLOT, 448), 1) - start
        row = lax.broadcasted_iota(jnp.int32, (SLOT, 448), 0)
        block = jnp.where((col == row) & (row < 14), 1.0, 0.0).astype(BF16)
        sel_out[pl.ds(pl.multiple_of(t * SLOT, SLOT), SLOT), :] = block

    for xx in (x, xl, xr, xo):
        block = xx * 2 + 1 - c
        arrive(wbuf.at[block], w_recv.at[block, 0])

    row32 = lax.broadcasted_iota(jnp.int32, (32, 128), 0)
    is_low = (row32 % 8) < 4
    zero = jnp.zeros((32, 128), BF16)
    y_all = jnp.zeros((32, 128), F32)
    for i in (0, 1, 7, 2, 6, 3, 5, 4):
        other = (y + i) % YS
        if i:
            arrive(vh.at[other], vh_recv.at[other])
        for half in range(2):
            block = vh[other, half * 32: half * 32 + 32]
            block = jnp.concatenate(
                [jnp.where(is_low, block, zero), jnp.where(is_low, zero, block)], axis=1
            )
            columns = pl.ds(pl.multiple_of((half * YS + other) * 256, 256), 256)
            y_all = y_all + dot_nt(block, wbuf[:, :, columns].reshape(8 * SLOT, 256))
    ysend[...] = y_all.reshape(ZS, 8, 128)

    for k in range(1, ZS):
        remote(
            ysend.at[zk[k]], yrecv.at[z], y_send.at[0], y_recv.at[z],
            {"batch": index(x, zk[k], c)},
        ).start()
    yrecv[z, :, :] = ysend[z]
    for k in range(1, ZS):
        arrive(yrecv.at[zk[k]], y_recv.at[zk[k]])
    pieces = []
    for zz in range(ZS):
        piece = yrecv[zz]
        pieces.append(piece + pltpu.roll(piece, 4, 0))
    summed = jnp.concatenate(pieces, axis=1).astype(BF16)
    y_ref[...] = dot_nn(summed, sel_out[...])[0:4]

    for ref, sem in (
        (qbuf.at[0:3], q_send), (kvbuf.at[0, 0:3], kvz_send), (kvbuf.at[0:4], kvp_send),
        (kvbuf.at[0:3], kvb_send),
        (qlbuf.at[0:7], ql_send), (qsend.at[0:7], qx_send), (wbuf.at[0:7], w_send),
        (vx.at[0:7], vx_send), (vh.at[0:7], vh_send), (ysend.at[0:3], y_send),
    ):
        arrive(ref, sem.at[0])


def shards(
    q_latent, new_latent, new_rope, latent_cache, rope_cache, lengths, q_up, kv_up, out_proj
):
    hbm = pl.BlockSpec(memory_space=pltpu.HBM)
    dma = pltpu.SemaphoreType.DMA
    return pl.pallas_call(
        kernel,
        out_shape=jax.ShapeDtypeStruct((4, 448), F32),
        in_specs=[hbm] * 9,
        out_specs=pl.BlockSpec(memory_space=pltpu.VMEM),
        scratch_shapes=[
            pltpu.VMEM((4, QR), BF16),
            pltpu.VMEM((4, KVR), BF16),
            pltpu.VMEM((4, ROPE), BF16),
            pltpu.SMEM((4,), jnp.int32),
            pltpu.VMEM((QROWS, QR), BF16),
            pltpu.VMEM((14, OUT_K), BF16),
            pltpu.VMEM((4, CACHE, KVR), BF16),
            pltpu.VMEM((4, ROPE, CACHE), BF16),
            pltpu.VMEM((XS, SLOT, QR), BF16),
            pltpu.VMEM((8, SLOT, QC), BF16),
            pltpu.VMEM((8, 8, 128), F32),
            pltpu.VMEM((8, 8, 128), F32),
            pltpu.VMEM((8, ZS, SLOT, KVR), BF16),
            pltpu.VMEM((8, SLOT, OUT_K), BF16),
            pltpu.VMEM((512, 2 * NOPE + 2 * ROPE), BF16),
            pltpu.VMEM((512, 448), BF16),
            pltpu.VMEM((2 * ZS, 8, 128), F32),
            pltpu.VMEM((YS, 64, 128), BF16),
            pltpu.VMEM((ZS, 8, 128), F32),
            pltpu.VMEM((ZS, 8, 128), F32),
            dma((9,)),
            dma((1,)), dma((XS, 2)),
            dma((1,)), dma((8,)),
            dma((1,)), dma((8,)),
            dma((1,)), dma((1,)), dma((1,)), dma((18,)),
            dma((1,)), dma((8, 2)),
            dma((1,)), dma((2 * ZS,)),
            dma((1,)), dma((YS,)),
            dma((1,)), dma((ZS,)),
        ],
        compiler_params=pltpu.CompilerParams(
            collective_id=0, has_side_effects=True, vmem_limit_bytes=60 * 2**20
        ),
        cost_estimate=pl.CostEstimate(
            flops=4 * 10**8, bytes_accessed=5 * 10**6, transcendentals=10**4
        ),
    )(
        q_latent, new_latent, new_rope, latent_cache, jnp.swapaxes(rope_cache, 1, 2), lengths,
        q_up, kv_up, out_proj,
    ).astype(BF16)


def solution(mesh):
    placed = (
        P("batch", None),
        P("batch", None),
        P("batch", None),
        P("batch", None, None),
        P("batch", None, None),
        P("batch"),
        P(("heads", "batch"), None),
        P(("heads", "batch"), None),
        P(("heads", "batch"), None),
    )
    return jax.shard_map(
        shards, mesh=mesh, in_specs=placed, out_specs=P("batch", "heads"), check_vma=False
    )
```

```python
import functools
import math

import jax
import jax.numpy as jnp
from jax import lax
from jax.experimental import pallas as pl
from jax.experimental.pallas import tpu as pltpu
from jax.sharding import PartitionSpec as P

QR = 1536
KVR = 512
NOPE = 128
ROPE = 64
CACHE = 1024
QROWS = 12
SLOT = 16
XS, ZS = 4, 4
YS = 8
QC = QR // 4
OUT_K = 4096
F32 = jnp.float32
BF16 = jnp.bfloat16
NT = (((1,), (1,)), ((), ()))


def dot_nt(a, b):
    return lax.dot_general(a, b, NT, preferred_element_type=F32)


def dot_nn(a, b):
    return jnp.dot(a, b, preferred_element_type=F32)


def kernel(
    ql_hbm, nl_hbm, nr_hbm, lat_hbm, rope_hbm, len_hbm, qup_hbm, kvup_hbm, outp_hbm, y_ref,
    ql_in, nl_in, nr_in, len_in, qup_in, outp_in, lat, rope,
    qbuf, qlbuf, qsend, qrecv, kvbuf, wbuf, sel, sel_out, vx, vh, ysend, yrecv,
    in_sem, q_send, q_recv, ql_send, ql_recv, qx_send, qx_recv, kvz_send, kvp_send, kvb_send, kv_recv,
    w_send, w_recv, vx_send, vx_recv, vh_send, vh_recv, y_send, y_recv,
):
    h = lax.axis_index("heads")
    b = lax.axis_index("batch")
    x, z, c = b // 8, (b // 2) % 4, b % 2
    y, up = h % YS, h // YS

    def index(xx, zz, cc):
        return xx * 8 + zz * 2 + cc

    zk = [z, z + 1 - 2 * (z % 2), (z + 2) % 4, 3 - z]
    xr, xl, xo = (x + 1) % 4, (x + 3) % 4, (x + 2) % 4
    right, left, sibling = index(xr, z, c), index(xl, z, c), index(x, z, 1 - c)
    mine, theirs = x * 2 + c, x * 2 + 1 - c
    own = z * 2 + c

    loads = [
        pltpu.make_async_copy(source, target, in_sem.at[i])
        for i, (source, target) in enumerate(
            [
                (qup_hbm, qup_in), (ql_hbm, ql_in), (kvup_hbm, kvbuf.at[mine, z]),
                (nl_hbm, nl_in), (nr_hbm, nr_in), (len_hbm, len_in), (outp_hbm, outp_in),
                (lat_hbm, lat), (rope_hbm, rope),
            ]
        )
    ]
    barrier = pltpu.get_barrier_semaphore()

    def greet(target):
        pl.semaphore_signal(barrier, inc=1, device_id={"batch": target})

    across = (1 - up) * YS + y
    for k in range(ZS):
        pl.semaphore_signal(
            barrier, inc=1, device_id={"heads": across, "batch": index(x, zk[k], c)}
        )

    @pl.loop(1, YS)
    def _(i):
        pl.semaphore_signal(barrier, inc=1, device_id={"heads": up * YS + (y + i) % YS})

    for k in range(1, ZS):
        greet(index(x, zk[k], c))
        greet(index(x, zk[k], 1 - c))
    for cc in (c, 1 - c):
        greet(index(xr, z, cc))
        greet(index(xl, z, cc))
    greet(sibling)

    for i in (2, 0, 1, 3, 4, 5, 6, 7, 8):
        loads[i].start()
    loads[2].wait()
    pl.semaphore_wait(barrier, ZS + YS - 1 + 6 + 4 + 1)

    def remote(source, target, send_sem, recv_sem, device):
        return pltpu.make_async_remote_copy(
            src_ref=source, dst_ref=target, send_sem=send_sem, recv_sem=recv_sem,
            device_id=device,
        )

    def push(ref, send_sem, recv_sem, target):
        remote(ref, ref, send_sem, recv_sem, {"batch": target}).start()

    def arrive(ref, recv_sem):
        pltpu.make_async_copy(ref, ref, recv_sem).wait()

    for k in (3, 2, 1):
        push(kvbuf.at[mine, z], kvz_send.at[0], kv_recv.at[z], index(x, zk[k], c))

    loads[0].wait()
    qbuf[x, :, :] = jnp.concatenate([qup_in[...], jnp.zeros((SLOT - QROWS, QR), BF16)], axis=0)
    for target in (right, left):
        push(qbuf.at[x], q_send.at[0], q_recv.at[x, 0], target)
    loads[1].wait()
    ql_own = ql_in[...].astype(F32)
    qlbuf[own, :, :] = jnp.concatenate(
        [ql_own[:, j * QC: (j + 1) * QC] for j in range(4)], axis=0
    ).astype(BF16)
    for k in range(1, ZS):
        push(qlbuf.at[own], ql_send.at[0], ql_recv.at[own], index(x, zk[k], c))
    push(qlbuf.at[own], ql_send.at[0], ql_recv.at[own], sibling)

    @pl.loop(0, 32)
    def _(t):
        x_t = (x + t % 4 + (t % 4) // 2 - 2 * ((t % 4) // 3)) % 4
        first_row = QROWS * ((x_t % 2) * 8 + (t // 8) * 2 + (t // 4) % 2)
        shape = (SLOT, 2 * NOPE + 2 * ROPE)
        within = lax.broadcasted_iota(jnp.int32, shape, 0)
        col = lax.broadcasted_iota(jnp.int32, shape, 1)
        row = within + first_row
        nope = (row < NOPE) & (col == row + (x_t // 2) * NOPE)
        rotary = row - NOPE
        swapped = (rotary + ROPE // 2) % ROPE
        rope_at = (row >= NOPE) & (
            (col == 2 * NOPE + rotary) | (col == 2 * NOPE + ROPE + swapped)
        )
        block = jnp.where((within < QROWS) & (nope | rope_at), 1.0, 0.0).astype(BF16)
        sel[pl.ds(pl.multiple_of(t * SLOT, SLOT), SLOT), :] = block

    arrive(qbuf.at[xl], q_recv.at[xl, 0])
    push(qbuf.at[xl, :, pl.ds(0, QR // 2)], q_send.at[0], q_recv.at[xl, 0], right)
    arrive(qbuf.at[xr], q_recv.at[xr, 0])
    push(qbuf.at[xr, :, pl.ds(QR // 2, QR // 2)], q_send.at[0], q_recv.at[xr, 1], left)

    def pair(block, half):
        return kvbuf.at[block, pl.ds(2 * half, 2)]

    def kv_pair_out(half):
        for target in (right, left):
            push(pair(mine, half), kvp_send.at[0], kv_recv.at[4 + x * 2 + half], target)

    arrive(kvbuf.at[mine, zk[1]], kv_recv.at[zk[1]])
    kv_pair_out(z // 2)
    for k in range(2, ZS):
        arrive(kvbuf.at[mine, zk[k]], kv_recv.at[zk[k]])
    kv_pair_out(1 - z // 2)
    push(kvbuf.at[mine], kvb_send.at[0], kv_recv.at[12 + x], sibling)
    for k in range(1, ZS):
        slot = zk[k] * 2 + c
        arrive(qlbuf.at[slot], ql_recv.at[slot])
        push(qlbuf.at[slot], ql_send.at[0], ql_recv.at[slot], sibling)

    loads[6].wait()
    wbuf[mine, :, :] = jnp.concatenate([outp_in[...], jnp.zeros((2, OUT_K), BF16)], axis=0)

    from_left, from_right, from_far = xl * 2 + c, xr * 2 + c, xo * 2 + c
    arrive(pair(from_left, 0), kv_recv.at[4 + xl * 2])
    push(pair(from_left, 0), kvp_send.at[0], kv_recv.at[4 + xl * 2], right)
    push(pair(from_left, 0), kvp_send.at[0], kv_recv.at[16], index(xr, z, 1 - c))
    arrive(pair(from_right, 1), kv_recv.at[4 + xr * 2 + 1])
    push(pair(from_right, 1), kvp_send.at[0], kv_recv.at[4 + xr * 2 + 1], left)
    push(pair(from_right, 1), kvp_send.at[0], kv_recv.at[17], index(xl, z, 1 - c))
    arrive(pair(from_left, 1), kv_recv.at[4 + xl * 2 + 1])
    push(kvbuf.at[from_left], kvb_send.at[0], kv_recv.at[12 + xl], sibling)
    arrive(pair(from_right, 0), kv_recv.at[4 + xr * 2])
    push(kvbuf.at[from_right], kvb_send.at[0], kv_recv.at[12 + xr], sibling)

    for target in (right, left, sibling):
        push(wbuf.at[mine], w_send.at[0], w_recv.at[mine, 0], target)

    for zz in range(ZS):
        slot = zz * 2 + 1 - c
        arrive(qlbuf.at[slot], ql_recv.at[slot])
    ql_rows = qlbuf[...].reshape(8 * SLOT, QC)

    def partial_q(slots):
        width = len(slots) * SLOT
        block_of = (lax.broadcasted_iota(jnp.int32, (8 * SLOT, width), 0) // 4) % 4
        total = jnp.zeros((8 * SLOT, width), F32)
        for j in range(4):
            columns = jnp.concatenate(
                [qbuf[slot, :, j * QC: (j + 1) * QC] for slot in slots], axis=0
            )
            total = jnp.where(block_of == j, dot_nt(ql_rows, columns), total)
        return total

    near = partial_q([x, xr, xl])
    arrive(qbuf.at[xo, :, pl.ds(0, QR // 2)], q_recv.at[xo, 0])
    arrive(qbuf.at[xo, :, pl.ds(QR // 2, QR // 2)], q_recv.at[xo, 1])
    partial = jnp.concatenate([near, partial_q([xo])], axis=1)
    partial = partial.reshape(8, SLOT, XS * SLOT)
    partial = partial[:, 0:8] + partial[:, 8:16]
    partial = jnp.concatenate([partial, partial], axis=2)
    lane_of = lax.broadcasted_iota(jnp.int32, (8, 8, 128), 2)
    qsend[...] = jnp.where(lane_of // 64 == c, partial, 0.0)
    for k in range(1, ZS):
        for cc in (c, 1 - c):
            slot = zk[k] * 2 + cc
            remote(
                qsend.at[slot], qrecv.at[own], qx_send.at[0], qx_recv.at[own],
                {"batch": index(x, zk[k], cc)},
            ).start()
    remote(
        qsend.at[z * 2 + 1 - c], qrecv.at[own], qx_send.at[0], qx_recv.at[own], {"batch": sibling}
    ).start()
    qrecv[own, :, :] = qsend[own]

    row8 = lax.broadcasted_iota(jnp.int32, (8, 1), 0)
    row_of = row8 % 4
    low = row8 < 4
    for load in loads[3:6]:
        load.wait()
    length = jnp.zeros((8, 1), jnp.int32)
    for r in range(4):
        length = jnp.where(row_of == r, len_in[r], length)

    lane64 = lax.broadcasted_iota(jnp.int32, (8, ROPE), 1)
    inverse = jnp.exp((lane64 % (ROPE // 2)).astype(F32) * (-2.0 * math.log(50000.0) / ROPE))
    angles = length.astype(F32) * inverse
    cosine = jnp.cos(angles)
    sine = jnp.sin(angles)
    sine = jnp.where(lane64 < ROPE // 2, -sine, sine)

    def twice(values):
        return jnp.concatenate([values, values], axis=0)

    nr8 = twice(nr_in[...].astype(F32))
    nr_swapped = jnp.concatenate([nr8[:, ROPE // 2:], nr8[:, : ROPE // 2]], axis=1)
    key_new = (nr8 * cosine + nr_swapped * sine).astype(BF16).astype(F32)
    nl8 = twice(nl_in[...].astype(F32))

    for k in range(1, ZS):
        for cc in (c, 1 - c):
            slot = zk[k] * 2 + cc
            arrive(qrecv.at[slot], qx_recv.at[slot])
    arrive(qrecv.at[z * 2 + 1 - c], qx_recv.at[z * 2 + 1 - c])
    pieces = []
    for zz in range(ZS):
        piece = qrecv[2 * zz] + qrecv[2 * zz + 1]
        pieces.append(piece + pltpu.roll(piece, 4, 0))
    q_all = jnp.concatenate(pieces, axis=1)
    lane_q = lax.broadcasted_iota(jnp.int32, (8, 512), 1)
    turn = lane_q % 64 // 16
    x_of = (x + turn + turn // 2 - 2 * (turn // 3)) % 4
    q_all = jnp.where((x_of < 2) == low, q_all, 0.0)
    q_hi = q_all.astype(BF16)
    q_lo = (q_all - q_hi.astype(F32)).astype(BF16)
    selection = sel[...]
    q_sel = dot_nn(q_hi, selection) + dot_nn(q_lo, selection)
    q_nope = q_sel[:, 0: 2 * NOPE].astype(BF16)
    query_rope = (
        q_sel[:, 2 * NOPE: 2 * NOPE + ROPE] * cosine + q_sel[:, 2 * NOPE + ROPE:] * sine
    ).astype(BF16)

    loads[8].wait()

    def rope_row(r, scores):
        return jnp.where(row_of == r, dot_nn(query_rope, rope[r]), scores)

    rope_scores = lax.fori_loop(0, 4, rope_row, jnp.zeros((8, CACHE), F32))

    for xx in (x, xl, xr):
        block = xx * 2 + 1 - c
        arrive(kvbuf.at[block], kv_recv.at[12 + xx])
    for half in range(2):
        arrive(pair(from_far, half), kv_recv.at[4 + xo * 2 + half])
        arrive(pair(xo * 2 + 1 - c, half), kv_recv.at[16 + half])

    def kv_rows(xx):
        return jnp.concatenate(
            [kvbuf[xx * 2 + cc, zz] for zz in range(ZS) for cc in range(2)], axis=0
        )

    query_abs = (
        dot_nn(q_nope[:, :NOPE], kv_rows(0)) + dot_nn(q_nope[:, NOPE:], kv_rows(2))
    ).astype(BF16)

    loads[7].wait()
    scale = (NOPE + ROPE) ** (-0.5)
    def score_row(r, scores):
        return jnp.where(row_of == r, scores + dot_nt(query_abs, lat[r]), scores)

    scores = lax.fori_loop(0, 4, score_row, rope_scores)
    score_new = scale * (
        jnp.sum(query_abs.astype(F32) * nl8, axis=1, keepdims=True)
        + jnp.sum(query_rope.astype(F32) * key_new, axis=1, keepdims=True)
    )
    position = lax.broadcasted_iota(jnp.int32, (8, CACHE), 1)
    scores = jnp.where(position < length, scores * scale, -1e30)
    top = jnp.maximum(jnp.max(scores, axis=1, keepdims=True), score_new)
    old = jnp.exp(scores - top)
    new = jnp.exp(score_new - top)
    denom = jnp.sum(old, axis=1, keepdims=True) + new
    probs = (old / denom).astype(BF16)
    prob_new = (new / denom).astype(BF16).astype(F32)
    def context_row(r, context):
        return jnp.where(row_of == r, dot_nn(probs, lat[r]), context)

    context = lax.fori_loop(0, 4, context_row, jnp.zeros((8, KVR), F32))
    context = (context + prob_new * nl8).astype(BF16)
    value = jnp.where(low, dot_nt(context, kv_rows(1)), dot_nt(context, kv_rows(3)))
    z_of_8 = up * ZS + z
    vx[z_of_8, :, :] = value.astype(BF16).astype(F32)

    def vx_push(heads, k):
        remote(
            vx.at[z_of_8], vx.at[z_of_8], vx_send.at[0], vx_recv.at[z_of_8],
            {"heads": heads, "batch": index(x, zk[k], c)},
        ).start()

    for k in range(ZS):
        vx_push(across, k)
    for k in range(1, ZS):
        vx_push(h, k)

    arrive(wbuf.at[from_left], w_recv.at[from_left, 0])
    push(
        wbuf.at[from_left, :, pl.ds(0, OUT_K // 2)], w_send.at[0], w_recv.at[from_left, 0], right
    )
    push(wbuf.at[from_left], w_send.at[0], w_recv.at[from_left, 0], sibling)
    arrive(wbuf.at[from_right], w_recv.at[from_right, 0])
    push(
        wbuf.at[from_right, :, pl.ds(OUT_K // 2, OUT_K // 2)], w_send.at[0],
        w_recv.at[from_right, 1], left,
    )
    push(wbuf.at[from_right], w_send.at[0], w_recv.at[from_right, 0], sibling)

    for k in range(1, ZS):
        arrive(vx.at[up * ZS + zk[k]], vx_recv.at[up * ZS + zk[k]])
    for k in range(ZS):
        slot = (1 - up) * ZS + zk[k]
        arrive(vx.at[slot], vx_recv.at[slot])
    vh[y, :, :] = vx[...].reshape(64, 128).astype(BF16)

    for i in (4, 3, 5, 2, 6, 1, 7):
        remote(
            vh.at[y], vh.at[y], vh_send.at[0], vh_recv.at[y],
            {"heads": up * YS + (y + i) % YS},
        ).start()

    arrive(wbuf.at[from_far, :, pl.ds(0, OUT_K // 2)], w_recv.at[from_far, 0])
    arrive(wbuf.at[from_far, :, pl.ds(OUT_K // 2, OUT_K // 2)], w_recv.at[from_far, 1])
    push(wbuf.at[from_far], w_send.at[0], w_recv.at[from_far, 0], sibling)

    @pl.loop(0, 32)
    def _(t):
        start = (((t // 2) % 4) * 8 + (t // 8) * 2 + t % 2) * 14
        col = lax.broadcasted_iota(jnp.int32, (SLOT, 448), 1) - start
        row = lax.broadcasted_iota(jnp.int32, (SLOT, 448), 0)
        block = jnp.where((col == row) & (row < 14), 1.0, 0.0).astype(BF16)
        sel_out[pl.ds(pl.multiple_of(t * SLOT, SLOT), SLOT), :] = block

    for xx in (x, xl, xr, xo):
        block = xx * 2 + 1 - c
        arrive(wbuf.at[block], w_recv.at[block, 0])

    row32 = lax.broadcasted_iota(jnp.int32, (32, 128), 0)
    is_low = (row32 % 8) < 4
    zero = jnp.zeros((32, 128), BF16)
    y_all = jnp.zeros((32, 128), F32)
    for i in (0, 1, 7, 2, 6, 3, 5, 4):
        other = (y + i) % YS
        if i:
            arrive(vh.at[other], vh_recv.at[other])
        for half in range(2):
            block = vh[other, half * 32: half * 32 + 32]
            block = jnp.concatenate(
                [jnp.where(is_low, block, zero), jnp.where(is_low, zero, block)], axis=1
            )
            columns = pl.ds(pl.multiple_of((half * YS + other) * 256, 256), 256)
            y_all = y_all + dot_nt(block, wbuf[:, :, columns].reshape(8 * SLOT, 256))
    ysend[...] = y_all.reshape(ZS, 8, 128)

    for k in range(1, ZS):
        remote(
            ysend.at[zk[k]], yrecv.at[z], y_send.at[0], y_recv.at[z],
            {"batch": index(x, zk[k], c)},
        ).start()
    yrecv[z, :, :] = ysend[z]
    for k in range(1, ZS):
        arrive(yrecv.at[zk[k]], y_recv.at[zk[k]])
    pieces = []
    for zz in range(ZS):
        piece = yrecv[zz]
        pieces.append(piece + pltpu.roll(piece, 4, 0))
    summed = jnp.concatenate(pieces, axis=1).astype(BF16)
    y_ref[...] = dot_nn(summed, sel_out[...])[0:4]

    for ref, sem in (
        (qbuf.at[0:3], q_send), (kvbuf.at[0, 0:3], kvz_send), (kvbuf.at[0:4], kvp_send),
        (kvbuf.at[0:3], kvb_send),
        (qlbuf.at[0:7], ql_send), (qsend.at[0:7], qx_send), (wbuf.at[0:7], w_send),
        (vx.at[0:7], vx_send), (vh.at[0:7], vh_send), (ysend.at[0:3], y_send),
    ):
        arrive(ref, sem.at[0])


def shards(
    q_latent, new_latent, new_rope, latent_cache, rope_cache, lengths, q_up, kv_up, out_proj
):
    hbm = pl.BlockSpec(memory_space=pltpu.HBM)
    dma = pltpu.SemaphoreType.DMA
    return pl.pallas_call(
        kernel,
        out_shape=jax.ShapeDtypeStruct((4, 448), F32),
        in_specs=[hbm] * 9,
        out_specs=pl.BlockSpec(memory_space=pltpu.VMEM),
        scratch_shapes=[
            pltpu.VMEM((4, QR), BF16),
            pltpu.VMEM((4, KVR), BF16),
            pltpu.VMEM((4, ROPE), BF16),
            pltpu.SMEM((4,), jnp.int32),
            pltpu.VMEM((QROWS, QR), BF16),
            pltpu.VMEM((14, OUT_K), BF16),
            pltpu.VMEM((4, CACHE, KVR), BF16),
            pltpu.VMEM((4, ROPE, CACHE), BF16),
            pltpu.VMEM((XS, SLOT, QR), BF16),
            pltpu.VMEM((8, SLOT, QC), BF16),
            pltpu.VMEM((8, 8, 128), F32),
            pltpu.VMEM((8, 8, 128), F32),
            pltpu.VMEM((8, ZS, SLOT, KVR), BF16),
            pltpu.VMEM((8, SLOT, OUT_K), BF16),
            pltpu.VMEM((512, 2 * NOPE + 2 * ROPE), BF16),
            pltpu.VMEM((512, 448), BF16),
            pltpu.VMEM((2 * ZS, 8, 128), F32),
            pltpu.VMEM((YS, 64, 128), BF16),
            pltpu.VMEM((ZS, 8, 128), F32),
            pltpu.VMEM((ZS, 8, 128), F32),
            dma((9,)),
            dma((1,)), dma((XS, 2)),
            dma((1,)), dma((8,)),
            dma((1,)), dma((8,)),
            dma((1,)), dma((1,)), dma((1,)), dma((18,)),
            dma((1,)), dma((8, 2)),
            dma((1,)), dma((2 * ZS,)),
            dma((1,)), dma((YS,)),
            dma((1,)), dma((ZS,)),
        ],
        compiler_params=pltpu.CompilerParams(
            collective_id=0, has_side_effects=True, vmem_limit_bytes=60 * 2**20
        ),
        cost_estimate=pl.CostEstimate(
            flops=4 * 10**8, bytes_accessed=5 * 10**6, transcendentals=10**4
        ),
    )(
        q_latent, new_latent, new_rope, latent_cache, jnp.swapaxes(rope_cache, 1, 2), lengths,
        q_up, kv_up, out_proj,
    ).astype(BF16)


def solution(mesh):
    placed = (
        P("batch", None),
        P("batch", None),
        P("batch", None),
        P("batch", None, None),
        P("batch", None, None),
        P("batch"),
        P(("heads", "batch"), None),
        P(("heads", "batch"), None),
        P(("heads", "batch"), None),
    )
    return jax.shard_map(
        shards, mesh=mesh, in_specs=placed, out_specs=P("batch", "heads"), check_vma=False
    )
```

```python
import functools
import math

import jax
import jax.numpy as jnp
from jax import lax
from jax.experimental import pallas as pl
from jax.experimental.pallas import tpu as pltpu
from jax.sharding import PartitionSpec as P

QR = 1536
KVR = 512
NOPE = 128
ROPE = 64
CACHE = 1024
QROWS = 12
SLOT = 16
XS, ZS = 4, 4
YS = 8
QC = QR // 4
OUT_K = 4096
F32 = jnp.float32
BF16 = jnp.bfloat16
NT = (((1,), (1,)), ((), ()))


def dot_nt(a, b):
    return lax.dot_general(a, b, NT, preferred_element_type=F32)


def dot_nn(a, b):
    return jnp.dot(a, b, preferred_element_type=F32)


def kernel(
    ql_hbm, nl_hbm, nr_hbm, lat_hbm, rope_hbm, len_hbm, qup_hbm, kvup_hbm, outp_hbm, y_ref,
    ql_in, nl_in, nr_in, len_in, qup_in, outp_in, lat, rope,
    qbuf, qlbuf, qsend, qrecv, kvbuf, wbuf, sel, sel_out, vx, vh, ysend, yrecv,
    in_sem, q_send, q_recv, ql_send, ql_recv, qx_send, qx_recv, kvz_send, kvp_send, kvb_send, kv_recv,
    w_send, w_recv, vx_send, vx_recv, vh_send, vh_recv, y_send, y_recv,
):
    h = lax.axis_index("heads")
    b = lax.axis_index("batch")
    x, z, c = b // 8, (b // 2) % 4, b % 2
    y, up = h % YS, h // YS

    def index(xx, zz, cc):
        return xx * 8 + zz * 2 + cc

    zk = [z, z + 1 - 2 * (z % 2), (z + 2) % 4, 3 - z]
    xr, xl, xo = (x + 1) % 4, (x + 3) % 4, (x + 2) % 4
    right, left, sibling = index(xr, z, c), index(xl, z, c), index(x, z, 1 - c)
    mine, theirs = x * 2 + c, x * 2 + 1 - c
    own = z * 2 + c

    loads = [
        pltpu.make_async_copy(source, target, in_sem.at[i])
        for i, (source, target) in enumerate(
            [
                (qup_hbm, qup_in), (ql_hbm, ql_in), (kvup_hbm, kvbuf.at[mine, z]),
                (nl_hbm, nl_in), (nr_hbm, nr_in), (len_hbm, len_in), (outp_hbm, outp_in),
                (lat_hbm, lat), (rope_hbm, rope),
            ]
        )
    ]
    barrier = pltpu.get_barrier_semaphore()

    def greet(target):
        pl.semaphore_signal(barrier, inc=1, device_id={"batch": target})

    across = (1 - up) * YS + y
    for k in range(ZS):
        pl.semaphore_signal(
            barrier, inc=1, device_id={"heads": across, "batch": index(x, zk[k], c)}
        )

    @pl.loop(1, YS)
    def _(i):
        pl.semaphore_signal(barrier, inc=1, device_id={"heads": up * YS + (y + i) % YS})

    for k in range(1, ZS):
        greet(index(x, zk[k], c))
        greet(index(x, zk[k], 1 - c))
    for cc in (c, 1 - c):
        greet(index(xr, z, cc))
        greet(index(xl, z, cc))
    greet(sibling)

    for i in (2, 0, 1, 3, 4, 5, 6, 7, 8):
        loads[i].start()
    loads[2].wait()
    pl.semaphore_wait(barrier, ZS + YS - 1 + 6 + 4 + 1)

    def remote(source, target, send_sem, recv_sem, device):
        return pltpu.make_async_remote_copy(
            src_ref=source, dst_ref=target, send_sem=send_sem, recv_sem=recv_sem,
            device_id=device,
        )

    def push(ref, send_sem, recv_sem, target):
        remote(ref, ref, send_sem, recv_sem, {"batch": target}).start()

    def arrive(ref, recv_sem):
        pltpu.make_async_copy(ref, ref, recv_sem).wait()

    for k in (3, 2, 1):
        push(kvbuf.at[mine, z], kvz_send.at[0], kv_recv.at[z], index(x, zk[k], c))

    loads[0].wait()
    qbuf[x, :, :] = jnp.concatenate([qup_in[...], jnp.zeros((SLOT - QROWS, QR), BF16)], axis=0)
    for target in (right, left):
        push(qbuf.at[x], q_send.at[0], q_recv.at[x, 0], target)
    loads[1].wait()
    ql_own = ql_in[...].astype(F32)
    qlbuf[own, :, :] = jnp.concatenate(
        [ql_own[:, j * QC: (j + 1) * QC] for j in range(4)], axis=0
    ).astype(BF16)
    for k in range(1, ZS):
        push(qlbuf.at[own], ql_send.at[0], ql_recv.at[own], index(x, zk[k], c))
    push(qlbuf.at[own], ql_send.at[0], ql_recv.at[own], sibling)

    @pl.loop(0, 32)
    def _(t):
        x_t = (x + t % 4 + (t % 4) // 2 - 2 * ((t % 4) // 3)) % 4
        first_row = QROWS * ((x_t % 2) * 8 + (t // 8) * 2 + (t // 4) % 2)
        shape = (SLOT, 2 * NOPE + 2 * ROPE)
        within = lax.broadcasted_iota(jnp.int32, shape, 0)
        col = lax.broadcasted_iota(jnp.int32, shape, 1)
        row = within + first_row
        nope = (row < NOPE) & (col == row + (x_t // 2) * NOPE)
        rotary = row - NOPE
        swapped = (rotary + ROPE // 2) % ROPE
        rope_at = (row >= NOPE) & (
            (col == 2 * NOPE + rotary) | (col == 2 * NOPE + ROPE + swapped)
        )
        block = jnp.where((within < QROWS) & (nope | rope_at), 1.0, 0.0).astype(BF16)
        sel[pl.ds(pl.multiple_of(t * SLOT, SLOT), SLOT), :] = block

    arrive(qbuf.at[xl], q_recv.at[xl, 0])
    push(qbuf.at[xl, :, pl.ds(0, QR // 2)], q_send.at[0], q_recv.at[xl, 0], right)
    arrive(qbuf.at[xr], q_recv.at[xr, 0])
    push(qbuf.at[xr, :, pl.ds(QR // 2, QR // 2)], q_send.at[0], q_recv.at[xr, 1], left)

    def pair(block, half):
        return kvbuf.at[block, pl.ds(2 * half, 2)]

    def kv_pair_out(half):
        for target in (right, left):
            push(pair(mine, half), kvp_send.at[0], kv_recv.at[4 + x * 2 + half], target)

    arrive(kvbuf.at[mine, zk[1]], kv_recv.at[zk[1]])
    kv_pair_out(z // 2)
    for k in range(2, ZS):
        arrive(kvbuf.at[mine, zk[k]], kv_recv.at[zk[k]])
    kv_pair_out(1 - z // 2)
    push(kvbuf.at[mine], kvb_send.at[0], kv_recv.at[12 + x], sibling)
    for k in range(1, ZS):
        slot = zk[k] * 2 + c
        arrive(qlbuf.at[slot], ql_recv.at[slot])
        push(qlbuf.at[slot], ql_send.at[0], ql_recv.at[slot], sibling)

    loads[6].wait()
    wbuf[mine, :, :] = jnp.concatenate([outp_in[...], jnp.zeros((2, OUT_K), BF16)], axis=0)

    from_left, from_right, from_far = xl * 2 + c, xr * 2 + c, xo * 2 + c
    arrive(pair(from_left, 0), kv_recv.at[4 + xl * 2])
    push(pair(from_left, 0), kvp_send.at[0], kv_recv.at[4 + xl * 2], right)
    push(pair(from_left, 0), kvp_send.at[0], kv_recv.at[16], index(xr, z, 1 - c))
    arrive(pair(from_right, 1), kv_recv.at[4 + xr * 2 + 1])
    push(pair(from_right, 1), kvp_send.at[0], kv_recv.at[4 + xr * 2 + 1], left)
    push(pair(from_right, 1), kvp_send.at[0], kv_recv.at[17], index(xl, z, 1 - c))
    arrive(pair(from_left, 1), kv_recv.at[4 + xl * 2 + 1])
    push(kvbuf.at[from_left], kvb_send.at[0], kv_recv.at[12 + xl], sibling)
    arrive(pair(from_right, 0), kv_recv.at[4 + xr * 2])
    push(kvbuf.at[from_right], kvb_send.at[0], kv_recv.at[12 + xr], sibling)

    for target in (right, left, sibling):
        push(wbuf.at[mine], w_send.at[0], w_recv.at[mine, 0], target)

    for zz in range(ZS):
        slot = zz * 2 + 1 - c
        arrive(qlbuf.at[slot], ql_recv.at[slot])
    ql_rows = qlbuf[...].reshape(8 * SLOT, QC)

    def partial_q(slots):
        width = len(slots) * SLOT
        block_of = (lax.broadcasted_iota(jnp.int32, (8 * SLOT, width), 0) // 4) % 4
        total = jnp.zeros((8 * SLOT, width), F32)
        for j in range(4):
            columns = jnp.concatenate(
                [qbuf[slot, :, j * QC: (j + 1) * QC] for slot in slots], axis=0
            )
            total = jnp.where(block_of == j, dot_nt(ql_rows, columns), total)
        return total

    near = partial_q([x, xr, xl])
    arrive(qbuf.at[xo, :, pl.ds(0, QR // 2)], q_recv.at[xo, 0])
    arrive(qbuf.at[xo, :, pl.ds(QR // 2, QR // 2)], q_recv.at[xo, 1])
    partial = jnp.concatenate([near, partial_q([xo])], axis=1)
    partial = partial.reshape(8, SLOT, XS * SLOT)
    partial = partial[:, 0:8] + partial[:, 8:16]
    partial = jnp.concatenate([partial, partial], axis=2)
    lane_of = lax.broadcasted_iota(jnp.int32, (8, 8, 128), 2)
    qsend[...] = jnp.where(lane_of // 64 == c, partial, 0.0)
    for k in range(1, ZS):
        for cc in (c, 1 - c):
            slot = zk[k] * 2 + cc
            remote(
                qsend.at[slot], qrecv.at[own], qx_send.at[0], qx_recv.at[own],
                {"batch": index(x, zk[k], cc)},
            ).start()
    remote(
        qsend.at[z * 2 + 1 - c], qrecv.at[own], qx_send.at[0], qx_recv.at[own], {"batch": sibling}
    ).start()
    qrecv[own, :, :] = qsend[own]

    row8 = lax.broadcasted_iota(jnp.int32, (8, 1), 0)
    row_of = row8 % 4
    low = row8 < 4
    for load in loads[3:6]:
        load.wait()
    length = jnp.zeros((8, 1), jnp.int32)
    for r in range(4):
        length = jnp.where(row_of == r, len_in[r], length)

    lane64 = lax.broadcasted_iota(jnp.int32, (8, ROPE), 1)
    inverse = jnp.exp((lane64 % (ROPE // 2)).astype(F32) * (-2.0 * math.log(50000.0) / ROPE))
    angles = length.astype(F32) * inverse
    cosine = jnp.cos(angles)
    sine = jnp.sin(angles)
    sine = jnp.where(lane64 < ROPE // 2, -sine, sine)

    def twice(values):
        return jnp.concatenate([values, values], axis=0)

    nr8 = twice(nr_in[...].astype(F32))
    nr_swapped = jnp.concatenate([nr8[:, ROPE // 2:], nr8[:, : ROPE // 2]], axis=1)
    key_new = (nr8 * cosine + nr_swapped * sine).astype(BF16).astype(F32)
    nl8 = twice(nl_in[...].astype(F32))

    for k in range(1, ZS):
        for cc in (c, 1 - c):
            slot = zk[k] * 2 + cc
            arrive(qrecv.at[slot], qx_recv.at[slot])
    arrive(qrecv.at[z * 2 + 1 - c], qx_recv.at[z * 2 + 1 - c])
    pieces = []
    for zz in range(ZS):
        piece = qrecv[2 * zz] + qrecv[2 * zz + 1]
        pieces.append(piece + pltpu.roll(piece, 4, 0))
    q_all = jnp.concatenate(pieces, axis=1)
    lane_q = lax.broadcasted_iota(jnp.int32, (8, 512), 1)
    turn = lane_q % 64 // 16
    x_of = (x + turn + turn // 2 - 2 * (turn // 3)) % 4
    q_all = jnp.where((x_of < 2) == low, q_all, 0.0)
    q_hi = q_all.astype(BF16)
    q_lo = (q_all - q_hi.astype(F32)).astype(BF16)
    selection = sel[...]
    q_sel = dot_nn(q_hi, selection) + dot_nn(q_lo, selection)
    q_nope = q_sel[:, 0: 2 * NOPE].astype(BF16)
    query_rope = (
        q_sel[:, 2 * NOPE: 2 * NOPE + ROPE] * cosine + q_sel[:, 2 * NOPE + ROPE:] * sine
    ).astype(BF16)

    loads[8].wait()
    rope_scores = jnp.zeros((8, CACHE), F32)
    for r in range(4):
        rope_scores = jnp.where(row_of == r, dot_nn(query_rope, rope[r]), rope_scores)

    for xx in (x, xl, xr):
        block = xx * 2 + 1 - c
        arrive(kvbuf.at[block], kv_recv.at[12 + xx])
    for half in range(2):
        arrive(pair(from_far, half), kv_recv.at[4 + xo * 2 + half])
        arrive(pair(xo * 2 + 1 - c, half), kv_recv.at[16 + half])

    def kv_rows(xx):
        return jnp.concatenate(
            [kvbuf[xx * 2 + cc, zz] for zz in range(ZS) for cc in range(2)], axis=0
        )

    query_abs = (
        dot_nn(q_nope[:, :NOPE], kv_rows(0)) + dot_nn(q_nope[:, NOPE:], kv_rows(2))
    ).astype(BF16)

    loads[7].wait()
    scale = (NOPE + ROPE) ** (-0.5)
    scores = jnp.zeros((8, CACHE), F32)
    for r in range(4):
        scores = jnp.where(row_of == r, dot_nt(query_abs, lat[r]), scores)
    scores = scores + rope_scores
    score_new = scale * (
        jnp.sum(query_abs.astype(F32) * nl8, axis=1, keepdims=True)
        + jnp.sum(query_rope.astype(F32) * key_new, axis=1, keepdims=True)
    )
    position = lax.broadcasted_iota(jnp.int32, (8, CACHE), 1)
    scores = jnp.where(position < length, scores * scale, -1e30)
    top = jnp.maximum(jnp.max(scores, axis=1, keepdims=True), score_new)
    old = jnp.exp(scores - top)
    new = jnp.exp(score_new - top)
    denom = jnp.sum(old, axis=1, keepdims=True) + new
    probs = (old / denom).astype(BF16)
    prob_new = (new / denom).astype(BF16).astype(F32)
    context = jnp.zeros((8, KVR), F32)
    for r in range(4):
        context = jnp.where(row_of == r, dot_nn(probs, lat[r]), context)
    context = (context + prob_new * nl8).astype(BF16)
    value = jnp.where(low, dot_nt(context, kv_rows(1)), dot_nt(context, kv_rows(3)))
    z_of_8 = up * ZS + z
    first_at = z_of_8 * (1 - c) + y * c
    second_at = y * (1 - c) + z_of_8 * c

    def ring_peer(steps_z, steps_y):
        to_z, to_y = (z_of_8 + steps_z) % 8, (y + steps_y) % YS
        return {"heads": to_z // ZS * YS + to_y, "batch": index(x, to_z % ZS, c)}

    vx[first_at, :, :] = value.astype(BF16).astype(F32)
    for i in (4, 3, 5, 2, 6, 1, 7):
        remote(
            vx.at[first_at], vx.at[first_at], vx_send.at[0], vx_recv.at[first_at],
            ring_peer(i * (1 - c), i * c),
        ).start()

    arrive(wbuf.at[from_left], w_recv.at[from_left, 0])
    push(
        wbuf.at[from_left, :, pl.ds(0, OUT_K // 2)], w_send.at[0], w_recv.at[from_left, 0], right
    )
    push(wbuf.at[from_left], w_send.at[0], w_recv.at[from_left, 0], sibling)
    arrive(wbuf.at[from_right], w_recv.at[from_right, 0])
    push(
        wbuf.at[from_right, :, pl.ds(OUT_K // 2, OUT_K // 2)], w_send.at[0],
        w_recv.at[from_right, 1], left,
    )
    push(wbuf.at[from_right], w_send.at[0], w_recv.at[from_right, 0], sibling)

    for i in (1, 7, 2, 6, 3, 5, 4):
        slot = (first_at + i) % 8
        arrive(vx.at[slot], vx_recv.at[slot])
    vh[second_at, :, :] = vx[...].reshape(64, 128).astype(BF16)

    for i in (4, 3, 5, 2, 6, 1, 7):
        remote(
            vh.at[second_at], vh.at[second_at], vh_send.at[0], vh_recv.at[second_at],
            ring_peer(i * c, i * (1 - c)),
        ).start()

    arrive(wbuf.at[from_far, :, pl.ds(0, OUT_K // 2)], w_recv.at[from_far, 0])
    arrive(wbuf.at[from_far, :, pl.ds(OUT_K // 2, OUT_K // 2)], w_recv.at[from_far, 1])
    push(wbuf.at[from_far], w_send.at[0], w_recv.at[from_far, 0], sibling)

    @pl.loop(0, 32)
    def _(t):
        start = (((t // 2) % 4) * 8 + (t // 8) * 2 + t % 2) * 14
        col = lax.broadcasted_iota(jnp.int32, (SLOT, 448), 1) - start
        row = lax.broadcasted_iota(jnp.int32, (SLOT, 448), 0)
        block = jnp.where((col == row) & (row < 14), 1.0, 0.0).astype(BF16)
        sel_out[pl.ds(pl.multiple_of(t * SLOT, SLOT), SLOT), :] = block

    for xx in (x, xl, xr, xo):
        block = xx * 2 + 1 - c
        arrive(wbuf.at[block], w_recv.at[block, 0])

    row32 = lax.broadcasted_iota(jnp.int32, (32, 128), 0)
    is_low = (row32 % 8) < 4
    zero = jnp.zeros((32, 128), BF16)

    def by_head(block):
        return jnp.concatenate(
            [jnp.where(is_low, block, zero), jnp.where(is_low, zero, block)], axis=1
        )

    def out_rows(half, at_y):
        columns = pl.ds(pl.multiple_of((half * YS + at_y) * 256, 256), 256)
        return wbuf[:, :, columns].reshape(8 * SLOT, 256)

    @pl.when(c == 0)
    def _():
        y_all = jnp.zeros((32, 128), F32)
        for i in (0, 1, 7, 2, 6, 3, 5, 4):
            other = (y + i) % YS
            if i:
                arrive(vh.at[other], vh_recv.at[other])
            for half in range(2):
                block = vh[other, half * 32: half * 32 + 32]
                y_all = y_all + dot_nt(by_head(block), out_rows(half, other))
        ysend[...] = y_all.reshape(ZS, 8, 128)

    @pl.when(c == 1)
    def _():
        for i in (1, 7, 2, 6, 3, 5, 4):
            other = (z_of_8 + i) % 8
            arrive(vh.at[other], vh_recv.at[other])
        y_all = jnp.zeros((32, 128), F32)
        for half in range(2):
            blocks = vh[half * ZS: half * ZS + ZS].astype(F32).reshape(ZS, YS, 8, 128)
            for at_y in range(YS):
                block = blocks[:, at_y].reshape(32, 128).astype(BF16)
                y_all = y_all + dot_nt(by_head(block), out_rows(half, at_y))
        ysend[...] = y_all.reshape(ZS, 8, 128)

    for k in range(1, ZS):
        remote(
            ysend.at[zk[k]], yrecv.at[z], y_send.at[0], y_recv.at[z],
            {"batch": index(x, zk[k], c)},
        ).start()
    yrecv[z, :, :] = ysend[z]
    for k in range(1, ZS):
        arrive(yrecv.at[zk[k]], y_recv.at[zk[k]])
    pieces = []
    for zz in range(ZS):
        piece = yrecv[zz]
        pieces.append(piece + pltpu.roll(piece, 4, 0))
    summed = jnp.concatenate(pieces, axis=1).astype(BF16)
    y_ref[...] = dot_nn(summed, sel_out[...])[0:4]

    for ref, sem in (
        (qbuf.at[0:3], q_send), (kvbuf.at[0, 0:3], kvz_send), (kvbuf.at[0:4], kvp_send),
        (kvbuf.at[0:3], kvb_send),
        (qlbuf.at[0:7], ql_send), (qsend.at[0:7], qx_send), (wbuf.at[0:7], w_send),
        (vx.at[0:7], vx_send), (vh.at[0:7], vh_send), (ysend.at[0:3], y_send),
    ):
        arrive(ref, sem.at[0])


def shards(
    q_latent, new_latent, new_rope, latent_cache, rope_cache, lengths, q_up, kv_up, out_proj
):
    hbm = pl.BlockSpec(memory_space=pltpu.HBM)
    dma = pltpu.SemaphoreType.DMA
    return pl.pallas_call(
        kernel,
        out_shape=jax.ShapeDtypeStruct((4, 448), F32),
        in_specs=[hbm] * 9,
        out_specs=pl.BlockSpec(memory_space=pltpu.VMEM),
        scratch_shapes=[
            pltpu.VMEM((4, QR), BF16),
            pltpu.VMEM((4, KVR), BF16),
            pltpu.VMEM((4, ROPE), BF16),
            pltpu.SMEM((4,), jnp.int32),
            pltpu.VMEM((QROWS, QR), BF16),
            pltpu.VMEM((14, OUT_K), BF16),
            pltpu.VMEM((4, CACHE, KVR), BF16),
            pltpu.VMEM((4, ROPE, CACHE), BF16),
            pltpu.VMEM((XS, SLOT, QR), BF16),
            pltpu.VMEM((8, SLOT, QC), BF16),
            pltpu.VMEM((8, 8, 128), F32),
            pltpu.VMEM((8, 8, 128), F32),
            pltpu.VMEM((8, ZS, SLOT, KVR), BF16),
            pltpu.VMEM((8, SLOT, OUT_K), BF16),
            pltpu.VMEM((512, 2 * NOPE + 2 * ROPE), BF16),
            pltpu.VMEM((512, 448), BF16),
            pltpu.VMEM((2 * ZS, 8, 128), F32),
            pltpu.VMEM((YS, 64, 128), BF16),
            pltpu.VMEM((ZS, 8, 128), F32),
            pltpu.VMEM((ZS, 8, 128), F32),
            dma((9,)),
            dma((1,)), dma((XS, 2)),
            dma((1,)), dma((8,)),
            dma((1,)), dma((8,)),
            dma((1,)), dma((1,)), dma((1,)), dma((18,)),
            dma((1,)), dma((8, 2)),
            dma((1,)), dma((2 * ZS,)),
            dma((1,)), dma((YS,)),
            dma((1,)), dma((ZS,)),
        ],
        compiler_params=pltpu.CompilerParams(
            collective_id=0, has_side_effects=True, vmem_limit_bytes=60 * 2**20
        ),
        cost_estimate=pl.CostEstimate(
            flops=4 * 10**8, bytes_accessed=5 * 10**6, transcendentals=10**4
        ),
    )(
        q_latent, new_latent, new_rope, latent_cache, jnp.swapaxes(rope_cache, 1, 2), lengths,
        q_up, kv_up, out_proj,
    ).astype(BF16)


def solution(mesh):
    placed = (
        P("batch", None),
        P("batch", None),
        P("batch", None),
        P("batch", None, None),
        P("batch", None, None),
        P("batch"),
        P(("heads", "batch"), None),
        P(("heads", "batch"), None),
        P(("heads", "batch"), None),
    )
    return jax.shard_map(
        shards, mesh=mesh, in_specs=placed, out_specs=P("batch", "heads"), check_vma=False
    )
```

```python
import functools
import math

import jax
import jax.numpy as jnp
from jax import lax
from jax.experimental import pallas as pl
from jax.experimental.pallas import tpu as pltpu
from jax.sharding import PartitionSpec as P

QR = 1536
KVR = 512
NOPE = 128
ROPE = 64
CACHE = 1024
QROWS = 12
SLOT = 16
XS, ZS = 4, 4
YS = 8
QC = QR // 4
OUT_K = 4096
F32 = jnp.float32
BF16 = jnp.bfloat16
NT = (((1,), (1,)), ((), ()))


def dot_nt(a, b):
    return lax.dot_general(a, b, NT, preferred_element_type=F32)


def dot_nn(a, b):
    return jnp.dot(a, b, preferred_element_type=F32)


def kernel(
    ql_hbm, nl_hbm, nr_hbm, lat_hbm, rope_hbm, len_hbm, qup_hbm, kvup_hbm, outp_hbm, y_ref,
    ql_in, nl_in, nr_in, len_in, qup_in, outp_in, lat, rope,
    qbuf, qlbuf, qsend, qrecv, kvbuf, wbuf, sel, sel_out, vx, vh, ysend, yrecv,
    in_sem, q_send, q_recv, ql_send, ql_recv, qx_send, qx_recv, kvz_send, kvp_send, kvb_send, kv_recv,
    w_send, w_recv, vx_send, vx_recv, vh_send, vh_recv, y_send, y_recv,
):
    h = lax.axis_index("heads")
    b = lax.axis_index("batch")
    x, z, c = b // 8, (b // 2) % 4, b % 2
    y, up = h % YS, h // YS

    def index(xx, zz, cc):
        return xx * 8 + zz * 2 + cc

    zk = [z, z + 1 - 2 * (z % 2), (z + 2) % 4, 3 - z]
    xr, xl, xo = (x + 1) % 4, (x + 3) % 4, (x + 2) % 4
    right, left, sibling = index(xr, z, c), index(xl, z, c), index(x, z, 1 - c)
    mine, theirs = x * 2 + c, x * 2 + 1 - c
    own = z * 2 + c

    loads = [
        pltpu.make_async_copy(source, target, in_sem.at[i])
        for i, (source, target) in enumerate(
            [
                (qup_hbm, qup_in), (ql_hbm, ql_in), (kvup_hbm, kvbuf.at[mine, z]),
                (nl_hbm, nl_in), (nr_hbm, nr_in), (len_hbm, len_in), (outp_hbm, outp_in),
                (lat_hbm, lat), (rope_hbm, rope),
            ]
        )
    ]
    barrier = pltpu.get_barrier_semaphore()

    def greet(target):
        pl.semaphore_signal(barrier, inc=1, device_id={"batch": target})

    across = (1 - up) * YS + y
    for k in range(ZS):
        pl.semaphore_signal(
            barrier, inc=1, device_id={"heads": across, "batch": index(x, zk[k], c)}
        )

    @pl.loop(1, YS)
    def _(i):
        pl.semaphore_signal(barrier, inc=1, device_id={"heads": up * YS + (y + i) % YS})

    for k in range(1, ZS):
        greet(index(x, zk[k], c))
        greet(index(x, zk[k], 1 - c))
    for cc in (c, 1 - c):
        greet(index(xr, z, cc))
        greet(index(xl, z, cc))
    greet(sibling)

    for i in (2, 0, 1, 3, 4, 5, 6, 7, 8):
        loads[i].start()
    loads[2].wait()
    pl.semaphore_wait(barrier, ZS + YS - 1 + 6 + 4 + 1)

    def remote(source, target, send_sem, recv_sem, device):
        return pltpu.make_async_remote_copy(
            src_ref=source, dst_ref=target, send_sem=send_sem, recv_sem=recv_sem,
            device_id=device,
        )

    def push(ref, send_sem, recv_sem, target):
        remote(ref, ref, send_sem, recv_sem, {"batch": target}).start()

    def arrive(ref, recv_sem):
        pltpu.make_async_copy(ref, ref, recv_sem).wait()

    for k in (3, 2, 1):
        push(kvbuf.at[mine, z], kvz_send.at[0], kv_recv.at[z], index(x, zk[k], c))

    loads[0].wait()
    qbuf[x, :, :] = jnp.concatenate([qup_in[...], jnp.zeros((SLOT - QROWS, QR), BF16)], axis=0)
    for target in (right, left):
        push(qbuf.at[x], q_send.at[0], q_recv.at[x, 0], target)
    loads[1].wait()
    ql_own = ql_in[...].astype(F32)
    qlbuf[own, :, :] = jnp.concatenate(
        [ql_own[:, j * QC: (j + 1) * QC] for j in range(4)], axis=0
    ).astype(BF16)
    for k in range(1, ZS):
        push(qlbuf.at[own], ql_send.at[0], ql_recv.at[own], index(x, zk[k], c))
    push(qlbuf.at[own], ql_send.at[0], ql_recv.at[own], sibling)

    @pl.loop(0, 32)
    def _(t):
        x_t = (x + t % 4 + (t % 4) // 2 - 2 * ((t % 4) // 3)) % 4
        first_row = QROWS * ((x_t % 2) * 8 + (t // 8) * 2 + (t // 4) % 2)
        shape = (SLOT, 2 * NOPE + 2 * ROPE)
        within = lax.broadcasted_iota(jnp.int32, shape, 0)
        col = lax.broadcasted_iota(jnp.int32, shape, 1)
        row = within + first_row
        nope = (row < NOPE) & (col == row + (x_t // 2) * NOPE)
        rotary = row - NOPE
        swapped = (rotary + ROPE // 2) % ROPE
        rope_at = (row >= NOPE) & (
            (col == 2 * NOPE + rotary) | (col == 2 * NOPE + ROPE + swapped)
        )
        block = jnp.where((within < QROWS) & (nope | rope_at), 1.0, 0.0).astype(BF16)
        sel[pl.ds(pl.multiple_of(t * SLOT, SLOT), SLOT), :] = block

    arrive(qbuf.at[xl], q_recv.at[xl, 0])
    push(qbuf.at[xl, :, pl.ds(0, QR // 2)], q_send.at[0], q_recv.at[xl, 0], right)
    arrive(qbuf.at[xr], q_recv.at[xr, 0])
    push(qbuf.at[xr, :, pl.ds(QR // 2, QR // 2)], q_send.at[0], q_recv.at[xr, 1], left)

    def pair(block, half):
        return kvbuf.at[block, pl.ds(2 * half, 2)]

    def kv_pair_out(half):
        for target in (right, left):
            push(pair(mine, half), kvp_send.at[0], kv_recv.at[4 + x * 2 + half], target)

    arrive(kvbuf.at[mine, zk[1]], kv_recv.at[zk[1]])
    kv_pair_out(z // 2)
    for k in range(2, ZS):
        arrive(kvbuf.at[mine, zk[k]], kv_recv.at[zk[k]])
    kv_pair_out(1 - z // 2)
    push(kvbuf.at[mine], kvb_send.at[0], kv_recv.at[12 + x], sibling)
    for k in range(1, ZS):
        slot = zk[k] * 2 + c
        arrive(qlbuf.at[slot], ql_recv.at[slot])
        push(qlbuf.at[slot], ql_send.at[0], ql_recv.at[slot], sibling)

    loads[6].wait()
    wbuf[mine, :, :] = jnp.concatenate([outp_in[...], jnp.zeros((2, OUT_K), BF16)], axis=0)

    from_left, from_right, from_far = xl * 2 + c, xr * 2 + c, xo * 2 + c
    arrive(pair(from_left, 0), kv_recv.at[4 + xl * 2])
    push(pair(from_left, 0), kvp_send.at[0], kv_recv.at[4 + xl * 2], right)
    push(pair(from_left, 0), kvp_send.at[0], kv_recv.at[16], index(xr, z, 1 - c))
    arrive(pair(from_right, 1), kv_recv.at[4 + xr * 2 + 1])
    push(pair(from_right, 1), kvp_send.at[0], kv_recv.at[4 + xr * 2 + 1], left)
    push(pair(from_right, 1), kvp_send.at[0], kv_recv.at[17], index(xl, z, 1 - c))
    arrive(pair(from_left, 1), kv_recv.at[4 + xl * 2 + 1])
    push(kvbuf.at[from_left], kvb_send.at[0], kv_recv.at[12 + xl], sibling)
    arrive(pair(from_right, 0), kv_recv.at[4 + xr * 2])
    push(kvbuf.at[from_right], kvb_send.at[0], kv_recv.at[12 + xr], sibling)

    for target in (right, left, sibling):
        push(wbuf.at[mine], w_send.at[0], w_recv.at[mine, 0], target)

    for zz in range(ZS):
        slot = zz * 2 + 1 - c
        arrive(qlbuf.at[slot], ql_recv.at[slot])
    ql_rows = qlbuf[...].reshape(8 * SLOT, QC)

    def partial_q(slots):
        width = len(slots) * SLOT
        block_of = (lax.broadcasted_iota(jnp.int32, (8 * SLOT, width), 0) // 4) % 4
        total = jnp.zeros((8 * SLOT, width), F32)
        for j in range(4):
            columns = jnp.concatenate(
                [qbuf[slot, :, j * QC: (j + 1) * QC] for slot in slots], axis=0
            )
            total = jnp.where(block_of == j, dot_nt(ql_rows, columns), total)
        return total

    near = partial_q([x, xr, xl])
    arrive(qbuf.at[xo, :, pl.ds(0, QR // 2)], q_recv.at[xo, 0])
    arrive(qbuf.at[xo, :, pl.ds(QR // 2, QR // 2)], q_recv.at[xo, 1])
    partial = jnp.concatenate([near, partial_q([xo])], axis=1)
    partial = partial.reshape(8, SLOT, XS * SLOT)
    partial = partial[:, 0:8] + partial[:, 8:16]
    partial = jnp.concatenate([partial, partial], axis=2)
    lane_of = lax.broadcasted_iota(jnp.int32, (8, 8, 128), 2)
    qsend[...] = jnp.where(lane_of // 64 == c, partial, 0.0)
    for k in range(1, ZS):
        for cc in (c, 1 - c):
            slot = zk[k] * 2 + cc
            remote(
                qsend.at[slot], qrecv.at[own], qx_send.at[0], qx_recv.at[own],
                {"batch": index(x, zk[k], cc)},
            ).start()
    remote(
        qsend.at[z * 2 + 1 - c], qrecv.at[own], qx_send.at[0], qx_recv.at[own], {"batch": sibling}
    ).start()
    qrecv[own, :, :] = qsend[own]

    row8 = lax.broadcasted_iota(jnp.int32, (8, 1), 0)
    row_of = row8 % 4
    low = row8 < 4
    for load in loads[3:6]:
        load.wait()
    length = jnp.zeros((8, 1), jnp.int32)
    for r in range(4):
        length = jnp.where(row_of == r, len_in[r], length)

    lane64 = lax.broadcasted_iota(jnp.int32, (8, ROPE), 1)
    inverse = jnp.exp((lane64 % (ROPE // 2)).astype(F32) * (-2.0 * math.log(50000.0) / ROPE))
    angles = length.astype(F32) * inverse
    cosine = jnp.cos(angles)
    sine = jnp.sin(angles)
    sine = jnp.where(lane64 < ROPE // 2, -sine, sine)

    def twice(values):
        return jnp.concatenate([values, values], axis=0)

    nr8 = twice(nr_in[...].astype(F32))
    nr_swapped = jnp.concatenate([nr8[:, ROPE // 2:], nr8[:, : ROPE // 2]], axis=1)
    key_new = (nr8 * cosine + nr_swapped * sine).astype(BF16).astype(F32)
    nl8 = twice(nl_in[...].astype(F32))

    for k in range(1, ZS):
        for cc in (c, 1 - c):
            slot = zk[k] * 2 + cc
            arrive(qrecv.at[slot], qx_recv.at[slot])
    arrive(qrecv.at[z * 2 + 1 - c], qx_recv.at[z * 2 + 1 - c])
    pieces = []
    for zz in range(ZS):
        piece = qrecv[2 * zz] + qrecv[2 * zz + 1]
        pieces.append(piece + pltpu.roll(piece, 4, 0))
    q_all = jnp.concatenate(pieces, axis=1)
    lane_q = lax.broadcasted_iota(jnp.int32, (8, 512), 1)
    turn = lane_q % 64 // 16
    x_of = (x + turn + turn // 2 - 2 * (turn // 3)) % 4
    q_all = jnp.where((x_of < 2) == low, q_all, 0.0)
    q_hi = q_all.astype(BF16)
    q_lo = (q_all - q_hi.astype(F32)).astype(BF16)
    selection = sel[...]
    q_sel = dot_nn(q_hi, selection) + dot_nn(q_lo, selection)
    q_nope = q_sel[:, 0: 2 * NOPE].astype(BF16)
    query_rope = (
        q_sel[:, 2 * NOPE: 2 * NOPE + ROPE] * cosine + q_sel[:, 2 * NOPE + ROPE:] * sine
    ).astype(BF16)

    loads[8].wait()
    rope_scores = jnp.zeros((8, CACHE), F32)
    for r in range(4):
        rope_scores = jnp.where(row_of == r, dot_nn(query_rope, rope[r]), rope_scores)

    for xx in (x, xl, xr):
        block = xx * 2 + 1 - c
        arrive(kvbuf.at[block], kv_recv.at[12 + xx])
    for half in range(2):
        arrive(pair(from_far, half), kv_recv.at[4 + xo * 2 + half])
        arrive(pair(xo * 2 + 1 - c, half), kv_recv.at[16 + half])

    def kv_rows(xx):
        return jnp.concatenate(
            [kvbuf[xx * 2 + cc, zz] for zz in range(ZS) for cc in range(2)], axis=0
        )

    query_abs = (
        dot_nn(q_nope[:, :NOPE], kv_rows(0)) + dot_nn(q_nope[:, NOPE:], kv_rows(2))
    ).astype(BF16)

    loads[7].wait()
    scale = (NOPE + ROPE) ** (-0.5)
    scores = jnp.zeros((8, CACHE), F32)
    for r in range(4):
        scores = jnp.where(row_of == r, dot_nt(query_abs, lat[r]), scores)
    scores = scores + rope_scores
    score_new = scale * (
        jnp.sum(query_abs.astype(F32) * nl8, axis=1, keepdims=True)
        + jnp.sum(query_rope.astype(F32) * key_new, axis=1, keepdims=True)
    )
    position = lax.broadcasted_iota(jnp.int32, (8, CACHE), 1)
    scores = jnp.where(position < length, scores * scale, -1e30)
    top = jnp.maximum(jnp.max(scores, axis=1, keepdims=True), score_new)
    old = jnp.exp(scores - top)
    new = jnp.exp(score_new - top)
    denom = jnp.sum(old, axis=1, keepdims=True) + new
    probs = (old / denom).astype(BF16)
    prob_new = (new / denom).astype(BF16).astype(F32)
    context = jnp.zeros((8, KVR), F32)
    for r in range(4):
        context = jnp.where(row_of == r, dot_nn(probs, lat[r]), context)
    context = (context + prob_new * nl8).astype(BF16)
    value = jnp.where(low, dot_nt(context, kv_rows(1)), dot_nt(context, kv_rows(3)))
    z_of_8 = up * ZS + z
    first_at = z_of_8 * c + y * (1 - c)
    second_at = y * c + z_of_8 * (1 - c)

    def ring_peer(steps_z, steps_y):
        to_z, to_y = (z_of_8 + steps_z) % 8, (y + steps_y) % YS
        return {"heads": to_z // ZS * YS + to_y, "batch": index(x, to_z % ZS, c)}

    vx[first_at, :, :] = value.astype(BF16).astype(F32)
    for i in (4, 3, 5, 2, 6, 1, 7):
        remote(
            vx.at[first_at], vx.at[first_at], vx_send.at[0], vx_recv.at[first_at],
            ring_peer(i * c, i * (1 - c)),
        ).start()

    arrive(wbuf.at[from_left], w_recv.at[from_left, 0])
    push(
        wbuf.at[from_left, :, pl.ds(0, OUT_K // 2)], w_send.at[0], w_recv.at[from_left, 0], right
    )
    push(wbuf.at[from_left], w_send.at[0], w_recv.at[from_left, 0], sibling)
    arrive(wbuf.at[from_right], w_recv.at[from_right, 0])
    push(
        wbuf.at[from_right, :, pl.ds(OUT_K // 2, OUT_K // 2)], w_send.at[0],
        w_recv.at[from_right, 1], left,
    )
    push(wbuf.at[from_right], w_send.at[0], w_recv.at[from_right, 0], sibling)

    for i in (1, 7, 2, 6, 3, 5, 4):
        slot = (first_at + i) % 8
        arrive(vx.at[slot], vx_recv.at[slot])
    vh[second_at, :, :] = vx[...].reshape(64, 128).astype(BF16)

    for i in (4, 3, 5, 2, 6, 1, 7):
        remote(
            vh.at[second_at], vh.at[second_at], vh_send.at[0], vh_recv.at[second_at],
            ring_peer(i * (1 - c), i * c),
        ).start()

    arrive(wbuf.at[from_far, :, pl.ds(0, OUT_K // 2)], w_recv.at[from_far, 0])
    arrive(wbuf.at[from_far, :, pl.ds(OUT_K // 2, OUT_K // 2)], w_recv.at[from_far, 1])
    push(wbuf.at[from_far], w_send.at[0], w_recv.at[from_far, 0], sibling)

    @pl.loop(0, 32)
    def _(t):
        start = (((t // 2) % 4) * 8 + (t // 8) * 2 + t % 2) * 14
        col = lax.broadcasted_iota(jnp.int32, (SLOT, 448), 1) - start
        row = lax.broadcasted_iota(jnp.int32, (SLOT, 448), 0)
        block = jnp.where((col == row) & (row < 14), 1.0, 0.0).astype(BF16)
        sel_out[pl.ds(pl.multiple_of(t * SLOT, SLOT), SLOT), :] = block

    for xx in (x, xl, xr, xo):
        block = xx * 2 + 1 - c
        arrive(wbuf.at[block], w_recv.at[block, 0])

    row32 = lax.broadcasted_iota(jnp.int32, (32, 128), 0)
    is_low = (row32 % 8) < 4
    zero = jnp.zeros((32, 128), BF16)

    def by_head(block):
        return jnp.concatenate(
            [jnp.where(is_low, block, zero), jnp.where(is_low, zero, block)], axis=1
        )

    def out_rows(half, at_y):
        columns = pl.ds(pl.multiple_of((half * YS + at_y) * 256, 256), 256)
        return wbuf[:, :, columns].reshape(8 * SLOT, 256)

    @pl.when(c == 1)
    def _():
        y_all = jnp.zeros((32, 128), F32)
        for i in (0, 1, 7, 2, 6, 3, 5, 4):
            other = (y + i) % YS
            if i:
                arrive(vh.at[other], vh_recv.at[other])
            for half in range(2):
                block = vh[other, half * 32: half * 32 + 32]
                y_all = y_all + dot_nt(by_head(block), out_rows(half, other))
        ysend[...] = y_all.reshape(ZS, 8, 128)

    @pl.when(c == 0)
    def _():
        for i in (1, 7, 2, 6, 3, 5, 4):
            other = (z_of_8 + i) % 8
            arrive(vh.at[other], vh_recv.at[other])
        y_all = jnp.zeros((32, 128), F32)
        for half in range(2):
            blocks = vh[half * ZS: half * ZS + ZS].astype(F32).reshape(ZS, YS, 8, 128)
            for at_y in range(YS):
                block = blocks[:, at_y].reshape(32, 128).astype(BF16)
                y_all = y_all + dot_nt(by_head(block), out_rows(half, at_y))
        ysend[...] = y_all.reshape(ZS, 8, 128)

    for k in range(1, ZS):
        remote(
            ysend.at[zk[k]], yrecv.at[z], y_send.at[0], y_recv.at[z],
            {"batch": index(x, zk[k], c)},
        ).start()
    yrecv[z, :, :] = ysend[z]
    for k in range(1, ZS):
        arrive(yrecv.at[zk[k]], y_recv.at[zk[k]])
    pieces = []
    for zz in range(ZS):
        piece = yrecv[zz]
        pieces.append(piece + pltpu.roll(piece, 4, 0))
    summed = jnp.concatenate(pieces, axis=1).astype(BF16)
    y_ref[...] = dot_nn(summed, sel_out[...])[0:4]

    for ref, sem in (
        (qbuf.at[0:3], q_send), (kvbuf.at[0, 0:3], kvz_send), (kvbuf.at[0:4], kvp_send),
        (kvbuf.at[0:3], kvb_send),
        (qlbuf.at[0:7], ql_send), (qsend.at[0:7], qx_send), (wbuf.at[0:7], w_send),
        (vx.at[0:7], vx_send), (vh.at[0:7], vh_send), (ysend.at[0:3], y_send),
    ):
        arrive(ref, sem.at[0])


def shards(
    q_latent, new_latent, new_rope, latent_cache, rope_cache, lengths, q_up, kv_up, out_proj
):
    hbm = pl.BlockSpec(memory_space=pltpu.HBM)
    dma = pltpu.SemaphoreType.DMA
    return pl.pallas_call(
        kernel,
        out_shape=jax.ShapeDtypeStruct((4, 448), F32),
        in_specs=[hbm] * 9,
        out_specs=pl.BlockSpec(memory_space=pltpu.VMEM),
        scratch_shapes=[
            pltpu.VMEM((4, QR), BF16),
            pltpu.VMEM((4, KVR), BF16),
            pltpu.VMEM((4, ROPE), BF16),
            pltpu.SMEM((4,), jnp.int32),
            pltpu.VMEM((QROWS, QR), BF16),
            pltpu.VMEM((14, OUT_K), BF16),
            pltpu.VMEM((4, CACHE, KVR), BF16),
            pltpu.VMEM((4, ROPE, CACHE), BF16),
            pltpu.VMEM((XS, SLOT, QR), BF16),
            pltpu.VMEM((8, SLOT, QC), BF16),
            pltpu.VMEM((8, 8, 128), F32),
            pltpu.VMEM((8, 8, 128), F32),
            pltpu.VMEM((8, ZS, SLOT, KVR), BF16),
            pltpu.VMEM((8, SLOT, OUT_K), BF16),
            pltpu.VMEM((512, 2 * NOPE + 2 * ROPE), BF16),
            pltpu.VMEM((512, 448), BF16),
            pltpu.VMEM((2 * ZS, 8, 128), F32),
            pltpu.VMEM((YS, 64, 128), BF16),
            pltpu.VMEM((ZS, 8, 128), F32),
            pltpu.VMEM((ZS, 8, 128), F32),
            dma((9,)),
            dma((1,)), dma((XS, 2)),
            dma((1,)), dma((8,)),
            dma((1,)), dma((8,)),
            dma((1,)), dma((1,)), dma((1,)), dma((18,)),
            dma((1,)), dma((8, 2)),
            dma((1,)), dma((2 * ZS,)),
            dma((1,)), dma((YS,)),
            dma((1,)), dma((ZS,)),
        ],
        compiler_params=pltpu.CompilerParams(
            collective_id=0, has_side_effects=True, vmem_limit_bytes=60 * 2**20
        ),
        cost_estimate=pl.CostEstimate(
            flops=4 * 10**8, bytes_accessed=5 * 10**6, transcendentals=10**4
        ),
    )(
        q_latent, new_latent, new_rope, latent_cache, jnp.swapaxes(rope_cache, 1, 2), lengths,
        q_up, kv_up, out_proj,
    ).astype(BF16)


def solution(mesh):
    placed = (
        P("batch", None),
        P("batch", None),
        P("batch", None),
        P("batch", None, None),
        P("batch", None, None),
        P("batch"),
        P(("heads", "batch"), None),
        P(("heads", "batch"), None),
        P(("heads", "batch"), None),
    )
    return jax.shard_map(
        shards, mesh=mesh, in_specs=placed, out_specs=P("batch", "heads"), check_vma=False
    )
```

```python
import functools
import math

import jax
import jax.numpy as jnp
from jax import lax
from jax.experimental import pallas as pl
from jax.experimental.pallas import tpu as pltpu
from jax.sharding import PartitionSpec as P

QR = 1536
KVR = 512
NOPE = 128
ROPE = 64
CACHE = 1024
QROWS = 12
SLOT = 16
XS, ZS = 4, 4
YS = 8
QC = QR // 4
OUT_K = 4096
F32 = jnp.float32
BF16 = jnp.bfloat16
NT = (((1,), (1,)), ((), ()))


def dot_nt(a, b):
    return lax.dot_general(a, b, NT, preferred_element_type=F32)


def dot_nn(a, b):
    return jnp.dot(a, b, preferred_element_type=F32)


def kernel(
    ql_hbm, nl_hbm, nr_hbm, lat_hbm, rope_hbm, len_hbm, qup_hbm, kvup_hbm, outp_hbm, y_ref,
    ql_in, nl_in, nr_in, len_in, qup_in, outp_in, lat, rope,
    qbuf, qlbuf, qsend, qrecv, kvbuf, wbuf, sel, sel_out, vx, vh, ysend, yrecv,
    in_sem, q_send, q_recv, ql_send, ql_recv, qx_send, qx_recv, kvz_send, kvp_send, kvb_send, kv_recv,
    w_send, w_recv, vx_send, vx_recv, vh_send, vh_recv, y_send, y_recv,
):
    h = lax.axis_index("heads")
    b = lax.axis_index("batch")
    x, z, c = b // 8, (b // 2) % 4, b % 2
    y, up = h % YS, h // YS

    def index(xx, zz, cc):
        return xx * 8 + zz * 2 + cc

    zk = [z, z + 1 - 2 * (z % 2), (z + 2) % 4, 3 - z]
    xr, xl, xo = (x + 1) % 4, (x + 3) % 4, (x + 2) % 4
    right, left, sibling = index(xr, z, c), index(xl, z, c), index(x, z, 1 - c)
    mine, theirs = x * 2 + c, x * 2 + 1 - c
    own = z * 2 + c

    loads = [
        pltpu.make_async_copy(source, target, in_sem.at[i])
        for i, (source, target) in enumerate(
            [
                (qup_hbm, qup_in), (ql_hbm, ql_in), (kvup_hbm, kvbuf.at[mine, z]),
                (nl_hbm, nl_in), (nr_hbm, nr_in), (len_hbm, len_in), (outp_hbm, outp_in),
                (lat_hbm, lat), (rope_hbm, rope),
            ]
        )
    ]
    barrier = pltpu.get_barrier_semaphore()

    def greet(target):
        pl.semaphore_signal(barrier, inc=1, device_id={"batch": target})

    across = (1 - up) * YS + y
    for k in range(ZS):
        pl.semaphore_signal(
            barrier, inc=1, device_id={"heads": across, "batch": index(x, zk[k], c)}
        )

    @pl.loop(1, YS)
    def _(i):
        pl.semaphore_signal(barrier, inc=1, device_id={"heads": up * YS + (y + i) % YS})

    for k in range(1, ZS):
        greet(index(x, zk[k], c))
        greet(index(x, zk[k], 1 - c))
    for cc in (c, 1 - c):
        greet(index(xr, z, cc))
        greet(index(xl, z, cc))
    greet(sibling)

    for i in (2, 0, 1, 3, 4, 5, 6, 7, 8):
        loads[i].start()
    loads[2].wait()
    pl.semaphore_wait(barrier, ZS + YS - 1 + 6 + 4 + 1)

    def remote(source, target, send_sem, recv_sem, device):
        return pltpu.make_async_remote_copy(
            src_ref=source, dst_ref=target, send_sem=send_sem, recv_sem=recv_sem,
            device_id=device,
        )

    def push(ref, send_sem, recv_sem, target):
        remote(ref, ref, send_sem, recv_sem, {"batch": target}).start()

    def arrive(ref, recv_sem):
        pltpu.make_async_copy(ref, ref, recv_sem).wait()

    for k in (3, 2, 1):
        push(kvbuf.at[mine, z], kvz_send.at[0], kv_recv.at[z], index(x, zk[k], c))

    loads[0].wait()
    qbuf[x, :, :] = jnp.concatenate([qup_in[...], jnp.zeros((SLOT - QROWS, QR), BF16)], axis=0)
    for target in (right, left):
        push(qbuf.at[x], q_send.at[0], q_recv.at[x, 0], target)
    loads[1].wait()
    ql_own = ql_in[...].astype(F32)
    qlbuf[own, :, :] = jnp.concatenate(
        [ql_own[:, j * QC: (j + 1) * QC] for j in range(4)], axis=0
    ).astype(BF16)
    for k in range(1, ZS):
        push(qlbuf.at[own], ql_send.at[0], ql_recv.at[own], index(x, zk[k], c))
    push(qlbuf.at[own], ql_send.at[0], ql_recv.at[own], sibling)

    @pl.loop(0, 32)
    def _(t):
        x_t = (x + t % 4 + (t % 4) // 2 - 2 * ((t % 4) // 3)) % 4
        first_row = QROWS * ((x_t % 2) * 8 + (t // 8) * 2 + (t // 4) % 2)
        shape = (SLOT, 2 * NOPE + 2 * ROPE)
        within = lax.broadcasted_iota(jnp.int32, shape, 0)
        col = lax.broadcasted_iota(jnp.int32, shape, 1)
        row = within + first_row
        nope = (row < NOPE) & (col == row + (x_t // 2) * NOPE)
        rotary = row - NOPE
        swapped = (rotary + ROPE // 2) % ROPE
        rope_at = (row >= NOPE) & (
            (col == 2 * NOPE + rotary) | (col == 2 * NOPE + ROPE + swapped)
        )
        block = jnp.where((within < QROWS) & (nope | rope_at), 1.0, 0.0).astype(BF16)
        sel[pl.ds(pl.multiple_of(t * SLOT, SLOT), SLOT), :] = block

    arrive(qbuf.at[xl], q_recv.at[xl, 0])
    push(qbuf.at[xl, :, pl.ds(0, QR // 2)], q_send.at[0], q_recv.at[xl, 0], right)
    arrive(qbuf.at[xr], q_recv.at[xr, 0])
    push(qbuf.at[xr, :, pl.ds(QR // 2, QR // 2)], q_send.at[0], q_recv.at[xr, 1], left)

    def pair(block, half):
        return kvbuf.at[block, pl.ds(2 * half, 2)]

    def kv_pair_out(half):
        for target in (right, left):
            push(pair(mine, half), kvp_send.at[0], kv_recv.at[4 + x * 2 + half], target)

    arrive(kvbuf.at[mine, zk[1]], kv_recv.at[zk[1]])
    kv_pair_out(z // 2)
    for k in range(2, ZS):
        arrive(kvbuf.at[mine, zk[k]], kv_recv.at[zk[k]])
    kv_pair_out(1 - z // 2)
    push(kvbuf.at[mine], kvb_send.at[0], kv_recv.at[12 + x], sibling)
    for k in range(1, ZS):
        slot = zk[k] * 2 + c
        arrive(qlbuf.at[slot], ql_recv.at[slot])
        push(qlbuf.at[slot], ql_send.at[0], ql_recv.at[slot], sibling)

    loads[6].wait()
    wbuf[mine, :, :] = jnp.concatenate([outp_in[...], jnp.zeros((2, OUT_K), BF16)], axis=0)

    from_left, from_right, from_far = xl * 2 + c, xr * 2 + c, xo * 2 + c
    arrive(pair(from_left, 0), kv_recv.at[4 + xl * 2])
    push(pair(from_left, 0), kvp_send.at[0], kv_recv.at[4 + xl * 2], right)
    push(pair(from_left, 0), kvp_send.at[0], kv_recv.at[16], index(xr, z, 1 - c))
    arrive(pair(from_right, 1), kv_recv.at[4 + xr * 2 + 1])
    push(pair(from_right, 1), kvp_send.at[0], kv_recv.at[4 + xr * 2 + 1], left)
    push(pair(from_right, 1), kvp_send.at[0], kv_recv.at[17], index(xl, z, 1 - c))
    arrive(pair(from_left, 1), kv_recv.at[4 + xl * 2 + 1])
    push(kvbuf.at[from_left], kvb_send.at[0], kv_recv.at[12 + xl], sibling)
    arrive(pair(from_right, 0), kv_recv.at[4 + xr * 2])
    push(kvbuf.at[from_right], kvb_send.at[0], kv_recv.at[12 + xr], sibling)

    for target in (right, left, sibling):
        push(wbuf.at[mine], w_send.at[0], w_recv.at[mine, 0], target)

    for zz in range(ZS):
        slot = zz * 2 + 1 - c
        arrive(qlbuf.at[slot], ql_recv.at[slot])
    ql_rows = qlbuf[...].reshape(8 * SLOT, QC)

    def partial_q(slots):
        width = len(slots) * SLOT
        block_of = (lax.broadcasted_iota(jnp.int32, (8 * SLOT, width), 0) // 4) % 4
        total = jnp.zeros((8 * SLOT, width), F32)
        for j in range(4):
            columns = jnp.concatenate(
                [qbuf[slot, :, j * QC: (j + 1) * QC] for slot in slots], axis=0
            )
            total = jnp.where(block_of == j, dot_nt(ql_rows, columns), total)
        return total

    near = partial_q([x, xr, xl])
    arrive(qbuf.at[xo, :, pl.ds(0, QR // 2)], q_recv.at[xo, 0])
    arrive(qbuf.at[xo, :, pl.ds(QR // 2, QR // 2)], q_recv.at[xo, 1])
    partial = jnp.concatenate([near, partial_q([xo])], axis=1)
    partial = partial.reshape(8, SLOT, XS * SLOT)
    partial = partial[:, 0:8] + partial[:, 8:16]
    partial = jnp.concatenate([partial, partial], axis=2)
    lane_of = lax.broadcasted_iota(jnp.int32, (8, 8, 128), 2)
    qsend[...] = jnp.where(lane_of // 64 == c, partial, 0.0)
    for k in range(1, ZS):
        for cc in (c, 1 - c):
            slot = zk[k] * 2 + cc
            remote(
                qsend.at[slot], qrecv.at[own], qx_send.at[0], qx_recv.at[own],
                {"batch": index(x, zk[k], cc)},
            ).start()
    remote(
        qsend.at[z * 2 + 1 - c], qrecv.at[own], qx_send.at[0], qx_recv.at[own], {"batch": sibling}
    ).start()
    qrecv[own, :, :] = qsend[own]

    row8 = lax.broadcasted_iota(jnp.int32, (8, 1), 0)
    row_of = row8 % 4
    low = row8 < 4
    for load in loads[3:6]:
        load.wait()
    length = jnp.zeros((8, 1), jnp.int32)
    for r in range(4):
        length = jnp.where(row_of == r, len_in[r], length)

    lane64 = lax.broadcasted_iota(jnp.int32, (8, ROPE), 1)
    inverse = jnp.exp((lane64 % (ROPE // 2)).astype(F32) * (-2.0 * math.log(50000.0) / ROPE))
    angles = length.astype(F32) * inverse
    cosine = jnp.cos(angles)
    sine = jnp.sin(angles)
    sine = jnp.where(lane64 < ROPE // 2, -sine, sine)

    def twice(values):
        return jnp.concatenate([values, values], axis=0)

    nr8 = twice(nr_in[...].astype(F32))
    nr_swapped = jnp.concatenate([nr8[:, ROPE // 2:], nr8[:, : ROPE // 2]], axis=1)
    key_new = (nr8 * cosine + nr_swapped * sine).astype(BF16).astype(F32)
    nl8 = twice(nl_in[...].astype(F32))

    for k in range(1, ZS):
        for cc in (c, 1 - c):
            slot = zk[k] * 2 + cc
            arrive(qrecv.at[slot], qx_recv.at[slot])
    arrive(qrecv.at[z * 2 + 1 - c], qx_recv.at[z * 2 + 1 - c])
    pieces = []
    for zz in range(ZS):
        piece = qrecv[2 * zz] + qrecv[2 * zz + 1]
        pieces.append(piece + pltpu.roll(piece, 4, 0))
    q_all = jnp.concatenate(pieces, axis=1)
    lane_q = lax.broadcasted_iota(jnp.int32, (8, 512), 1)
    turn = lane_q % 64 // 16
    x_of = (x + turn + turn // 2 - 2 * (turn // 3)) % 4
    q_all = jnp.where((x_of < 2) == low, q_all, 0.0)
    q_hi = q_all.astype(BF16)
    q_lo = q_all - q_hi.astype(F32)
    selection = sel[...]
    q_both = jnp.concatenate([q_hi.astype(F32), q_lo], axis=0).astype(BF16)
    q_both = dot_nn(q_both, selection)
    q_sel = q_both[0:8] + q_both[8:16]
    q_nope = q_sel[:, 0: 2 * NOPE].astype(BF16)
    query_rope = (
        q_sel[:, 2 * NOPE: 2 * NOPE + ROPE] * cosine + q_sel[:, 2 * NOPE + ROPE:] * sine
    ).astype(BF16)

    loads[8].wait()
    rope_scores = jnp.zeros((8, CACHE), F32)
    for r in range(4):
        rope_scores = jnp.where(row_of == r, dot_nn(query_rope, rope[r]), rope_scores)

    def blocks_for(parity):
        @pl.when(x % 2 == parity)
        def _():
            arrive(kvbuf.at[x * 2 + 1 - c], kv_recv.at[12 + x])
            for half in range(2):
                arrive(pair(from_far, half), kv_recv.at[4 + xo * 2 + half])
                arrive(pair(xo * 2 + 1 - c, half), kv_recv.at[16 + half])

        @pl.when(x % 2 != parity)
        def _():
            for xx in (xl, xr):
                arrive(kvbuf.at[xx * 2 + 1 - c], kv_recv.at[12 + xx])

    blocks_for(0)

    def kv_rows(xx):
        return jnp.concatenate(
            [kvbuf[xx * 2 + cc, zz] for zz in range(ZS) for cc in range(2)], axis=0
        )

    query_abs = (
        dot_nn(q_nope[:, :NOPE], kv_rows(0)) + dot_nn(q_nope[:, NOPE:], kv_rows(2))
    ).astype(BF16)

    loads[7].wait()
    scale = (NOPE + ROPE) ** (-0.5)
    scores = jnp.zeros((8, CACHE), F32)
    for r in range(4):
        scores = jnp.where(row_of == r, dot_nt(query_abs, lat[r]), scores)
    scores = scores + rope_scores
    score_new = scale * (
        jnp.sum(query_abs.astype(F32) * nl8, axis=1, keepdims=True)
        + jnp.sum(query_rope.astype(F32) * key_new, axis=1, keepdims=True)
    )
    position = lax.broadcasted_iota(jnp.int32, (8, CACHE), 1)
    scores = jnp.where(position < length, scores * scale, -1e30)
    top = jnp.maximum(jnp.max(scores, axis=1, keepdims=True), score_new)
    old = jnp.exp(scores - top)
    new = jnp.exp(score_new - top)
    denom = jnp.sum(old, axis=1, keepdims=True) + new
    probs = (old / denom).astype(BF16)
    prob_new = (new / denom).astype(BF16).astype(F32)
    context = jnp.zeros((8, KVR), F32)
    for r in range(4):
        context = jnp.where(row_of == r, dot_nn(probs, lat[r]), context)
    context = (context + prob_new * nl8).astype(BF16)
    blocks_for(1)
    value = jnp.where(low, dot_nt(context, kv_rows(1)), dot_nt(context, kv_rows(3)))
    z_of_8 = up * ZS + z
    first_at = z_of_8 * (1 - c) + y * c
    second_at = y * (1 - c) + z_of_8 * c

    def ring_peer(steps_z, steps_y):
        to_z, to_y = (z_of_8 + steps_z) % 8, (y + steps_y) % YS
        return {"heads": to_z // ZS * YS + to_y, "batch": index(x, to_z % ZS, c)}

    vx[first_at, :, :] = value.astype(BF16).astype(F32)
    for i in (4, 3, 5, 2, 6, 1, 7):
        remote(
            vx.at[first_at], vx.at[first_at], vx_send.at[0], vx_recv.at[first_at],
            ring_peer(i * (1 - c), i * c),
        ).start()

    arrive(wbuf.at[from_left], w_recv.at[from_left, 0])
    push(
        wbuf.at[from_left, :, pl.ds(0, OUT_K // 2)], w_send.at[0], w_recv.at[from_left, 0], right
    )
    push(wbuf.at[from_left], w_send.at[0], w_recv.at[from_left, 0], sibling)
    arrive(wbuf.at[from_right], w_recv.at[from_right, 0])
    push(
        wbuf.at[from_right, :, pl.ds(OUT_K // 2, OUT_K // 2)], w_send.at[0],
        w_recv.at[from_right, 1], left,
    )
    push(wbuf.at[from_right], w_send.at[0], w_recv.at[from_right, 0], sibling)

    for i in (1, 7, 2, 6, 3, 5, 4):
        slot = (first_at + i) % 8
        arrive(vx.at[slot], vx_recv.at[slot])
    vh[second_at, :, :] = vx[...].reshape(64, 128).astype(BF16)

    for i in (4, 3, 5, 2, 6, 1, 7):
        remote(
            vh.at[second_at], vh.at[second_at], vh_send.at[0], vh_recv.at[second_at],
            ring_peer(i * c, i * (1 - c)),
        ).start()

    arrive(wbuf.at[from_far, :, pl.ds(0, OUT_K // 2)], w_recv.at[from_far, 0])
    arrive(wbuf.at[from_far, :, pl.ds(OUT_K // 2, OUT_K // 2)], w_recv.at[from_far, 1])
    push(wbuf.at[from_far], w_send.at[0], w_recv.at[from_far, 0], sibling)

    @pl.loop(0, 32)
    def _(t):
        start = (((t // 2) % 4) * 8 + (t // 8) * 2 + t % 2) * 14
        col = lax.broadcasted_iota(jnp.int32, (SLOT, 448), 1) - start
        row = lax.broadcasted_iota(jnp.int32, (SLOT, 448), 0)
        block = jnp.where((col == row) & (row < 14), 1.0, 0.0).astype(BF16)
        sel_out[pl.ds(pl.multiple_of(t * SLOT, SLOT), SLOT), :] = block

    for xx in (x, xl, xr, xo):
        block = xx * 2 + 1 - c
        arrive(wbuf.at[block], w_recv.at[block, 0])

    row32 = lax.broadcasted_iota(jnp.int32, (32, 128), 0)
    is_low = (row32 % 8) < 4
    zero = jnp.zeros((32, 128), BF16)

    def by_head(block):
        return jnp.concatenate(
            [jnp.where(is_low, block, zero), jnp.where(is_low, zero, block)], axis=1
        )

    def out_rows(half, at_y):
        columns = pl.ds(pl.multiple_of((half * YS + at_y) * 256, 256), 256)
        return wbuf[:, :, columns].reshape(8 * SLOT, 256)

    @pl.when(c == 0)
    def _():
        y_all = jnp.zeros((32, 128), F32)
        for i in (0, 1, 7, 2, 6, 3, 5, 4):
            other = (y + i) % YS
            if i:
                arrive(vh.at[other], vh_recv.at[other])
            for half in range(2):
                block = vh[other, half * 32: half * 32 + 32]
                y_all = y_all + dot_nt(by_head(block), out_rows(half, other))
        ysend[...] = y_all.reshape(ZS, 8, 128)

    @pl.when(c == 1)
    def _():
        for i in (1, 7, 2, 6, 3, 5, 4):
            other = (z_of_8 + i) % 8
            arrive(vh.at[other], vh_recv.at[other])
        y_all = jnp.zeros((32, 128), F32)
        for half in range(2):
            blocks = vh[half * ZS: half * ZS + ZS].astype(F32).reshape(ZS, YS, 8, 128)
            for at_y in range(YS):
                block = blocks[:, at_y].reshape(32, 128).astype(BF16)
                y_all = y_all + dot_nt(by_head(block), out_rows(half, at_y))
        ysend[...] = y_all.reshape(ZS, 8, 128)

    for k in range(1, ZS):
        remote(
            ysend.at[zk[k]], yrecv.at[z], y_send.at[0], y_recv.at[z],
            {"batch": index(x, zk[k], c)},
        ).start()
    yrecv[z, :, :] = ysend[z]
    for k in range(1, ZS):
        arrive(yrecv.at[zk[k]], y_recv.at[zk[k]])
    pieces = []
    for zz in range(ZS):
        piece = yrecv[zz]
        pieces.append(piece + pltpu.roll(piece, 4, 0))
    summed = jnp.concatenate(pieces, axis=1).astype(BF16)
    y_ref[...] = dot_nn(summed, sel_out[...])[0:4]

    for ref, sem in (
        (qbuf.at[0:3], q_send), (kvbuf.at[0, 0:3], kvz_send), (kvbuf.at[0:4], kvp_send),
        (kvbuf.at[0:3], kvb_send),
        (qlbuf.at[0:7], ql_send), (qsend.at[0:7], qx_send), (wbuf.at[0:7], w_send),
        (vx.at[0:7], vx_send), (vh.at[0:7], vh_send), (ysend.at[0:3], y_send),
    ):
        arrive(ref, sem.at[0])


def shards(
    q_latent, new_latent, new_rope, latent_cache, rope_cache, lengths, q_up, kv_up, out_proj
):
    hbm = pl.BlockSpec(memory_space=pltpu.HBM)
    dma = pltpu.SemaphoreType.DMA
    return pl.pallas_call(
        kernel,
        out_shape=jax.ShapeDtypeStruct((4, 448), F32),
        in_specs=[hbm] * 9,
        out_specs=pl.BlockSpec(memory_space=pltpu.VMEM),
        scratch_shapes=[
            pltpu.VMEM((4, QR), BF16),
            pltpu.VMEM((4, KVR), BF16),
            pltpu.VMEM((4, ROPE), BF16),
            pltpu.SMEM((4,), jnp.int32),
            pltpu.VMEM((QROWS, QR), BF16),
            pltpu.VMEM((14, OUT_K), BF16),
            pltpu.VMEM((4, CACHE, KVR), BF16),
            pltpu.VMEM((4, ROPE, CACHE), BF16),
            pltpu.VMEM((XS, SLOT, QR), BF16),
            pltpu.VMEM((8, SLOT, QC), BF16),
            pltpu.VMEM((8, 8, 128), F32),
            pltpu.VMEM((8, 8, 128), F32),
            pltpu.VMEM((8, ZS, SLOT, KVR), BF16),
            pltpu.VMEM((8, SLOT, OUT_K), BF16),
            pltpu.VMEM((512, 2 * NOPE + 2 * ROPE), BF16),
            pltpu.VMEM((512, 448), BF16),
            pltpu.VMEM((2 * ZS, 8, 128), F32),
            pltpu.VMEM((YS, 64, 128), BF16),
            pltpu.VMEM((ZS, 8, 128), F32),
            pltpu.VMEM((ZS, 8, 128), F32),
            dma((9,)),
            dma((1,)), dma((XS, 2)),
            dma((1,)), dma((8,)),
            dma((1,)), dma((8,)),
            dma((1,)), dma((1,)), dma((1,)), dma((18,)),
            dma((1,)), dma((8, 2)),
            dma((1,)), dma((2 * ZS,)),
            dma((1,)), dma((YS,)),
            dma((1,)), dma((ZS,)),
        ],
        compiler_params=pltpu.CompilerParams(
            collective_id=0, has_side_effects=True, vmem_limit_bytes=60 * 2**20
        ),
        cost_estimate=pl.CostEstimate(
            flops=4 * 10**8, bytes_accessed=5 * 10**6, transcendentals=10**4
        ),
    )(
        q_latent, new_latent, new_rope, latent_cache, jnp.swapaxes(rope_cache, 1, 2), lengths,
        q_up, kv_up, out_proj,
    ).astype(BF16)


def solution(mesh):
    placed = (
        P("batch", None),
        P("batch", None),
        P("batch", None),
        P("batch", None, None),
        P("batch", None, None),
        P("batch"),
        P(("heads", "batch"), None),
        P(("heads", "batch"), None),
        P(("heads", "batch"), None),
    )
    return jax.shard_map(
        shards, mesh=mesh, in_specs=placed, out_specs=P("batch", "heads"), check_vma=False
    )
```

```python
import functools
import math

import jax
import jax.numpy as jnp
from jax import lax
from jax.experimental import pallas as pl
from jax.experimental.pallas import tpu as pltpu
from jax.sharding import PartitionSpec as P

QR = 1536
KVR = 512
NOPE = 128
ROPE = 64
CACHE = 1024
QROWS = 12
SLOT = 16
XS, ZS = 4, 4
YS = 8
QC = QR // 4
OUT_K = 4096
F32 = jnp.float32
BF16 = jnp.bfloat16
NT = (((1,), (1,)), ((), ()))


def dot_nt(a, b):
    return lax.dot_general(a, b, NT, preferred_element_type=F32)


def dot_nn(a, b):
    return jnp.dot(a, b, preferred_element_type=F32)


def kernel(
    ql_hbm, nl_hbm, nr_hbm, lat_hbm, rope_hbm, len_hbm, qup_hbm, kvup_hbm, outp_hbm, y_ref,
    ql_in, nl_in, nr_in, len_in, qup_in, outp_in, lat, rope,
    qbuf, qlbuf, qsend, qrecv, kvbuf, wbuf, sel, sel_out, vx, vh, ysend, yrecv,
    in_sem, q_send, q_recv, ql_send, ql_recv, qx_send, qx_recv, kvz_send, kvp_send, kvb_send, kv_recv,
    w_send, w_recv, vx_send, vx_recv, vh_send, vh_recv, y_send, y_recv,
):
    h = lax.axis_index("heads")
    b = lax.axis_index("batch")
    x, z, c = b // 8, (b // 2) % 4, b % 2
    y, up = h % YS, h // YS

    def index(xx, zz, cc):
        return xx * 8 + zz * 2 + cc

    zk = [z, z + 1 - 2 * (z % 2), (z + 2) % 4, 3 - z]
    xr, xl, xo = (x + 1) % 4, (x + 3) % 4, (x + 2) % 4
    right, left, sibling = index(xr, z, c), index(xl, z, c), index(x, z, 1 - c)
    mine, theirs = x * 2 + c, x * 2 + 1 - c
    own = z * 2 + c

    loads = [
        pltpu.make_async_copy(source, target, in_sem.at[i])
        for i, (source, target) in enumerate(
            [
                (qup_hbm, qup_in), (ql_hbm, ql_in), (kvup_hbm, kvbuf.at[mine, z]),
                (nl_hbm, nl_in), (nr_hbm, nr_in), (len_hbm, len_in), (outp_hbm, outp_in),
                (lat_hbm, lat), (rope_hbm, rope),
            ]
        )
    ]
    barrier = pltpu.get_barrier_semaphore()

    def greet(target):
        pl.semaphore_signal(barrier, inc=1, device_id={"batch": target})

    across = (1 - up) * YS + y
    for k in range(ZS):
        pl.semaphore_signal(
            barrier, inc=1, device_id={"heads": across, "batch": index(x, zk[k], c)}
        )

    @pl.loop(1, YS)
    def _(i):
        pl.semaphore_signal(barrier, inc=1, device_id={"heads": up * YS + (y + i) % YS})

    for k in range(1, ZS):
        greet(index(x, zk[k], c))
        greet(index(x, zk[k], 1 - c))
    for cc in (c, 1 - c):
        greet(index(xr, z, cc))
        greet(index(xl, z, cc))
    greet(sibling)

    for i in (2, 0, 1, 3, 4, 5, 6, 7, 8):
        loads[i].start()
    loads[2].wait()
    pl.semaphore_wait(barrier, ZS + YS - 1 + 6 + 4 + 1)

    def remote(source, target, send_sem, recv_sem, device):
        return pltpu.make_async_remote_copy(
            src_ref=source, dst_ref=target, send_sem=send_sem, recv_sem=recv_sem,
            device_id=device,
        )

    def push(ref, send_sem, recv_sem, target):
        remote(ref, ref, send_sem, recv_sem, {"batch": target}).start()

    def arrive(ref, recv_sem):
        pltpu.make_async_copy(ref, ref, recv_sem).wait()

    for k in (3, 2, 1):
        push(kvbuf.at[mine, z], kvz_send.at[0], kv_recv.at[z], index(x, zk[k], c))

    loads[0].wait()
    qbuf[x, :, :] = jnp.concatenate([qup_in[...], jnp.zeros((SLOT - QROWS, QR), BF16)], axis=0)
    for target in (right, left):
        push(qbuf.at[x], q_send.at[0], q_recv.at[x, 0], target)
    loads[1].wait()
    ql_own = ql_in[...].astype(F32)
    qlbuf[own, :, :] = jnp.concatenate(
        [ql_own[:, j * QC: (j + 1) * QC] for j in range(4)], axis=0
    ).astype(BF16)
    for k in range(1, ZS):
        push(qlbuf.at[own], ql_send.at[0], ql_recv.at[own], index(x, zk[k], c))
    push(qlbuf.at[own], ql_send.at[0], ql_recv.at[own], sibling)

    @pl.loop(0, 32)
    def _(t):
        x_t = (x + t % 4 + (t % 4) // 2 - 2 * ((t % 4) // 3)) % 4
        first_row = QROWS * ((x_t % 2) * 8 + (t // 8) * 2 + (t // 4) % 2)
        shape = (SLOT, 2 * NOPE + 2 * ROPE)
        within = lax.broadcasted_iota(jnp.int32, shape, 0)
        col = lax.broadcasted_iota(jnp.int32, shape, 1)
        row = within + first_row
        nope = (row < NOPE) & (col == row + (x_t // 2) * NOPE)
        rotary = row - NOPE
        swapped = (rotary + ROPE // 2) % ROPE
        rope_at = (row >= NOPE) & (
            (col == 2 * NOPE + rotary) | (col == 2 * NOPE + ROPE + swapped)
        )
        block = jnp.where((within < QROWS) & (nope | rope_at), 1.0, 0.0).astype(BF16)
        sel[pl.ds(pl.multiple_of(t * SLOT, SLOT), SLOT), :] = block

    arrive(qbuf.at[xl], q_recv.at[xl, 0])
    push(qbuf.at[xl, :, pl.ds(0, QR // 2)], q_send.at[0], q_recv.at[xl, 0], right)
    arrive(qbuf.at[xr], q_recv.at[xr, 0])
    push(qbuf.at[xr, :, pl.ds(QR // 2, QR // 2)], q_send.at[0], q_recv.at[xr, 1], left)

    def pair(block, half):
        return kvbuf.at[block, pl.ds(2 * half, 2)]

    def kv_pair_out(half):
        for target in (right, left):
            push(pair(mine, half), kvp_send.at[0], kv_recv.at[4 + x * 2 + half], target)

    arrive(kvbuf.at[mine, zk[1]], kv_recv.at[zk[1]])
    kv_pair_out(z // 2)
    for k in range(2, ZS):
        arrive(kvbuf.at[mine, zk[k]], kv_recv.at[zk[k]])
    kv_pair_out(1 - z // 2)
    push(kvbuf.at[mine], kvb_send.at[0], kv_recv.at[12 + x], sibling)
    for k in range(1, ZS):
        slot = zk[k] * 2 + c
        arrive(qlbuf.at[slot], ql_recv.at[slot])
        push(qlbuf.at[slot], ql_send.at[0], ql_recv.at[slot], sibling)

    loads[6].wait()
    wbuf[mine, :, :] = jnp.concatenate([outp_in[...], jnp.zeros((2, OUT_K), BF16)], axis=0)

    from_left, from_right, from_far = xl * 2 + c, xr * 2 + c, xo * 2 + c
    arrive(pair(from_left, 0), kv_recv.at[4 + xl * 2])
    push(pair(from_left, 0), kvp_send.at[0], kv_recv.at[4 + xl * 2], right)
    push(pair(from_left, 0), kvp_send.at[0], kv_recv.at[16], index(xr, z, 1 - c))
    arrive(pair(from_right, 1), kv_recv.at[4 + xr * 2 + 1])
    push(pair(from_right, 1), kvp_send.at[0], kv_recv.at[4 + xr * 2 + 1], left)
    push(pair(from_right, 1), kvp_send.at[0], kv_recv.at[17], index(xl, z, 1 - c))
    arrive(pair(from_left, 1), kv_recv.at[4 + xl * 2 + 1])
    push(kvbuf.at[from_left], kvb_send.at[0], kv_recv.at[12 + xl], sibling)
    arrive(pair(from_right, 0), kv_recv.at[4 + xr * 2])
    push(kvbuf.at[from_right], kvb_send.at[0], kv_recv.at[12 + xr], sibling)

    for target in (right, left, sibling):
        push(wbuf.at[mine], w_send.at[0], w_recv.at[mine, 0], target)

    for zz in range(ZS):
        slot = zz * 2 + 1 - c
        arrive(qlbuf.at[slot], ql_recv.at[slot])
    ql_rows = qlbuf[...].reshape(8 * SLOT, QC)

    def partial_q(slots):
        width = len(slots) * SLOT
        block_of = (lax.broadcasted_iota(jnp.int32, (8 * SLOT, width), 0) // 4) % 4
        total = jnp.zeros((8 * SLOT, width), F32)
        for j in range(4):
            columns = jnp.concatenate(
                [qbuf[slot, :, j * QC: (j + 1) * QC] for slot in slots], axis=0
            )
            total = jnp.where(block_of == j, dot_nt(ql_rows, columns), total)
        return total

    near = partial_q([x, xr, xl])
    arrive(qbuf.at[xo, :, pl.ds(0, QR // 2)], q_recv.at[xo, 0])
    arrive(qbuf.at[xo, :, pl.ds(QR // 2, QR // 2)], q_recv.at[xo, 1])
    partial = jnp.concatenate([near, partial_q([xo])], axis=1)
    partial = partial.reshape(8, SLOT, XS * SLOT)
    partial = partial[:, 0:8] + partial[:, 8:16]
    partial = jnp.concatenate([partial, partial], axis=2)
    lane_of = lax.broadcasted_iota(jnp.int32, (8, 8, 128), 2)
    qsend[...] = jnp.where(lane_of // 64 == c, partial, 0.0)
    for k in (3, 2, 1):
        for cc in (c, 1 - c):
            slot = zk[k] * 2 + cc
            remote(
                qsend.at[slot], qrecv.at[own], qx_send.at[0], qx_recv.at[own],
                {"batch": index(x, zk[k], cc)},
            ).start()
    remote(
        qsend.at[z * 2 + 1 - c], qrecv.at[own], qx_send.at[0], qx_recv.at[own], {"batch": sibling}
    ).start()
    qrecv[own, :, :] = qsend[own]

    row8 = lax.broadcasted_iota(jnp.int32, (8, 1), 0)
    row_of = row8 % 4
    low = row8 < 4
    for load in loads[3:6]:
        load.wait()
    length = jnp.zeros((8, 1), jnp.int32)
    for r in range(4):
        length = jnp.where(row_of == r, len_in[r], length)

    lane64 = lax.broadcasted_iota(jnp.int32, (8, ROPE), 1)
    inverse = jnp.exp((lane64 % (ROPE // 2)).astype(F32) * (-2.0 * math.log(50000.0) / ROPE))
    angles = length.astype(F32) * inverse
    cosine = jnp.cos(angles)
    sine = jnp.sin(angles)
    sine = jnp.where(lane64 < ROPE // 2, -sine, sine)

    def twice(values):
        return jnp.concatenate([values, values], axis=0)

    nr8 = twice(nr_in[...].astype(F32))
    nr_swapped = jnp.concatenate([nr8[:, ROPE // 2:], nr8[:, : ROPE // 2]], axis=1)
    key_new = (nr8 * cosine + nr_swapped * sine).astype(BF16).astype(F32)
    nl8 = twice(nl_in[...].astype(F32))

    for k in range(1, ZS):
        for cc in (c, 1 - c):
            slot = zk[k] * 2 + cc
            arrive(qrecv.at[slot], qx_recv.at[slot])
    arrive(qrecv.at[z * 2 + 1 - c], qx_recv.at[z * 2 + 1 - c])
    pieces = []
    for zz in range(ZS):
        piece = qrecv[2 * zz] + qrecv[2 * zz + 1]
        pieces.append(piece + pltpu.roll(piece, 4, 0))
    q_all = jnp.concatenate(pieces, axis=1)
    lane_q = lax.broadcasted_iota(jnp.int32, (8, 512), 1)
    turn = lane_q % 64 // 16
    x_of = (x + turn + turn // 2 - 2 * (turn // 3)) % 4
    q_all = jnp.where((x_of < 2) == low, q_all, 0.0)
    q_hi = q_all.astype(BF16)
    q_lo = q_all - q_hi.astype(F32)
    selection = sel[...]
    q_both = jnp.concatenate([q_hi.astype(F32), q_lo], axis=0).astype(BF16)
    q_both = dot_nn(q_both, selection)
    q_sel = q_both[0:8] + q_both[8:16]
    q_nope = q_sel[:, 0: 2 * NOPE].astype(BF16)
    query_rope = (
        q_sel[:, 2 * NOPE: 2 * NOPE + ROPE] * cosine + q_sel[:, 2 * NOPE + ROPE:] * sine
    ).astype(BF16)

    loads[8].wait()
    rope_scores = jnp.zeros((8, CACHE), F32)
    for r in range(4):
        rope_scores = jnp.where(row_of == r, dot_nn(query_rope, rope[r]), rope_scores)

    def blocks_for(parity):
        @pl.when(x % 2 == parity)
        def _():
            arrive(kvbuf.at[x * 2 + 1 - c], kv_recv.at[12 + x])
            for half in range(2):
                arrive(pair(from_far, half), kv_recv.at[4 + xo * 2 + half])
                arrive(pair(xo * 2 + 1 - c, half), kv_recv.at[16 + half])

        @pl.when(x % 2 != parity)
        def _():
            for xx in (xl, xr):
                arrive(kvbuf.at[xx * 2 + 1 - c], kv_recv.at[12 + xx])

    blocks_for(0)

    def kv_rows(xx):
        return jnp.concatenate(
            [kvbuf[xx * 2 + cc, zz] for zz in range(ZS) for cc in range(2)], axis=0
        )

    query_abs = (
        dot_nn(q_nope[:, :NOPE], kv_rows(0)) + dot_nn(q_nope[:, NOPE:], kv_rows(2))
    ).astype(BF16)

    loads[7].wait()
    scale = (NOPE + ROPE) ** (-0.5)
    scores = jnp.zeros((8, CACHE), F32)
    for r in range(4):
        scores = jnp.where(row_of == r, dot_nt(query_abs, lat[r]), scores)
    scores = scores + rope_scores
    score_new = scale * (
        jnp.sum(query_abs.astype(F32) * nl8, axis=1, keepdims=True)
        + jnp.sum(query_rope.astype(F32) * key_new, axis=1, keepdims=True)
    )
    position = lax.broadcasted_iota(jnp.int32, (8, CACHE), 1)
    scores = jnp.where(position < length, scores * scale, -1e30)
    top = jnp.maximum(jnp.max(scores, axis=1, keepdims=True), score_new)
    old = jnp.exp(scores - top)
    new = jnp.exp(score_new - top)
    denom = jnp.sum(old, axis=1, keepdims=True) + new
    probs = (old / denom).astype(BF16)
    prob_new = (new / denom).astype(BF16).astype(F32)
    context = jnp.zeros((8, KVR), F32)
    for r in range(4):
        context = jnp.where(row_of == r, dot_nn(probs, lat[r]), context)
    context = (context + prob_new * nl8).astype(BF16)
    blocks_for(1)
    value = jnp.where(low, dot_nt(context, kv_rows(1)), dot_nt(context, kv_rows(3)))
    z_of_8 = up * ZS + z
    first_at = z_of_8 * (1 - c) + y * c
    second_at = y * (1 - c) + z_of_8 * c

    def ring_peer(steps_z, steps_y):
        to_z, to_y = (z_of_8 + steps_z) % 8, (y + steps_y) % YS
        return {"heads": to_z // ZS * YS + to_y, "batch": index(x, to_z % ZS, c)}

    vx[first_at, :, :] = value.astype(BF16).astype(F32)
    for i in (4, 3, 5, 2, 6, 1, 7):
        remote(
            vx.at[first_at], vx.at[first_at], vx_send.at[0], vx_recv.at[first_at],
            ring_peer(i * (1 - c), i * c),
        ).start()

    arrive(wbuf.at[from_left], w_recv.at[from_left, 0])
    push(
        wbuf.at[from_left, :, pl.ds(0, OUT_K // 2)], w_send.at[0], w_recv.at[from_left, 0], right
    )
    push(wbuf.at[from_left], w_send.at[0], w_recv.at[from_left, 0], sibling)
    arrive(wbuf.at[from_right], w_recv.at[from_right, 0])
    push(
        wbuf.at[from_right, :, pl.ds(OUT_K // 2, OUT_K // 2)], w_send.at[0],
        w_recv.at[from_right, 1], left,
    )
    push(wbuf.at[from_right], w_send.at[0], w_recv.at[from_right, 0], sibling)

    for i in (1, 7, 2, 6, 3, 5, 4):
        slot = (first_at + i) % 8
        arrive(vx.at[slot], vx_recv.at[slot])
    vh[second_at, :, :] = vx[...].reshape(64, 128).astype(BF16)

    for i in (4, 3, 5, 2, 6, 1, 7):
        remote(
            vh.at[second_at], vh.at[second_at], vh_send.at[0], vh_recv.at[second_at],
            ring_peer(i * c, i * (1 - c)),
        ).start()

    arrive(wbuf.at[from_far, :, pl.ds(0, OUT_K // 2)], w_recv.at[from_far, 0])
    arrive(wbuf.at[from_far, :, pl.ds(OUT_K // 2, OUT_K // 2)], w_recv.at[from_far, 1])
    push(wbuf.at[from_far], w_send.at[0], w_recv.at[from_far, 0], sibling)

    @pl.loop(0, 32)
    def _(t):
        start = (((t // 2) % 4) * 8 + (t // 8) * 2 + t % 2) * 14
        col = lax.broadcasted_iota(jnp.int32, (SLOT, 448), 1) - start
        row = lax.broadcasted_iota(jnp.int32, (SLOT, 448), 0)
        block = jnp.where((col == row) & (row < 14), 1.0, 0.0).astype(BF16)
        sel_out[pl.ds(pl.multiple_of(t * SLOT, SLOT), SLOT), :] = block

    for xx in (x, xl, xr, xo):
        block = xx * 2 + 1 - c
        arrive(wbuf.at[block], w_recv.at[block, 0])

    row32 = lax.broadcasted_iota(jnp.int32, (32, 128), 0)
    is_low = (row32 % 8) < 4
    zero = jnp.zeros((32, 128), BF16)

    def by_head(block):
        return jnp.concatenate(
            [jnp.where(is_low, block, zero), jnp.where(is_low, zero, block)], axis=1
        )

    def out_rows(half, at_y):
        columns = pl.ds(pl.multiple_of((half * YS + at_y) * 256, 256), 256)
        return wbuf[:, :, columns].reshape(8 * SLOT, 256)

    @pl.when(c == 0)
    def _():
        y_all = jnp.zeros((32, 128), F32)
        for i in (0, 1, 7, 2, 6, 3, 5, 4):
            other = (y + i) % YS
            if i:
                arrive(vh.at[other], vh_recv.at[other])
            for half in range(2):
                block = vh[other, half * 32: half * 32 + 32]
                y_all = y_all + dot_nt(by_head(block), out_rows(half, other))
        ysend[...] = y_all.reshape(ZS, 8, 128)

    @pl.when(c == 1)
    def _():
        for i in (1, 7, 2, 6, 3, 5, 4):
            other = (z_of_8 + i) % 8
            arrive(vh.at[other], vh_recv.at[other])
        y_all = jnp.zeros((32, 128), F32)
        for half in range(2):
            blocks = vh[half * ZS: half * ZS + ZS].astype(F32).reshape(ZS, YS, 8, 128)
            for at_y in range(YS):
                block = blocks[:, at_y].reshape(32, 128).astype(BF16)
                y_all = y_all + dot_nt(by_head(block), out_rows(half, at_y))
        ysend[...] = y_all.reshape(ZS, 8, 128)

    for k in (3, 2, 1):
        remote(
            ysend.at[zk[k]], yrecv.at[z], y_send.at[0], y_recv.at[z],
            {"batch": index(x, zk[k], c)},
        ).start()
    yrecv[z, :, :] = ysend[z]
    for k in range(1, ZS):
        arrive(yrecv.at[zk[k]], y_recv.at[zk[k]])
    pieces = []
    for zz in range(ZS):
        piece = yrecv[zz]
        pieces.append(piece + pltpu.roll(piece, 4, 0))
    summed = jnp.concatenate(pieces, axis=1).astype(BF16)
    y_ref[...] = dot_nn(summed, sel_out[...])[0:4]

    for ref, sem in (
        (qbuf.at[0:3], q_send), (kvbuf.at[0, 0:3], kvz_send), (kvbuf.at[0:4], kvp_send),
        (kvbuf.at[0:3], kvb_send),
        (qlbuf.at[0:7], ql_send), (qsend.at[0:7], qx_send), (wbuf.at[0:7], w_send),
        (vx.at[0:7], vx_send), (vh.at[0:7], vh_send), (ysend.at[0:3], y_send),
    ):
        arrive(ref, sem.at[0])


def shards(
    q_latent, new_latent, new_rope, latent_cache, rope_cache, lengths, q_up, kv_up, out_proj
):
    hbm = pl.BlockSpec(memory_space=pltpu.HBM)
    dma = pltpu.SemaphoreType.DMA
    return pl.pallas_call(
        kernel,
        out_shape=jax.ShapeDtypeStruct((4, 448), F32),
        in_specs=[hbm] * 9,
        out_specs=pl.BlockSpec(memory_space=pltpu.VMEM),
        scratch_shapes=[
            pltpu.VMEM((4, QR), BF16),
            pltpu.VMEM((4, KVR), BF16),
            pltpu.VMEM((4, ROPE), BF16),
            pltpu.SMEM((4,), jnp.int32),
            pltpu.VMEM((QROWS, QR), BF16),
            pltpu.VMEM((14, OUT_K), BF16),
            pltpu.VMEM((4, CACHE, KVR), BF16),
            pltpu.VMEM((4, ROPE, CACHE), BF16),
            pltpu.VMEM((XS, SLOT, QR), BF16),
            pltpu.VMEM((8, SLOT, QC), BF16),
            pltpu.VMEM((8, 8, 128), F32),
            pltpu.VMEM((8, 8, 128), F32),
            pltpu.VMEM((8, ZS, SLOT, KVR), BF16),
            pltpu.VMEM((8, SLOT, OUT_K), BF16),
            pltpu.VMEM((512, 2 * NOPE + 2 * ROPE), BF16),
            pltpu.VMEM((512, 448), BF16),
            pltpu.VMEM((2 * ZS, 8, 128), F32),
            pltpu.VMEM((YS, 64, 128), BF16),
            pltpu.VMEM((ZS, 8, 128), F32),
            pltpu.VMEM((ZS, 8, 128), F32),
            dma((9,)),
            dma((1,)), dma((XS, 2)),
            dma((1,)), dma((8,)),
            dma((1,)), dma((8,)),
            dma((1,)), dma((1,)), dma((1,)), dma((18,)),
            dma((1,)), dma((8, 2)),
            dma((1,)), dma((2 * ZS,)),
            dma((1,)), dma((YS,)),
            dma((1,)), dma((ZS,)),
        ],
        compiler_params=pltpu.CompilerParams(
            collective_id=0, has_side_effects=True, vmem_limit_bytes=60 * 2**20
        ),
        cost_estimate=pl.CostEstimate(
            flops=4 * 10**8, bytes_accessed=5 * 10**6, transcendentals=10**4
        ),
    )(
        q_latent, new_latent, new_rope, latent_cache, jnp.swapaxes(rope_cache, 1, 2), lengths,
        q_up, kv_up, out_proj,
    ).astype(BF16)


def solution(mesh):
    placed = (
        P("batch", None),
        P("batch", None),
        P("batch", None),
        P("batch", None, None),
        P("batch", None, None),
        P("batch"),
        P(("heads", "batch"), None),
        P(("heads", "batch"), None),
        P(("heads", "batch"), None),
    )
    return jax.shard_map(
        shards, mesh=mesh, in_specs=placed, out_specs=P("batch", "heads"), check_vma=False
    )
```

```python
import functools
import math

import jax
import jax.numpy as jnp
from jax import lax
from jax.experimental import pallas as pl
from jax.experimental.pallas import tpu as pltpu
from jax.sharding import PartitionSpec as P

QR = 1536
KVR = 512
NOPE = 128
ROPE = 64
CACHE = 1024
QROWS = 12
SLOT = 16
XS, ZS = 4, 4
YS = 8
QC = QR // 4
OUT_K = 4096
F32 = jnp.float32
BF16 = jnp.bfloat16
NT = (((1,), (1,)), ((), ()))


def dot_nt(a, b):
    return lax.dot_general(a, b, NT, preferred_element_type=F32)


def dot_nn(a, b):
    return jnp.dot(a, b, preferred_element_type=F32)


def kernel(
    ql_hbm, nl_hbm, nr_hbm, lat_hbm, rope_hbm, len_hbm, qup_hbm, kvup_hbm, outp_hbm, y_ref,
    ql_in, nl_in, nr_in, len_in, qup_in, outp_in, lat, rope,
    qbuf, qlbuf, qsend, qrecv, kvbuf, wbuf, sel, sel_out, vx, vh, ysend, yrecv,
    in_sem, q_send, q_recv, ql_send, ql_recv, qx_send, qx_recv, kvz_send, kvp_send, kvb_send, kv_recv,
    w_send, w_recv, vx_send, vx_recv, vh_send, vh_recv, y_send, y_recv,
):
    h = lax.axis_index("heads")
    b = lax.axis_index("batch")
    x, z, c = b // 8, (b // 2) % 4, b % 2
    y, up = h % YS, h // YS

    def index(xx, zz, cc):
        return xx * 8 + zz * 2 + cc

    zk = [z, z + 1 - 2 * (z % 2), (z + 2) % 4, 3 - z]
    xr, xl, xo = (x + 1) % 4, (x + 3) % 4, (x + 2) % 4
    right, left, sibling = index(xr, z, c), index(xl, z, c), index(x, z, 1 - c)
    mine, theirs = x * 2 + c, x * 2 + 1 - c
    own = z * 2 + c

    loads = [
        pltpu.make_async_copy(source, target, in_sem.at[i])
        for i, (source, target) in enumerate(
            [
                (qup_hbm, qup_in), (ql_hbm, ql_in), (kvup_hbm, kvbuf.at[mine, z]),
                (nl_hbm, nl_in), (nr_hbm, nr_in), (len_hbm, len_in), (outp_hbm, outp_in),
                (lat_hbm, lat), (rope_hbm, rope),
            ]
        )
    ]
    barrier = pltpu.get_barrier_semaphore()

    def greet(target):
        pl.semaphore_signal(barrier, inc=1, device_id={"batch": target})

    across = (1 - up) * YS + y
    for k in range(ZS):
        pl.semaphore_signal(
            barrier, inc=1, device_id={"heads": across, "batch": index(x, zk[k], c)}
        )

    @pl.loop(1, YS)
    def _(i):
        pl.semaphore_signal(barrier, inc=1, device_id={"heads": up * YS + (y + i) % YS})

    for k in (3, 2, 1):
        greet(index(x, zk[k], c))
        greet(index(x, zk[k], 1 - c))
    for cc in (c, 1 - c):
        greet(index(xr, z, cc))
        greet(index(xl, z, cc))
    greet(sibling)

    for i in (2, 0, 1, 3, 4, 5, 6, 7, 8):
        loads[i].start()
    loads[2].wait()
    pl.semaphore_wait(barrier, ZS + YS - 1 + 6 + 4 + 1)

    def remote(source, target, send_sem, recv_sem, device):
        return pltpu.make_async_remote_copy(
            src_ref=source, dst_ref=target, send_sem=send_sem, recv_sem=recv_sem,
            device_id=device,
        )

    def push(ref, send_sem, recv_sem, target):
        remote(ref, ref, send_sem, recv_sem, {"batch": target}).start()

    def arrive(ref, recv_sem):
        pltpu.make_async_copy(ref, ref, recv_sem).wait()

    for k in (3, 2, 1):
        push(kvbuf.at[mine, z], kvz_send.at[0], kv_recv.at[z], index(x, zk[k], c))

    loads[0].wait()
    qbuf[x, :, :] = jnp.concatenate([qup_in[...], jnp.zeros((SLOT - QROWS, QR), BF16)], axis=0)
    for target in (right, left):
        push(qbuf.at[x], q_send.at[0], q_recv.at[x, 0], target)
    loads[1].wait()
    ql_own = ql_in[...].astype(F32)
    qlbuf[own, :, :] = jnp.concatenate(
        [ql_own[:, j * QC: (j + 1) * QC] for j in range(4)], axis=0
    ).astype(BF16)
    for k in (3, 2, 1):
        push(qlbuf.at[own], ql_send.at[0], ql_recv.at[own], index(x, zk[k], c))
    push(qlbuf.at[own], ql_send.at[0], ql_recv.at[own], sibling)

    @pl.loop(0, 32)
    def _(t):
        x_t = (x + t % 4 + (t % 4) // 2 - 2 * ((t % 4) // 3)) % 4
        first_row = QROWS * ((x_t % 2) * 8 + (t // 8) * 2 + (t // 4) % 2)
        shape = (SLOT, 2 * NOPE + 2 * ROPE)
        within = lax.broadcasted_iota(jnp.int32, shape, 0)
        col = lax.broadcasted_iota(jnp.int32, shape, 1)
        row = within + first_row
        nope = (row < NOPE) & (col == row + (x_t // 2) * NOPE)
        rotary = row - NOPE
        swapped = (rotary + ROPE // 2) % ROPE
        rope_at = (row >= NOPE) & (
            (col == 2 * NOPE + rotary) | (col == 2 * NOPE + ROPE + swapped)
        )
        block = jnp.where((within < QROWS) & (nope | rope_at), 1.0, 0.0).astype(BF16)
        sel[pl.ds(pl.multiple_of(t * SLOT, SLOT), SLOT), :] = block

    arrive(qbuf.at[xl], q_recv.at[xl, 0])
    push(qbuf.at[xl, :, pl.ds(0, QR // 2)], q_send.at[0], q_recv.at[xl, 0], right)
    arrive(qbuf.at[xr], q_recv.at[xr, 0])
    push(qbuf.at[xr, :, pl.ds(QR // 2, QR // 2)], q_send.at[0], q_recv.at[xr, 1], left)

    def pair(block, half):
        return kvbuf.at[block, pl.ds(2 * half, 2)]

    def kv_pair_out(half):
        for target in (right, left):
            push(pair(mine, half), kvp_send.at[0], kv_recv.at[4 + x * 2 + half], target)

    arrive(kvbuf.at[mine, zk[1]], kv_recv.at[zk[1]])
    kv_pair_out(z // 2)
    for k in range(2, ZS):
        arrive(kvbuf.at[mine, zk[k]], kv_recv.at[zk[k]])
    kv_pair_out(1 - z // 2)
    push(kvbuf.at[mine], kvb_send.at[0], kv_recv.at[12 + x], sibling)
    for k in range(1, ZS):
        slot = zk[k] * 2 + c
        arrive(qlbuf.at[slot], ql_recv.at[slot])
        push(qlbuf.at[slot], ql_send.at[0], ql_recv.at[slot], sibling)

    loads[6].wait()
    wbuf[mine, :, :] = jnp.concatenate([outp_in[...], jnp.zeros((2, OUT_K), BF16)], axis=0)

    from_left, from_right, from_far = xl * 2 + c, xr * 2 + c, xo * 2 + c
    arrive(pair(from_left, 0), kv_recv.at[4 + xl * 2])
    push(pair(from_left, 0), kvp_send.at[0], kv_recv.at[4 + xl * 2], right)
    push(pair(from_left, 0), kvp_send.at[0], kv_recv.at[16], index(xr, z, 1 - c))
    arrive(pair(from_right, 1), kv_recv.at[4 + xr * 2 + 1])
    push(pair(from_right, 1), kvp_send.at[0], kv_recv.at[4 + xr * 2 + 1], left)
    push(pair(from_right, 1), kvp_send.at[0], kv_recv.at[17], index(xl, z, 1 - c))
    arrive(pair(from_left, 1), kv_recv.at[4 + xl * 2 + 1])
    push(kvbuf.at[from_left], kvb_send.at[0], kv_recv.at[12 + xl], sibling)
    arrive(pair(from_right, 0), kv_recv.at[4 + xr * 2])
    push(kvbuf.at[from_right], kvb_send.at[0], kv_recv.at[12 + xr], sibling)

    for target in (right, left, sibling):
        push(wbuf.at[mine], w_send.at[0], w_recv.at[mine, 0], target)

    for zz in range(ZS):
        slot = zz * 2 + 1 - c
        arrive(qlbuf.at[slot], ql_recv.at[slot])
    ql_rows = qlbuf[...].reshape(8 * SLOT, QC)

    def partial_q(slots):
        width = len(slots) * SLOT
        block_of = (lax.broadcasted_iota(jnp.int32, (8 * SLOT, width), 0) // 4) % 4
        total = jnp.zeros((8 * SLOT, width), F32)
        for j in range(4):
            columns = jnp.concatenate(
                [qbuf[slot, :, j * QC: (j + 1) * QC] for slot in slots], axis=0
            )
            total = jnp.where(block_of == j, dot_nt(ql_rows, columns), total)
        return total

    near = partial_q([x, xr, xl])
    arrive(qbuf.at[xo, :, pl.ds(0, QR // 2)], q_recv.at[xo, 0])
    arrive(qbuf.at[xo, :, pl.ds(QR // 2, QR // 2)], q_recv.at[xo, 1])
    partial = jnp.concatenate([near, partial_q([xo])], axis=1)
    partial = partial.reshape(8, SLOT, XS * SLOT)
    partial = partial[:, 0:8] + partial[:, 8:16]
    partial = jnp.concatenate([partial, partial], axis=2)
    lane_of = lax.broadcasted_iota(jnp.int32, (8, 8, 128), 2)
    qsend[...] = jnp.where(lane_of // 64 == c, partial, 0.0)
    for k in (3, 2, 1):
        for cc in (c, 1 - c):
            slot = zk[k] * 2 + cc
            remote(
                qsend.at[slot], qrecv.at[own], qx_send.at[0], qx_recv.at[own],
                {"batch": index(x, zk[k], cc)},
            ).start()
    remote(
        qsend.at[z * 2 + 1 - c], qrecv.at[own], qx_send.at[0], qx_recv.at[own], {"batch": sibling}
    ).start()
    qrecv[own, :, :] = qsend[own]

    row8 = lax.broadcasted_iota(jnp.int32, (8, 1), 0)
    row_of = row8 % 4
    low = row8 < 4
    for load in loads[3:6]:
        load.wait()
    length = jnp.zeros((8, 1), jnp.int32)
    for r in range(4):
        length = jnp.where(row_of == r, len_in[r], length)

    lane64 = lax.broadcasted_iota(jnp.int32, (8, ROPE), 1)
    inverse = jnp.exp((lane64 % (ROPE // 2)).astype(F32) * (-2.0 * math.log(50000.0) / ROPE))
    angles = length.astype(F32) * inverse
    cosine = jnp.cos(angles)
    sine = jnp.sin(angles)
    sine = jnp.where(lane64 < ROPE // 2, -sine, sine)

    def twice(values):
        return jnp.concatenate([values, values], axis=0)

    nr8 = twice(nr_in[...].astype(F32))
    nr_swapped = jnp.concatenate([nr8[:, ROPE // 2:], nr8[:, : ROPE // 2]], axis=1)
    key_new = (nr8 * cosine + nr_swapped * sine).astype(BF16).astype(F32)
    nl8 = twice(nl_in[...].astype(F32))

    for k in range(1, ZS):
        for cc in (c, 1 - c):
            slot = zk[k] * 2 + cc
            arrive(qrecv.at[slot], qx_recv.at[slot])
    arrive(qrecv.at[z * 2 + 1 - c], qx_recv.at[z * 2 + 1 - c])
    pieces = []
    for zz in range(ZS):
        piece = qrecv[2 * zz] + qrecv[2 * zz + 1]
        pieces.append(piece + pltpu.roll(piece, 4, 0))
    q_all = jnp.concatenate(pieces, axis=1)
    lane_q = lax.broadcasted_iota(jnp.int32, (8, 512), 1)
    turn = lane_q % 64 // 16
    x_of = (x + turn + turn // 2 - 2 * (turn // 3)) % 4
    q_all = jnp.where((x_of < 2) == low, q_all, 0.0)
    q_hi = q_all.astype(BF16)
    q_lo = q_all - q_hi.astype(F32)
    selection = sel[...]
    q_both = jnp.concatenate([q_hi.astype(F32), q_lo], axis=0).astype(BF16)
    q_both = dot_nn(q_both, selection)
    q_sel = q_both[0:8] + q_both[8:16]
    q_nope = q_sel[:, 0: 2 * NOPE].astype(BF16)
    query_rope = (
        q_sel[:, 2 * NOPE: 2 * NOPE + ROPE] * cosine + q_sel[:, 2 * NOPE + ROPE:] * sine
    ).astype(BF16)

    loads[8].wait()
    rope_scores = jnp.zeros((8, CACHE), F32)
    for r in range(4):
        rope_scores = jnp.where(row_of == r, dot_nn(query_rope, rope[r]), rope_scores)

    def blocks_for(parity):
        @pl.when(x % 2 == parity)
        def _():
            arrive(kvbuf.at[x * 2 + 1 - c], kv_recv.at[12 + x])
            for half in range(2):
                arrive(pair(from_far, half), kv_recv.at[4 + xo * 2 + half])
                arrive(pair(xo * 2 + 1 - c, half), kv_recv.at[16 + half])

        @pl.when(x % 2 != parity)
        def _():
            for xx in (xl, xr):
                arrive(kvbuf.at[xx * 2 + 1 - c], kv_recv.at[12 + xx])

    blocks_for(0)

    def kv_rows(xx):
        return jnp.concatenate(
            [kvbuf[xx * 2 + cc, zz] for zz in range(ZS) for cc in range(2)], axis=0
        )

    query_abs = (
        dot_nn(q_nope[:, :NOPE], kv_rows(0)) + dot_nn(q_nope[:, NOPE:], kv_rows(2))
    ).astype(BF16)

    loads[7].wait()
    scale = (NOPE + ROPE) ** (-0.5)
    scores = jnp.zeros((8, CACHE), F32)
    for r in range(4):
        scores = jnp.where(row_of == r, dot_nt(query_abs, lat[r]), scores)
    scores = scores + rope_scores
    score_new = scale * (
        jnp.sum(query_abs.astype(F32) * nl8, axis=1, keepdims=True)
        + jnp.sum(query_rope.astype(F32) * key_new, axis=1, keepdims=True)
    )
    position = lax.broadcasted_iota(jnp.int32, (8, CACHE), 1)
    scores = jnp.where(position < length, scores * scale, -1e30)
    top = jnp.maximum(jnp.max(scores, axis=1, keepdims=True), score_new)
    old = jnp.exp(scores - top)
    new = jnp.exp(score_new - top)
    denom = jnp.sum(old, axis=1, keepdims=True) + new
    probs = (old / denom).astype(BF16)
    prob_new = (new / denom).astype(BF16).astype(F32)
    context = jnp.zeros((8, KVR), F32)
    for r in range(4):
        context = jnp.where(row_of == r, dot_nn(probs, lat[r]), context)
    context = (context + prob_new * nl8).astype(BF16)
    blocks_for(1)
    value = jnp.where(low, dot_nt(context, kv_rows(1)), dot_nt(context, kv_rows(3)))
    z_of_8 = up * ZS + z
    first_at = z_of_8 * (1 - c) + y * c
    second_at = y * (1 - c) + z_of_8 * c

    def ring_peer(steps_z, steps_y):
        to_z, to_y = (z_of_8 + steps_z) % 8, (y + steps_y) % YS
        return {"heads": to_z // ZS * YS + to_y, "batch": index(x, to_z % ZS, c)}

    vx[first_at, :, :] = value.astype(BF16).astype(F32)
    for i in (4, 3, 5, 2, 6, 1, 7):
        remote(
            vx.at[first_at], vx.at[first_at], vx_send.at[0], vx_recv.at[first_at],
            ring_peer(i * (1 - c), i * c),
        ).start()

    arrive(wbuf.at[from_left], w_recv.at[from_left, 0])
    push(
        wbuf.at[from_left, :, pl.ds(0, OUT_K // 2)], w_send.at[0], w_recv.at[from_left, 0], right
    )
    push(wbuf.at[from_left], w_send.at[0], w_recv.at[from_left, 0], sibling)
    arrive(wbuf.at[from_right], w_recv.at[from_right, 0])
    push(
        wbuf.at[from_right, :, pl.ds(OUT_K // 2, OUT_K // 2)], w_send.at[0],
        w_recv.at[from_right, 1], left,
    )
    push(wbuf.at[from_right], w_send.at[0], w_recv.at[from_right, 0], sibling)

    for i in (1, 7, 2, 6, 3, 5, 4):
        slot = (first_at + i) % 8
        arrive(vx.at[slot], vx_recv.at[slot])
    vh[second_at, :, :] = vx[...].reshape(64, 128).astype(BF16)

    for i in (4, 3, 5, 2, 6, 1, 7):
        remote(
            vh.at[second_at], vh.at[second_at], vh_send.at[0], vh_recv.at[second_at],
            ring_peer(i * c, i * (1 - c)),
        ).start()

    arrive(wbuf.at[from_far, :, pl.ds(0, OUT_K // 2)], w_recv.at[from_far, 0])
    arrive(wbuf.at[from_far, :, pl.ds(OUT_K // 2, OUT_K // 2)], w_recv.at[from_far, 1])
    push(wbuf.at[from_far], w_send.at[0], w_recv.at[from_far, 0], sibling)

    @pl.loop(0, 32)
    def _(t):
        start = (((t // 2) % 4) * 8 + (t // 8) * 2 + t % 2) * 14
        col = lax.broadcasted_iota(jnp.int32, (SLOT, 448), 1) - start
        row = lax.broadcasted_iota(jnp.int32, (SLOT, 448), 0)
        block = jnp.where((col == row) & (row < 14), 1.0, 0.0).astype(BF16)
        sel_out[pl.ds(pl.multiple_of(t * SLOT, SLOT), SLOT), :] = block

    for xx in (x, xl, xr, xo):
        block = xx * 2 + 1 - c
        arrive(wbuf.at[block], w_recv.at[block, 0])

    row32 = lax.broadcasted_iota(jnp.int32, (32, 128), 0)
    is_low = (row32 % 8) < 4
    zero = jnp.zeros((32, 128), BF16)

    def by_head(block):
        return jnp.concatenate(
            [jnp.where(is_low, block, zero), jnp.where(is_low, zero, block)], axis=1
        )

    def out_rows(half, at_y):
        columns = pl.ds(pl.multiple_of((half * YS + at_y) * 256, 256), 256)
        return wbuf[:, :, columns].reshape(8 * SLOT, 256)

    @pl.when(c == 0)
    def _():
        y_all = jnp.zeros((32, 128), F32)
        for i in (0, 1, 7, 2, 6, 3, 5, 4):
            other = (y + i) % YS
            if i:
                arrive(vh.at[other], vh_recv.at[other])
            for half in range(2):
                block = vh[other, half * 32: half * 32 + 32]
                y_all = y_all + dot_nt(by_head(block), out_rows(half, other))
        ysend[...] = y_all.reshape(ZS, 8, 128)

    @pl.when(c == 1)
    def _():
        for i in (1, 7, 2, 6, 3, 5, 4):
            other = (z_of_8 + i) % 8
            arrive(vh.at[other], vh_recv.at[other])
        y_all = jnp.zeros((32, 128), F32)
        for half in range(2):
            blocks = vh[half * ZS: half * ZS + ZS].astype(F32).reshape(ZS, YS, 8, 128)
            for at_y in range(YS):
                block = blocks[:, at_y].reshape(32, 128).astype(BF16)
                y_all = y_all + dot_nt(by_head(block), out_rows(half, at_y))
        ysend[...] = y_all.reshape(ZS, 8, 128)

    for k in (3, 2, 1):
        remote(
            ysend.at[zk[k]], yrecv.at[z], y_send.at[0], y_recv.at[z],
            {"batch": index(x, zk[k], c)},
        ).start()
    yrecv[z, :, :] = ysend[z]
    for k in range(1, ZS):
        arrive(yrecv.at[zk[k]], y_recv.at[zk[k]])
    pieces = []
    for zz in range(ZS):
        piece = yrecv[zz]
        pieces.append(piece + pltpu.roll(piece, 4, 0))
    summed = jnp.concatenate(pieces, axis=1).astype(BF16)
    y_ref[...] = dot_nn(summed, sel_out[...])[0:4]

    for ref, sem in (
        (qbuf.at[0:3], q_send), (kvbuf.at[0, 0:3], kvz_send), (kvbuf.at[0:4], kvp_send),
        (kvbuf.at[0:3], kvb_send),
        (qlbuf.at[0:7], ql_send), (qsend.at[0:7], qx_send), (wbuf.at[0:7], w_send),
        (vx.at[0:7], vx_send), (vh.at[0:7], vh_send), (ysend.at[0:3], y_send),
    ):
        arrive(ref, sem.at[0])


def shards(
    q_latent, new_latent, new_rope, latent_cache, rope_cache, lengths, q_up, kv_up, out_proj
):
    hbm = pl.BlockSpec(memory_space=pltpu.HBM)
    dma = pltpu.SemaphoreType.DMA
    return pl.pallas_call(
        kernel,
        out_shape=jax.ShapeDtypeStruct((4, 448), F32),
        in_specs=[hbm] * 9,
        out_specs=pl.BlockSpec(memory_space=pltpu.VMEM),
        scratch_shapes=[
            pltpu.VMEM((4, QR), BF16),
            pltpu.VMEM((4, KVR), BF16),
            pltpu.VMEM((4, ROPE), BF16),
            pltpu.SMEM((4,), jnp.int32),
            pltpu.VMEM((QROWS, QR), BF16),
            pltpu.VMEM((14, OUT_K), BF16),
            pltpu.VMEM((4, CACHE, KVR), BF16),
            pltpu.VMEM((4, ROPE, CACHE), BF16),
            pltpu.VMEM((XS, SLOT, QR), BF16),
            pltpu.VMEM((8, SLOT, QC), BF16),
            pltpu.VMEM((8, 8, 128), F32),
            pltpu.VMEM((8, 8, 128), F32),
            pltpu.VMEM((8, ZS, SLOT, KVR), BF16),
            pltpu.VMEM((8, SLOT, OUT_K), BF16),
            pltpu.VMEM((512, 2 * NOPE + 2 * ROPE), BF16),
            pltpu.VMEM((512, 448), BF16),
            pltpu.VMEM((2 * ZS, 8, 128), F32),
            pltpu.VMEM((YS, 64, 128), BF16),
            pltpu.VMEM((ZS, 8, 128), F32),
            pltpu.VMEM((ZS, 8, 128), F32),
            dma((9,)),
            dma((1,)), dma((XS, 2)),
            dma((1,)), dma((8,)),
            dma((1,)), dma((8,)),
            dma((1,)), dma((1,)), dma((1,)), dma((18,)),
            dma((1,)), dma((8, 2)),
            dma((1,)), dma((2 * ZS,)),
            dma((1,)), dma((YS,)),
            dma((1,)), dma((ZS,)),
        ],
        compiler_params=pltpu.CompilerParams(
            collective_id=0, has_side_effects=True, vmem_limit_bytes=60 * 2**20
        ),
        cost_estimate=pl.CostEstimate(
            flops=4 * 10**8, bytes_accessed=5 * 10**6, transcendentals=10**4
        ),
    )(
        q_latent, new_latent, new_rope, latent_cache, jnp.swapaxes(rope_cache, 1, 2), lengths,
        q_up, kv_up, out_proj,
    ).astype(BF16)


def solution(mesh):
    placed = (
        P("batch", None),
        P("batch", None),
        P("batch", None),
        P("batch", None, None),
        P("batch", None, None),
        P("batch"),
        P(("heads", "batch"), None),
        P(("heads", "batch"), None),
        P(("heads", "batch"), None),
    )
    return jax.shard_map(
        shards, mesh=mesh, in_specs=placed, out_specs=P("batch", "heads"), check_vma=False
    )
```
